32 devices in a mesh: parts: 2 (over y), seq: 8 (over z, x), head: 2 (over core).
Axes of the slice: x: 2, y: 2, z: 4, core: 2. Of those that a mesh axis runs over, the one named last changes fastest.
Arguments:
- queries: bfloat16 [4096, 4096], P(('parts', 'seq'), 'head'), parts along dimension 0, may hold values from -144 to 144
- key_rows: bfloat16 [4096, 1024], P(('parts', 'seq'), 'head'), parts along dimension 0, may hold values from -4 to 4
- value_rows: bfloat16 [4096, 1024], P(('parts', 'seq'), 'head'), parts along dimension 0, may hold values from -4 to 4
- out_grad: bfloat16 [4096, 4096], P(('parts', 'seq'), 'head'), parts along dimension 0, may hold values from -4 to 4
- owner_slot: int32 [4096], P(('parts', 'seq')), parts along dimension 0, may hold values from 0 to 2047, as said below
- block_links: int32 [32, 5], P(('parts', 'seq')), parts along dimension 0, may hold values from 0 to 1, as said below
Outputs:
- query_grad: bfloat16 [4096, 4096], P(('parts', 'seq'), 'head'), parts along dimension 0
- key_grad: bfloat16 [4096, 1024], P(('parts', 'seq'), 'head'), parts along dimension 0
- value_grad: bfloat16 [4096, 1024], P(('parts', 'seq'), 'head'), parts along dimension 0
The draws below stay inside these ranges and needn't reach their ends.
There are 2 independent parts, one for each index of `parts`. The reference program is written for one: setup_inputs(seed, part) draws one part's arguments, and reference() takes and returns one part's arrays. A program takes and returns all parts, laid end to end along the dimension named above; each array names one. Nothing has to cross between parts.
Inputs may be any that keep to these rules, and one draw needn't show every extreme that they name: A permutation: token t goes to index owner_slot[t] // 256 of seq, row owner_slot[t] % 256. The 256 tokens of one index of seq send at most 64 tokens to one index, and exactly 64 to some index in every draw. `block_links`: every block is linked to itself (column 2 is 1); columns that name blocks outside the pack are 0.
All inputs are finite; a program needn't handle non-finite values.
Results may differ from the reference program's by a relative error of at most 0.0055.
Values may be sent and summed in bfloat16 or wider, within the bound.
No kernel may reach another device: no remote copies, remote signals or barrier semaphores. Data moves between devices by JAX's collectives and lax.ppermute only.
A program may use at most 64 MiB of HBM per device.

```python
import jax
import jax.numpy as jnp
from jax import lax

HEADS = 32
KV_HEADS = 8
HEAD_DIM = 128
BLOCK = 128
TOK_DEV = 256
TOKENS = 2048
BLOCKS_DEV = 2
NUM_BLOCKS = 16
LINK_SPAN = 5
CAPACITY = 64


def shared_keys(key):
    return jax.random.truncated_normal(key, -4.0, 4.0, (TOKENS, KV_HEADS * HEAD_DIM), jnp.float32)


def draw_key_rows(key, part):
    base_rows = shared_keys(key)
    return base_rows.astype(jnp.bfloat16)


def draw_queries(key, part):
    key = jax.random.fold_in(key, 7)
    drawn_rows = jax.random.truncated_normal(key, -4.0, 4.0, (TOKENS, HEADS * HEAD_DIM), jnp.float32)
    return drawn_rows.astype(jnp.bfloat16)


def draw_owner_slot(key, part):
    key = jax.random.fold_in(key, 11)
    seq_count = TOKENS // TOK_DEV
    first_key, second_key, third_key = jax.random.split(key, 3)
    shuffled = jax.random.permutation(first_key, seq_count)
    position = jnp.arange(TOK_DEV, dtype=jnp.int32)
    half_rows = TOK_DEV // 2
    bucket = jnp.where(position < half_rows, position // CAPACITY, half_rows // CAPACITY + (position - half_rows) // (CAPACITY // 2))
    offsets = shuffled[bucket]
    rotation = jax.random.randint(second_key, (seq_count, 1), 0, TOK_DEV)
    arrange = jax.random.permutation(third_key, TOK_DEV)
    source = jnp.arange(seq_count, dtype=jnp.int32)[:, None]
    turned = (position[None, :] + rotation) % TOK_DEV
    owner = (source + offsets[turned]) % seq_count
    return (owner * TOK_DEV + arrange[turned]).reshape(TOKENS).astype(jnp.int32)


def draw_block_links(key, part):
    key = jax.random.fold_in(key, 23)
    level_key, pick_key = jax.random.split(key, 2)
    block_ids = jnp.arange(NUM_BLOCKS, dtype=jnp.int32)[:, None]
    reach = jnp.arange(LINK_SPAN, dtype=jnp.int32)[None, :]
    partner = block_ids + reach - BLOCKS_DEV
    inside = (partner >= 0) & (partner < NUM_BLOCKS)
    level = jax.random.randint(level_key, (NUM_BLOCKS, 1), 1, 4)
    ticket = jax.random.randint(pick_key, (NUM_BLOCKS, LINK_SPAN), 0, 4)
    linked = (ticket < level) | (reach == BLOCKS_DEV)
    return jnp.where(inside & linked, 1, 0).astype(jnp.int32)


def level_of(rng, dims, shards, least, top_value):
    gain, own = 1.0, jax.random.fold_in(rng, 6)
    for axis_at, parts in shards:
        draws = jnp.exp(jax.random.uniform(jax.random.fold_in(own, axis_at), (parts,), jnp.float32, least / len(shards), top_value / len(shards)))
        gain = gain * jnp.repeat(draws, dims[axis_at] // parts).reshape([-1 if axis == axis_at else 1 for axis in range(len(dims))])
    return gain


def normal_values(key, dims, deviation, most, pieces=(), held_as=jnp.bfloat16):
    drawn = jax.random.normal(key, dims, jnp.float32) * deviation
    if len(pieces) > 0:
        drawn = level_of(key, dims, pieces, -0.22, 0.18) * drawn
    return jnp.clip(drawn, min=-most, max=most).astype(held_as)


def setup_inputs(seed: int = 0, part: int = 0) -> dict:
    streams_of = jax.random.split(jax.random.key(seed), 7)
    part_keys = jax.random.split(jax.random.fold_in(streams_of[6], part), 7)
    queries = draw_queries(jax.random.fold_in(jax.random.fold_in(streams_of[6], part), 71), part)
    key_rows = draw_key_rows(jax.random.fold_in(jax.random.fold_in(streams_of[6], part), 71), part)
    value_rows = normal_values(part_keys[2], (TOKENS, KV_HEADS * HEAD_DIM), 1.0, 4.0, ((0, 8), (1, 2)))
    out_grad = normal_values(part_keys[3], (TOKENS, HEADS * HEAD_DIM), 1.0, 4.0, ((0, 8), (1, 2)))
    owner_slot = draw_owner_slot(jax.random.fold_in(jax.random.fold_in(streams_of[6], part), 71), part)
    block_links = draw_block_links(jax.random.fold_in(jax.random.fold_in(streams_of[6], part), 71), part)
    return {"queries": queries, "key_rows": key_rows, "value_rows": value_rows, "out_grad": out_grad, "owner_slot": owner_slot, "block_links": block_links}


def reference(queries, key_rows, value_rows, out_grad, owner_slot, block_links):
    score_scale = HEAD_DIM ** -0.5
    group_size = HEADS // KV_HEADS
    margin = BLOCKS_DEV * BLOCK
    window = LINK_SPAN * BLOCK
    highest = lax.Precision.HIGHEST
    q_own = jnp.zeros_like(queries).at[owner_slot].set(queries)
    k_own = jnp.zeros_like(key_rows).at[owner_slot].set(key_rows)
    v_own = jnp.zeros_like(value_rows).at[owner_slot].set(value_rows)
    g_own = jnp.zeros_like(out_grad).at[owner_slot].set(out_grad)
    k_padded = jnp.pad(k_own, ((margin, margin), (0, 0)))
    v_padded = jnp.pad(v_own, ((margin, margin), (0, 0)))

    def one_block(carry, block_id):
        k_total, v_total = carry
        start = block_id * BLOCK
        q_rows = lax.dynamic_slice_in_dim(q_own, start, BLOCK, 0).astype(jnp.float32).reshape(BLOCK, KV_HEADS, group_size, HEAD_DIM)
        g_rows = lax.dynamic_slice_in_dim(g_own, start, BLOCK, 0).astype(jnp.float32).reshape(BLOCK, KV_HEADS, group_size, HEAD_DIM)
        k_window = lax.dynamic_slice_in_dim(k_padded, start, window, 0).astype(jnp.float32).reshape(window, KV_HEADS, HEAD_DIM)
        v_window = lax.dynamic_slice_in_dim(v_padded, start, window, 0).astype(jnp.float32).reshape(window, KV_HEADS, HEAD_DIM)
        key_mask = jnp.repeat(block_links[block_id] > 0, BLOCK)
        scores = jnp.einsum("rhgd,khd->hgrk", q_rows, k_window, precision=highest) * score_scale
        scores = jnp.where(key_mask, scores, -jnp.inf)
        row_top = jnp.max(scores, -1, keepdims=True)
        log_total = row_top + jnp.log(jnp.sum(jnp.exp(scores - row_top), -1, keepdims=True))
        weights = jnp.exp(scores - log_total)
        probs = lax.optimization_barrier(weights.astype(jnp.bfloat16)).astype(jnp.float32)
        attended = jnp.einsum("hgrk,khd->rhgd", probs, v_window, precision=highest).astype(jnp.bfloat16)
        row_delta = jnp.sum(g_rows * attended.astype(jnp.float32), -1).transpose(1, 2, 0)[:, :, :, None]
        d_probs = jnp.einsum("rhgd,khd->hgrk", g_rows, v_window, precision=highest)
        d_scores = lax.optimization_barrier((weights * (d_probs - row_delta)).astype(jnp.bfloat16)).astype(jnp.float32)
        q_grad = (jnp.einsum("hgrk,khd->rhgd", d_scores, k_window, precision=highest) * score_scale).astype(jnp.bfloat16)
        k_part = jnp.einsum("hgrk,rhgd->khd", d_scores, q_rows, precision=highest) * score_scale
        v_part = jnp.einsum("hgrk,rhgd->khd", probs, g_rows, precision=highest)
        k_total = lax.dynamic_update_slice_in_dim(k_total, lax.dynamic_slice_in_dim(k_total, start, window, 0) + k_part.reshape(window, KV_HEADS * HEAD_DIM), start, 0)
        v_total = lax.dynamic_update_slice_in_dim(v_total, lax.dynamic_slice_in_dim(v_total, start, window, 0) + v_part.reshape(window, KV_HEADS * HEAD_DIM), start, 0)
        return (k_total, v_total), q_grad.reshape(BLOCK, HEADS * HEAD_DIM)

    zeros_pad = jnp.zeros((TOKENS + 2 * margin, KV_HEADS * HEAD_DIM), jnp.float32)
    (k_total, v_total), q_blocks = lax.scan(one_block, (zeros_pad, zeros_pad), jnp.arange(NUM_BLOCKS, dtype=jnp.int32))
    q_grad_own = q_blocks.reshape(TOKENS, HEADS * HEAD_DIM)
    k_grad_own = k_total[margin:margin + TOKENS].astype(jnp.bfloat16)
    v_grad_own = v_total[margin:margin + TOKENS].astype(jnp.bfloat16)
    return q_grad_own[owner_slot], k_grad_own[owner_slot], v_grad_own[owner_slot]
```

```python
import functools

import jax
import jax.numpy as jnp
from jax import lax
from jax.experimental import pallas as pl
from jax.experimental.pallas import tpu as pltpu
from jax.sharding import PartitionSpec as P

HEAD_DIM = 128
BLOCK = 128


def padded(value, sides, width):
    for axis, dim in sides:
        peers, length = (lax.axis_size(axis), value.shape[dim])
        up = [(i, (i + 1) % peers) for i in range(peers - 1)]
        down = [(j, i) for i, j in up]
        last = lax.slice_in_dim(value, length - width, length, axis=dim)
        leading = lax.slice_in_dim(value, 0, width, axis=dim)
        before = lax.ppermute(last, axis, up)
        after = lax.ppermute(leading, axis, down)
        value = jnp.concatenate([before, value, after], axis=dim)
    return value


def from_behind(value, axis, by):
    peers = lax.axis_size(axis)
    pairs = [(i, i + by) for i in range(peers) if 0 <= i + by < peers]
    return lax.ppermute(value, axis, pairs)


def head_major(matrix, heads):
    return matrix.reshape(matrix.shape[0], heads, -1).transpose(1, 0, 2)


def relay_plan(queries, key_rows, value_rows, out_grad, owner_slot, block_links):
    row_count = queries.shape[0]
    seq_count = lax.axis_size("seq")
    capacity = 4 * max(1, row_count // seq_count // 2)
    slots = seq_count * capacity
    kv_width = key_rows.shape[1]
    kv_heads = kv_width // HEAD_DIM
    group_size = queries.shape[1] // kv_width
    score_scale = HEAD_DIM ** (-0.5)
    owner_dev = owner_slot // row_count
    owner_row = owner_slot % row_count
    member = (owner_dev[:, None] == jnp.arange(seq_count, dtype=jnp.int32)[None, :]).astype(
        jnp.int32
    )
    within = jnp.sum(jnp.cumsum(member, 0) * member, 1) - 1
    placed = owner_dev * capacity + within

    def pack_rows(matrix):
        return (
            jnp.zeros((slots, matrix.shape[1]), matrix.dtype)
            .at[placed]
            .set(matrix)
            .reshape(seq_count, capacity, matrix.shape[1])
        )

    vacant = jnp.array([row_count // 16, row_count % 16], jnp.float32)
    row_codes = jnp.stack([owner_row // 16, owner_row % 16], 1).astype(jnp.float32)
    code_buffer = (
        jnp.broadcast_to(vacant, (slots, 2))
        .at[placed]
        .set(row_codes)
        .astype(jnp.bfloat16)
        .reshape(seq_count, capacity, 2)
    )
    q_in, k_in, v_in, g_in, codes_in = (
        lax.all_to_all(pack_rows(queries), "seq", split_axis=0, concat_axis=0, tiled=True),
        lax.all_to_all(pack_rows(key_rows), "seq", split_axis=0, concat_axis=0, tiled=True),
        lax.all_to_all(pack_rows(value_rows), "seq", split_axis=0, concat_axis=0, tiled=True),
        lax.all_to_all(pack_rows(out_grad), "seq", split_axis=0, concat_axis=0, tiled=True),
        lax.all_to_all(code_buffer, "seq", split_axis=0, concat_axis=0, tiled=True),
    )
    arrived = codes_in.reshape(slots, 2).astype(jnp.float32)
    target = (arrived[:, 0] * 16.0 + arrived[:, 1]).astype(jnp.int32)

    def unpack_rows(buffer):
        flat_rows = buffer.reshape(slots, buffer.shape[2])
        return (
            jnp.zeros((row_count, flat_rows.shape[1]), flat_rows.dtype)
            .at[target]
            .set(flat_rows, mode="drop")
        )

    q_own = unpack_rows(q_in)
    k_own = unpack_rows(k_in)
    v_own = unpack_rows(v_in)
    g_own = unpack_rows(g_in)
    blocks = row_count // BLOCK
    span = block_links.shape[1]
    offset = (
        jnp.arange(3 * blocks, dtype=jnp.int32)[None, :]
        - jnp.arange(blocks, dtype=jnp.int32)[:, None]
    )
    selector = offset[:, :, None] == jnp.arange(span, dtype=jnp.int32)[None, None, :]
    allowed = jnp.sum(jnp.where(selector, block_links[:, None, :], 0), 2) > 0
    token_mask = jnp.repeat(jnp.repeat(allowed, BLOCK, 0), BLOCK, 1)
    kv_pair = jnp.concatenate([k_own, v_own], 1)
    kv_wide = padded(kv_pair, (("seq", 0),), row_count)

    def scores_of(q_group, k_group):
        raw_scores = (
            jnp.einsum("rgd,kd->grk", q_group, k_group, preferred_element_type=jnp.float32)
            * score_scale
        )
        return jnp.where(token_mask[None], raw_scores, -jnp.inf)

    def forward_head(operands):
        q_group, k_group, v_group = operands
        scores = scores_of(q_group, k_group)
        row_top = jnp.max(scores, -1, keepdims=True)
        log_total = row_top + jnp.log(jnp.sum(jnp.exp(scores - row_top), -1, keepdims=True))
        probs = jnp.exp(scores - log_total).astype(jnp.bfloat16)
        attended = jnp.einsum(
            "grk,kd->rgd", probs, v_group, preferred_element_type=jnp.float32
        ).astype(jnp.bfloat16)
        return (attended, log_total)

    def backward_head(operands):
        q_group, k_group, v_group, g_group, attended, log_total = operands
        weights = jnp.exp(scores_of(q_group, k_group) - log_total)
        row_delta = jnp.sum(g_group.astype(jnp.float32) * attended.astype(jnp.float32), -1).T[
            :, :, None
        ]
        d_probs = jnp.einsum("rgd,kd->grk", g_group, v_group, preferred_element_type=jnp.float32)
        d_scores = (weights * (d_probs - row_delta)).astype(jnp.bfloat16)
        q_grad = (
            jnp.einsum("grk,kd->rgd", d_scores, k_group, preferred_element_type=jnp.float32)
            * score_scale
        ).astype(jnp.bfloat16)
        k_grad = (
            jnp.einsum("grk,rgd->kd", d_scores, q_group, preferred_element_type=jnp.float32)
            * score_scale
        )
        v_grad = jnp.einsum(
            "grk,rgd->kd", weights.astype(jnp.bfloat16), g_group, preferred_element_type=jnp.float32
        )
        return (q_grad, k_grad, v_grad)

    query_heads = q_own.reshape(row_count, kv_heads, group_size, HEAD_DIM).transpose(1, 0, 2, 3)
    grad_heads = g_own.reshape(row_count, kv_heads, group_size, HEAD_DIM).transpose(1, 0, 2, 3)
    key_heads = head_major(kv_wide[:, :kv_width], kv_heads)
    value_heads = head_major(kv_wide[:, kv_width:], kv_heads)
    attended, log_total = lax.map(forward_head, (query_heads, key_heads, value_heads))
    q_grads, k_grads, v_grads = lax.map(
        backward_head, (query_heads, key_heads, value_heads, grad_heads, attended, log_total)
    )
    q_grad_own = q_grads.transpose(1, 0, 2, 3).reshape(row_count, kv_heads * group_size * HEAD_DIM)
    kv_grads = jnp.concatenate(
        [
            k_grads.transpose(1, 0, 2).reshape(3 * row_count, kv_width),
            v_grads.transpose(1, 0, 2).reshape(3 * row_count, kv_width),
        ],
        1,
    )
    from_above = from_behind(kv_grads[:row_count].astype(jnp.bfloat16), "seq", -1).astype(
        jnp.float32
    )
    from_below = from_behind(kv_grads[2 * row_count :].astype(jnp.bfloat16), "seq", 1).astype(
        jnp.float32
    )
    kv_total = (kv_grads[row_count : 2 * row_count] + from_above + from_below).astype(jnp.bfloat16)
    pick_rows = jnp.minimum(target, row_count - 1)

    def gather_back(matrix):
        return matrix[pick_rows].reshape(seq_count, capacity, matrix.shape[1])

    q_back, k_back, v_back = (
        lax.all_to_all(gather_back(q_grad_own), "seq", split_axis=0, concat_axis=0, tiled=True),
        lax.all_to_all(
            gather_back(kv_total[:, :kv_width]), "seq", split_axis=0, concat_axis=0, tiled=True
        ),
        lax.all_to_all(
            gather_back(kv_total[:, kv_width:]), "seq", split_axis=0, concat_axis=0, tiled=True
        ),
    )

    def settle_rows(buffer):
        return buffer.reshape(slots, buffer.shape[2])[placed]

    return (settle_rows(q_back), settle_rows(k_back), settle_rows(v_back))


LOG2_E = 1.4426950408889634
MASKED = -1e30
NT = (((1,), (1,)), ((), ()))
NN = (((1,), (0,)), ((), ()))


def dot(a, b, dims):
    return lax.dot_general(a, b, dims, preferred_element_type=jnp.float32)


def flip(a):
    return a.astype(jnp.float32).T.astype(jnp.bfloat16)


def head_of(ref, j):
    return ref[:, j * HEAD_DIM : (j + 1) * HEAD_DIM]


def absorb(q_ref, shards, j, state):
    factor = HEAD_DIM ** (-0.5) * LOG2_E
    q = head_of(q_ref, j)
    scores = [dot(k_ref[...], q, NT) * factor + bias_ref[...] for k_ref, _, bias_ref, _ in shards]
    tops = [jnp.max(s, 0, keepdims=True) for s in scores]
    top = functools.reduce(jnp.maximum, tops)
    if state is not None:
        top = jnp.maximum(top, state[0])
    weights = [jnp.exp2(s - top) for s in scores]
    total = sum(jnp.sum(w, 0, keepdims=True) for w in weights)
    mixed = sum(dot(s[3], w.astype(jnp.bfloat16), NN) for s, w in zip(shards, weights))
    if state is not None:
        keep = jnp.exp2(state[0] - top)
        total = total + state[1] * keep
        mixed = mixed + state[2] * keep
    return top, total, mixed


def backprop(q_ref, g_ref, shard, group, norm, delta, q_sums):
    k_ref, v_ref, bias_ref, k_flip = shard
    scale = HEAD_DIM ** (-0.5)
    k_grad, v_grad = 0.0, 0.0
    for j in range(group):
        q, g = head_of(q_ref, j), head_of(g_ref, j)
        w = jnp.exp2(dot(k_ref[...], q, NT) * (scale * LOG2_E) + bias_ref[...] - norm[j])
        d_probs = dot(v_ref[...], g, NT)
        d_scores = (w * (d_probs - delta[j])).astype(jnp.bfloat16)
        k_grad = k_grad + dot(d_scores, q, NN)
        v_grad = v_grad + dot(w.astype(jnp.bfloat16), g, NN)
        term = dot(k_flip, d_scores, NN)
        q_sums[j] = term if q_sums[j] is None else q_sums[j] + term
    return k_grad * scale, v_grad


def rows_of(ref, group):
    return [ref[j : j + 1, :] for j in range(group)]


def forward_kernel(count, group, first, q_ref, *refs):
    shards = [refs[3 * i : 3 * i + 3] for i in range(count)]
    refs = refs[3 * count :]
    if not first:
        top_in, total_in, mixed_in = refs[:3]
        refs = refs[3:]
    top_out, total_out, mixed_out = refs
    shards = [(k, v, b, flip(v[...])) for k, v, b in shards]
    for j in range(group):
        state = None if first else (top_in[j : j + 1, :], total_in[j : j + 1, :], mixed_in[j])
        top, total, mixed = absorb(q_ref, shards, j, state)
        top_out[j : j + 1, :] = top
        total_out[j : j + 1, :] = total
        mixed_out[j] = mixed


def turn_kernel(group, q_ref, g_ref, k_ref, v_ref, bias_ref, top_in, total_in, mixed_in, norm_out, delta_out, q_out, grads_out):
    shards = [(k_ref, v_ref, bias_ref, flip(v_ref[...]))]
    norm, delta = [], []
    for j in range(group):
        state = (top_in[j : j + 1, :], total_in[j : j + 1, :], mixed_in[j])
        top, total, mixed = absorb(q_ref, shards, j, state)
        attended = (mixed / total).astype(jnp.bfloat16).astype(jnp.float32)
        norm.append(top + jnp.log2(total))
        delta.append(jnp.sum(head_of(g_ref, j).astype(jnp.float32).T * attended, 0, keepdims=True))
        norm_out[j : j + 1, :] = norm[j]
        delta_out[j : j + 1, :] = delta[j]
    q_sums = [None] * group
    k_grad, v_grad = backprop(q_ref, g_ref, (k_ref, v_ref, bias_ref, flip(k_ref[...])), group, norm, delta, q_sums)
    grads_out[0] = k_grad.astype(jnp.bfloat16)
    grads_out[1] = v_grad.astype(jnp.bfloat16)
    for j in range(group):
        q_out[j] = q_sums[j]


def backward_kernel(count, group, last, q_ref, g_ref, *refs):
    shards = [refs[3 * i : 3 * i + 3] for i in range(count)]
    norm_ref, delta_ref, q_in, q_out = refs[3 * count : 3 * count + 4]
    grads_out = refs[3 * count + 4 :]
    norm, delta = rows_of(norm_ref, group), rows_of(delta_ref, group)
    q_sums = [q_in[j] for j in range(group)]
    for (k_ref, v_ref, bias_ref), out in zip(shards, grads_out):
        shard = (k_ref, v_ref, bias_ref, flip(k_ref[...]))
        out[0], out[1] = backprop(q_ref, g_ref, shard, group, norm, delta, q_sums)
    for j in range(group):
        if last:
            q_out[:, j * HEAD_DIM : (j + 1) * HEAD_DIM] = (q_sums[j].T * HEAD_DIM ** (-0.5)).astype(jnp.bfloat16)
        else:
            q_out[j] = q_sums[j]


def gather_plan(queries, key_rows, value_rows, out_grad, owner_slot, block_links):
    rows = queries.shape[0]
    peers = lax.axis_size("seq")
    half = peers // 2
    width = key_rows.shape[1]
    heads = width // HEAD_DIM
    group = queries.shape[1] // width
    ring = list(range(0, peers, 2)) + list(range(peers - 1, 0, -2))
    onward = [(ring[i], ring[(i + 1) % peers]) for i in range(peers)]
    back = [(b, a) for a, b in onward]

    def send_on(value):
        return lax.ppermute(value, "seq", onward)

    def send_back(value):
        return lax.ppermute(value, "seq", back)

    own = jnp.stack([key_rows, value_rows])
    behind, ahead = [own], [own]
    for _ in range(half - 1):
        behind.append(send_on(behind[-1]))
        ahead.append(send_back(ahead[-1]))
    far = (send_on(behind[-1][0]), send_back(ahead[-1][1]))

    blocks = peers * rows // BLOCK
    span = block_links.shape[1]
    notes = lax.all_gather(jnp.concatenate([owner_slot, block_links.reshape(-1)]), "seq")
    links = notes[:, rows:].reshape(blocks, span)
    ids = jnp.arange(blocks, dtype=jnp.int32)
    place = jnp.array([ring.index(i) for i in range(peers)], jnp.int32)[lax.axis_index("seq")]
    order = jnp.array(ring, jnp.int32)[(place - jnp.arange(peers, dtype=jnp.int32)) % peers]
    key_block = notes[order, :rows] // BLOCK
    reach = ids[None, :, None] - ids[:, None, None] + span // 2 == jnp.arange(span, dtype=jnp.int32)
    linked = jnp.sum(jnp.where(reach, links[:, None, :], 0), 2).astype(jnp.bfloat16)
    query_hot = (ids[:, None] == (owner_slot // BLOCK)[None, :]).astype(jnp.bfloat16)
    key_hot = (key_block[:, :, None] == ids).astype(jnp.bfloat16)
    query_links = dot(linked, query_hot, (((0,), (0,)), ((), ()))).astype(jnp.bfloat16)
    allowed = dot(key_hot.reshape(peers * rows, blocks), query_links, NN)
    bias = jnp.where(allowed > 0.5, 0.0, MASKED).reshape(peers, rows, rows)

    f32 = jnp.float32
    wide = pl.BlockSpec((rows, group * HEAD_DIM), lambda h: (0, h))
    line = pl.BlockSpec((None, group, rows), lambda h: (h, 0, 0))
    tall = pl.BlockSpec((None, group, HEAD_DIM, rows), lambda h: (h, 0, 0, 0))
    pair = pl.BlockSpec((2, rows, HEAD_DIM), lambda h: (0, 0, h))
    lines = jax.ShapeDtypeStruct((heads, group, rows), f32)
    talls = jax.ShapeDtypeStruct((heads, group, HEAD_DIM, rows), f32)

    def pairs(dtype):
        return jax.ShapeDtypeStruct((2, rows, width), dtype)

    def shard_args(shard, at):
        mask = (bias, pl.BlockSpec((None, rows, rows), lambda h: (at, 0, 0)))
        if isinstance(shard, tuple):
            narrow = pl.BlockSpec((rows, HEAD_DIM), lambda h: (0, h))
            return [(shard[0], narrow), (shard[1], narrow), mask]
        return [
            (shard, pl.BlockSpec((None, rows, HEAD_DIM), lambda h: (0, 0, h))),
            (shard, pl.BlockSpec((None, rows, HEAD_DIM), lambda h: (1, 0, h))),
            mask,
        ]

    def call(kernel, args, outs, products, aliases):
        flops = 2 * products * heads * group * rows * rows * HEAD_DIM
        moved = sum(2 * rows * width * 4 for _ in args)
        return pl.pallas_call(
            kernel,
            grid=(heads,),
            in_specs=[spec for _, spec in args],
            out_specs=[spec for _, spec in outs],
            out_shape=[shape for shape, _ in outs],
            input_output_aliases=aliases,
            cost_estimate=pl.CostEstimate(
                flops=flops, bytes_accessed=moved, transcendentals=products * heads * group * rows * rows // 2
            ),
            compiler_params=pltpu.CompilerParams(vmem_limit_bytes=48 * 1024 * 1024),
        )(*[value for value, _ in args])

    def forward(shards, state):
        first = state is None
        args = [(queries, wide)] + [a for shard, at in shards for a in shard_args(shard, at)]
        at = len(args)
        if not first:
            args += list(zip(state, (line, line, tall)))
        kernel = functools.partial(forward_kernel, len(shards), group, first)
        aliases = {} if first else {at + i: i for i in range(3)}
        return call(kernel, args, [(lines, line), (lines, line), (talls, tall)], 2 * len(shards), aliases)

    def backward(shards, norm, delta, q_sums, last):
        args = [(queries, wide), (out_grad, wide)] + [a for shard, at in shards for a in shard_args(shard, at)]
        args += [(norm, line), (delta, line), (q_sums, tall)]
        kernel = functools.partial(backward_kernel, len(shards), group, last)
        q_out = (jax.ShapeDtypeStruct(queries.shape, queries.dtype), wide) if last else (talls, tall)
        outs = [q_out] + [(pairs(f32), pair) for _ in shards]
        return call(kernel, args, outs, 5 * len(shards), {} if last else {len(args) - 1: 0})

    state = forward([(own, 0)], None)
    for r in range(1, half):
        state = forward([(behind[r], r), (ahead[r], peers - r)], state)
    args = [(queries, wide), (out_grad, wide)] + shard_args(far, half)
    args += list(zip(state, (line, line, tall)))
    norm, delta, q_sums, far_grads = call(
        functools.partial(turn_kernel, group),
        args,
        [(lines, line), (lines, line), (talls, tall), (pairs(jnp.bfloat16), pair)],
        7,
        {5: 0, 6: 1, 7: 2},
    )
    from_ahead, from_behind_ = send_back(far_grads[0]), send_on(far_grads[1])
    for r in range(half - 1, 0, -1):
        q_sums, low, high = backward([(behind[r], r), (ahead[r], peers - r)], norm, delta, q_sums, False)
        if r == half - 1:
            low = jnp.stack([low[0] + from_ahead.astype(f32), low[1]])
            high = jnp.stack([high[0], high[1] + from_behind_.astype(f32)])
        else:
            low = low + from_ahead.astype(f32)
            high = high + from_behind_.astype(f32)
        from_ahead, from_behind_ = send_back(low.astype(jnp.bfloat16)), send_on(high.astype(jnp.bfloat16))
    query_grad, mine = backward([(own, 0)], norm, delta, q_sums, True)
    if half == 1:
        total = jnp.stack([mine[0] + from_ahead.astype(f32), mine[1] + from_behind_.astype(f32)])
    else:
        total = mine + from_ahead.astype(f32) + from_behind_.astype(f32)
    total = total.astype(jnp.bfloat16)
    return query_grad, total[0], total[1]


def local(queries, key_rows, value_rows, out_grad, owner_slot, block_links):
    rows = queries.shape[0]
    peers = lax.axis_size("seq")
    q_width, kv_width = queries.shape[1], key_rows.shape[1]
    slots = 4 * peers * max(1, rows // peers // 2)
    gathered = 2 * (peers - 1) * rows * 2 * kv_width
    relayed = slots * (3 * q_width + 4 * kv_width) + 4 * rows * 2 * kv_width
    plan = gather_plan if peers % 2 == 0 and gathered <= relayed else relay_plan
    return plan(queries, key_rows, value_rows, out_grad, owner_slot, block_links)


def solution(mesh):
    return jax.shard_map(
        local,
        mesh=mesh,
        in_specs=(
            P(("parts", "seq"), "head"),
            P(("parts", "seq"), "head"),
            P(("parts", "seq"), "head"),
            P(("parts", "seq"), "head"),
            P(("parts", "seq")),
            P(("parts", "seq"), None),
        ),
        out_specs=(
            P(("parts", "seq"), "head"),
            P(("parts", "seq"), "head"),
            P(("parts", "seq"), "head"),
        ),
        check_vma=False,
    )
```

```python
import functools

import jax
import jax.numpy as jnp
from jax import lax
from jax.experimental import pallas as pl
from jax.experimental.pallas import tpu as pltpu
from jax.sharding import PartitionSpec as P

HEAD_DIM = 128
BLOCK = 128


def padded(value, sides, width):
    for axis, dim in sides:
        peers, length = (lax.axis_size(axis), value.shape[dim])
        up = [(i, (i + 1) % peers) for i in range(peers - 1)]
        down = [(j, i) for i, j in up]
        last = lax.slice_in_dim(value, length - width, length, axis=dim)
        leading = lax.slice_in_dim(value, 0, width, axis=dim)
        before = lax.ppermute(last, axis, up)
        after = lax.ppermute(leading, axis, down)
        value = jnp.concatenate([before, value, after], axis=dim)
    return value


def from_behind(value, axis, by):
    peers = lax.axis_size(axis)
    pairs = [(i, i + by) for i in range(peers) if 0 <= i + by < peers]
    return lax.ppermute(value, axis, pairs)


def head_major(matrix, heads):
    return matrix.reshape(matrix.shape[0], heads, -1).transpose(1, 0, 2)


def relay_plan(queries, key_rows, value_rows, out_grad, owner_slot, block_links):
    row_count = queries.shape[0]
    seq_count = lax.axis_size("seq")
    capacity = 4 * max(1, row_count // seq_count // 2)
    slots = seq_count * capacity
    kv_width = key_rows.shape[1]
    kv_heads = kv_width // HEAD_DIM
    group_size = queries.shape[1] // kv_width
    score_scale = HEAD_DIM ** (-0.5)
    owner_dev = owner_slot // row_count
    owner_row = owner_slot % row_count
    member = (owner_dev[:, None] == jnp.arange(seq_count, dtype=jnp.int32)[None, :]).astype(
        jnp.int32
    )
    within = jnp.sum(jnp.cumsum(member, 0) * member, 1) - 1
    placed = owner_dev * capacity + within

    def pack_rows(matrix):
        return (
            jnp.zeros((slots, matrix.shape[1]), matrix.dtype)
            .at[placed]
            .set(matrix)
            .reshape(seq_count, capacity, matrix.shape[1])
        )

    vacant = jnp.array([row_count // 16, row_count % 16], jnp.float32)
    row_codes = jnp.stack([owner_row // 16, owner_row % 16], 1).astype(jnp.float32)
    code_buffer = (
        jnp.broadcast_to(vacant, (slots, 2))
        .at[placed]
        .set(row_codes)
        .astype(jnp.bfloat16)
        .reshape(seq_count, capacity, 2)
    )
    q_in, k_in, v_in, g_in, codes_in = (
        lax.all_to_all(pack_rows(queries), "seq", split_axis=0, concat_axis=0, tiled=True),
        lax.all_to_all(pack_rows(key_rows), "seq", split_axis=0, concat_axis=0, tiled=True),
        lax.all_to_all(pack_rows(value_rows), "seq", split_axis=0, concat_axis=0, tiled=True),
        lax.all_to_all(pack_rows(out_grad), "seq", split_axis=0, concat_axis=0, tiled=True),
        lax.all_to_all(code_buffer, "seq", split_axis=0, concat_axis=0, tiled=True),
    )
    arrived = codes_in.reshape(slots, 2).astype(jnp.float32)
    target = (arrived[:, 0] * 16.0 + arrived[:, 1]).astype(jnp.int32)

    def unpack_rows(buffer):
        flat_rows = buffer.reshape(slots, buffer.shape[2])
        return (
            jnp.zeros((row_count, flat_rows.shape[1]), flat_rows.dtype)
            .at[target]
            .set(flat_rows, mode="drop")
        )

    q_own = unpack_rows(q_in)
    k_own = unpack_rows(k_in)
    v_own = unpack_rows(v_in)
    g_own = unpack_rows(g_in)
    blocks = row_count // BLOCK
    span = block_links.shape[1]
    offset = (
        jnp.arange(3 * blocks, dtype=jnp.int32)[None, :]
        - jnp.arange(blocks, dtype=jnp.int32)[:, None]
    )
    selector = offset[:, :, None] == jnp.arange(span, dtype=jnp.int32)[None, None, :]
    allowed = jnp.sum(jnp.where(selector, block_links[:, None, :], 0), 2) > 0
    token_mask = jnp.repeat(jnp.repeat(allowed, BLOCK, 0), BLOCK, 1)
    kv_pair = jnp.concatenate([k_own, v_own], 1)
    kv_wide = padded(kv_pair, (("seq", 0),), row_count)

    def scores_of(q_group, k_group):
        raw_scores = (
            jnp.einsum("rgd,kd->grk", q_group, k_group, preferred_element_type=jnp.float32)
            * score_scale
        )
        return jnp.where(token_mask[None], raw_scores, -jnp.inf)

    def forward_head(operands):
        q_group, k_group, v_group = operands
        scores = scores_of(q_group, k_group)
        row_top = jnp.max(scores, -1, keepdims=True)
        log_total = row_top + jnp.log(jnp.sum(jnp.exp(scores - row_top), -1, keepdims=True))
        probs = jnp.exp(scores - log_total).astype(jnp.bfloat16)
        attended = jnp.einsum(
            "grk,kd->rgd", probs, v_group, preferred_element_type=jnp.float32
        ).astype(jnp.bfloat16)
        return (attended, log_total)

    def backward_head(operands):
        q_group, k_group, v_group, g_group, attended, log_total = operands
        weights = jnp.exp(scores_of(q_group, k_group) - log_total)
        row_delta = jnp.sum(g_group.astype(jnp.float32) * attended.astype(jnp.float32), -1).T[
            :, :, None
        ]
        d_probs = jnp.einsum("rgd,kd->grk", g_group, v_group, preferred_element_type=jnp.float32)
        d_scores = (weights * (d_probs - row_delta)).astype(jnp.bfloat16)
        q_grad = (
            jnp.einsum("grk,kd->rgd", d_scores, k_group, preferred_element_type=jnp.float32)
            * score_scale
        ).astype(jnp.bfloat16)
        k_grad = (
            jnp.einsum("grk,rgd->kd", d_scores, q_group, preferred_element_type=jnp.float32)
            * score_scale
        )
        v_grad = jnp.einsum(
            "grk,rgd->kd", weights.astype(jnp.bfloat16), g_group, preferred_element_type=jnp.float32
        )
        return (q_grad, k_grad, v_grad)

    query_heads = q_own.reshape(row_count, kv_heads, group_size, HEAD_DIM).transpose(1, 0, 2, 3)
    grad_heads = g_own.reshape(row_count, kv_heads, group_size, HEAD_DIM).transpose(1, 0, 2, 3)
    key_heads = head_major(kv_wide[:, :kv_width], kv_heads)
    value_heads = head_major(kv_wide[:, kv_width:], kv_heads)
    attended, log_total = lax.map(forward_head, (query_heads, key_heads, value_heads))
    q_grads, k_grads, v_grads = lax.map(
        backward_head, (query_heads, key_heads, value_heads, grad_heads, attended, log_total)
    )
    q_grad_own = q_grads.transpose(1, 0, 2, 3).reshape(row_count, kv_heads * group_size * HEAD_DIM)
    kv_grads = jnp.concatenate(
        [
            k_grads.transpose(1, 0, 2).reshape(3 * row_count, kv_width),
            v_grads.transpose(1, 0, 2).reshape(3 * row_count, kv_width),
        ],
        1,
    )
    from_above = from_behind(kv_grads[:row_count].astype(jnp.bfloat16), "seq", -1).astype(
        jnp.float32
    )
    from_below = from_behind(kv_grads[2 * row_count :].astype(jnp.bfloat16), "seq", 1).astype(
        jnp.float32
    )
    kv_total = (kv_grads[row_count : 2 * row_count] + from_above + from_below).astype(jnp.bfloat16)
    pick_rows = jnp.minimum(target, row_count - 1)

    def gather_back(matrix):
        return matrix[pick_rows].reshape(seq_count, capacity, matrix.shape[1])

    q_back, k_back, v_back = (
        lax.all_to_all(gather_back(q_grad_own), "seq", split_axis=0, concat_axis=0, tiled=True),
        lax.all_to_all(
            gather_back(kv_total[:, :kv_width]), "seq", split_axis=0, concat_axis=0, tiled=True
        ),
        lax.all_to_all(
            gather_back(kv_total[:, kv_width:]), "seq", split_axis=0, concat_axis=0, tiled=True
        ),
    )

    def settle_rows(buffer):
        return buffer.reshape(slots, buffer.shape[2])[placed]

    return (settle_rows(q_back), settle_rows(k_back), settle_rows(v_back))


LOG2_E = 1.4426950408889634
MASKED = -1e30
LANES = 128
NT = (((1,), (1,)), ((), ()))
NN = (((1,), (0,)), ((), ()))
IN_VMEM = pl.BlockSpec(memory_space=pltpu.VMEM)
IN_SMEM = pl.BlockSpec(memory_space=pltpu.SMEM)


def dot(a, b, dims):
    return lax.dot_general(a, b, dims, preferred_element_type=jnp.float32)


def flip(a):
    return a.astype(jnp.float32).T.astype(jnp.bfloat16)


def columns(ref, at):
    return ref[:, at * HEAD_DIM : (at + 1) * HEAD_DIM]


def stacked_heads(ref, head, group):
    return jnp.concatenate([columns(ref, head * group + j) for j in range(group)], 0)


def masks_kernel(peers, blocks_dev, span, order_ref, notes_ref, slots_ref, key_hot_ref, query_mask_ref):
    f32, bf16 = jnp.float32, jnp.bfloat16
    rows = lax.broadcasted_iota(jnp.int32, (LANES, LANES), 0)
    lanes = lax.broadcasted_iota(jnp.int32, (LANES, LANES), 1)
    slot_rows = slots_ref.shape[0]

    def hot(slots):
        return (rows == slots // BLOCK).astype(f32).T.astype(bf16)

    for r in range(peers):
        shard = notes_ref[order_ref[r]]
        for i in range(slot_rows):
            key_hot_ref[r, i * LANES : (i + 1) * LANES, :] = hot(shard[i : i + 1, :])
    owners = lax.broadcasted_iota(jnp.int32, (LANES, peers), 0) // blocks_dev
    spread = (owners == lax.broadcasted_iota(jnp.int32, (LANES, peers), 1)).astype(f32)
    link_rows = jnp.concatenate([notes_ref[p][slot_rows : slot_rows + 1, :] for p in range(peers)], 0).astype(f32)
    of_block = dot(spread, link_rows, NN)
    table = jnp.zeros((LANES, LANES), f32)
    for s in range(span):
        picked = jnp.sum(jnp.where(lanes == (rows % blocks_dev) * span + s, of_block, 0.0), 1, keepdims=True)
        table = table + jnp.where(lanes == rows + s - span // 2, picked, 0.0)
    table = table.astype(bf16)
    for i in range(slot_rows):
        linked = dot(hot(slots_ref[i : i + 1, :]), table, NN)
        query_mask_ref[i * LANES : (i + 1) * LANES, :] = jnp.where(linked > 0.5, 0.0, MASKED).astype(bf16)


def keys_of(shards, head):
    return jnp.concatenate([columns(k, head) for k, _, _ in shards], 0)


def values_of(shards, head):
    return jnp.concatenate([columns(v, head) for _, v, _ in shards], 0)


def split(refs, count, hot_ref, at):
    shards = []
    for i in range(count):
        shards.append((refs[i].at[0], refs[i].at[1], hot_ref.at[at[i]]))
    return shards


def masked_scores(q_ref, mask, shards, hots, head, group):
    queries = jnp.concatenate([stacked_heads(q_ref, head, group), jnp.concatenate([mask] * group, 0)], 1)
    return dot(jnp.concatenate([keys_of(shards, head), hots], 1), queries, NT)


def absorb(scores, values, state):
    factor = HEAD_DIM ** (-0.5) * LOG2_E
    top = jnp.max(scores, 0, keepdims=True)
    if state is not None:
        top = jnp.maximum(top, state[0])
    weights = jnp.exp2((scores - top) * factor)
    total = jnp.sum(weights, 0, keepdims=True)
    mixed = dot(flip(values), weights.astype(jnp.bfloat16), NN)
    if state is not None:
        keep = jnp.exp2((state[0] - top) * factor)
        total = total + state[1] * keep
        mixed = mixed + state[2] * keep
    return top, total, mixed


def backprop(q_ref, g_ref, shards, scores, head, group, norm, delta):
    scale = HEAD_DIM ** (-0.5)
    queries, grads = stacked_heads(q_ref, head, group), stacked_heads(g_ref, head, group)
    weights = jnp.exp2(scores * (scale * LOG2_E) - norm)
    d_scores = (weights * (dot(values_of(shards, head), grads, NT) - delta)).astype(jnp.bfloat16)
    k_grad = dot(d_scores, queries, NN) * scale
    v_grad = dot(weights.astype(jnp.bfloat16), grads, NN)
    return k_grad, v_grad, dot(flip(keys_of(shards, head)), d_scores, NN)


def forward_kernel(at, heads, group, q_ref, mask_ref, hot_ref, *refs):
    shards = split(refs, len(at), hot_ref, at)
    state, outs = refs[len(at) : -3], refs[-3:]
    hots = jnp.concatenate([hot[...] for _, _, hot in shards], 0)
    for head in range(heads):
        scores = masked_scores(q_ref, mask_ref[...], shards, hots, head, group)
        before = [s[head] for s in state] if state else None
        for out, value in zip(outs, absorb(scores, values_of(shards, head), before)):
            out[head] = value


def turn_kernel(at, heads, group, q_ref, g_ref, mask_ref, hot_ref, k_ref, v_ref, top, total, mixed, norm_ref, delta_ref, q_out, k_out, v_out):
    shards = [(k_ref, v_ref, hot_ref.at[at])]
    for head in range(heads):
        scores = masked_scores(q_ref, mask_ref[...], shards, hot_ref[at], head, group)
        state = absorb(scores, values_of(shards, head), (top[head], total[head], mixed[head]))
        norm = state[0] * (HEAD_DIM ** (-0.5) * LOG2_E) + jnp.log2(state[1])
        attended = (state[2] / state[1]).astype(jnp.bfloat16).astype(jnp.float32)
        grads = stacked_heads(g_ref, head, group).astype(jnp.float32).T
        delta = jnp.sum(grads * attended, 0, keepdims=True)
        norm_ref[head], delta_ref[head] = norm, delta
        k_grad, v_grad, q_out[head] = backprop(q_ref, g_ref, shards, scores, head, group, norm, delta)
        span = slice(head * HEAD_DIM, (head + 1) * HEAD_DIM)
        k_out[:, span], v_out[:, span] = k_grad.astype(jnp.bfloat16), v_grad.astype(jnp.bfloat16)


def backward_kernel(at, heads, group, last, q_ref, g_ref, mask_ref, hot_ref, *refs):
    count = len(at)
    shards = split(refs, count, hot_ref, at)
    norm_ref, delta_ref, q_in, q_out = refs[count : count + 4]
    hots = jnp.concatenate([hot[...] for _, _, hot in shards], 0)
    rows = q_ref.shape[0]
    for head in range(heads):
        scores = masked_scores(q_ref, mask_ref[...], shards, hots, head, group)
        k_grad, v_grad, q_terms = backprop(q_ref, g_ref, shards, scores, head, group, norm_ref[head], delta_ref[head])
        span = slice(head * HEAD_DIM, (head + 1) * HEAD_DIM)
        for i, out in enumerate(refs[count + 4 :]):
            out[0, :, span] = k_grad[i * rows : (i + 1) * rows]
            out[1, :, span] = v_grad[i * rows : (i + 1) * rows]
        q_sums = q_in[head] + q_terms
        if last:
            q_sums = q_sums * HEAD_DIM ** (-0.5)
            for j in range(group):
                part = q_sums[:, j * rows : (j + 1) * rows].T
                q_out[:, (head * group + j) * HEAD_DIM : (head * group + j + 1) * HEAD_DIM] = part.astype(jnp.bfloat16)
        else:
            q_out[head] = q_sums


def gather_plan(queries, key_rows, value_rows, out_grad, owner_slot, block_links):
    rows = queries.shape[0]
    peers = lax.axis_size("seq")
    half = peers // 2
    width = key_rows.shape[1]
    heads = width // HEAD_DIM
    group = queries.shape[1] // width
    f32, bf16 = jnp.float32, jnp.bfloat16
    ring = list(range(0, peers, 2)) + list(range(peers - 1, 0, -2))
    onward = [(ring[i], ring[(i + 1) % peers]) for i in range(peers)]
    back = [(b, a) for a, b in onward]

    def send_on(value):
        return lax.ppermute(value, "seq", onward)

    def send_back(value):
        return lax.ppermute(value, "seq", back)

    def call(kernel, args, outs, products, aliases):
        return pl.pallas_call(
            kernel,
            in_specs=[IN_VMEM] * len(args),
            out_specs=[IN_VMEM] * len(outs),
            out_shape=outs,
            input_output_aliases=aliases,
            cost_estimate=pl.CostEstimate(
                flops=4 * products * heads * group * rows * rows * HEAD_DIM, bytes_accessed=4 * rows * width, transcendentals=0
            ),
            compiler_params=pltpu.CompilerParams(vmem_limit_bytes=32 * 1024 * 1024),
        )(*args)

    own = jnp.stack([key_rows, value_rows])
    behind, ahead = [own], [own]
    for _ in range(half - 1):
        behind.append(send_on(behind[-1]))
        ahead.append(send_back(ahead[-1]))
    far = (send_on(behind[-1][0]), send_back(ahead[-1][1]))

    span = block_links.shape[1]
    slots = owner_slot.reshape(rows // LANES, LANES)
    links = jnp.pad(block_links.reshape(1, -1), ((0, 0), (0, LANES - block_links.size)))
    notes = jnp.concatenate([slots, links], 0)
    notes = jnp.pad(notes, ((0, -notes.shape[0] % 8), (0, 0)))
    notes = jnp.broadcast_to(notes[None], (peers,) + notes.shape)
    notes = lax.all_to_all(notes, "seq", split_axis=0, concat_axis=0, tiled=True)
    me = lax.axis_index("seq")
    place = jnp.where(me % 2 == 0, me // 2, peers - (me + 1) // 2)
    place = (place - jnp.arange(peers, dtype=jnp.int32)) % peers
    order = jnp.where(place < half, 2 * place, 2 * peers - 1 - 2 * place)
    hot, mask = pl.pallas_call(
        functools.partial(masks_kernel, peers, rows // BLOCK, span),
        in_specs=[IN_SMEM, IN_VMEM, IN_VMEM],
        out_specs=[IN_VMEM] * 2,
        out_shape=[jax.ShapeDtypeStruct((peers, rows, LANES), bf16), jax.ShapeDtypeStruct((rows, LANES), bf16)],
        compiler_params=pltpu.CompilerParams(vmem_limit_bytes=32 * 1024 * 1024),
    )(order, notes, slots)

    lines = jax.ShapeDtypeStruct((heads, 1, group * rows), f32)
    talls = jax.ShapeDtypeStruct((heads, HEAD_DIM, group * rows), f32)
    pairs = jax.ShapeDtypeStruct((2, rows, width), f32)
    single = jax.ShapeDtypeStruct((rows, width), bf16)

    def forward(shards, at, state):
        args = [queries, mask, hot, *shards, *state]
        kernel = functools.partial(forward_kernel, at, heads, group)
        aliases = {len(args) - 3 + i: i for i in range(3)} if state else {}
        return call(kernel, args, [lines, lines, talls], 2 * len(at), aliases)

    def backward(shards, at, q_sums, last=False):
        args = [queries, out_grad, mask, hot, *shards, norm, delta, q_sums]
        q_out = jax.ShapeDtypeStruct(queries.shape, bf16) if last else talls
        kernel = functools.partial(backward_kernel, at, heads, group, last)
        return call(kernel, args, [q_out] + [pairs] * len(at), 5 * len(at), {} if last else {len(args) - 1: 0})

    near = [own] + ([behind[1], ahead[1]] if half > 1 else [])
    state = forward(near, (0, 1, peers - 1)[: len(near)], ())
    for r in range(2, half):
        state = forward([behind[r], ahead[r]], (r, peers - r), state)
    norm, delta, q_sums, far_k, far_v = call(
        functools.partial(turn_kernel, half, heads, group),
        [queries, out_grad, mask, hot, *far, *state],
        [lines, lines, talls, single, single],
        7,
        {6: 0, 7: 1, 8: 2},
    )
    down, up = send_back(far_k), send_on(far_v)
    for r in range(half - 1, 0, -1):
        q_sums, low, high = backward([behind[r], ahead[r]], (r, peers - r), q_sums)
        if r == half - 1:
            low = jnp.stack([low[0] + down.astype(f32), low[1]])
            high = jnp.stack([high[0], high[1] + up.astype(f32)])
        else:
            low, high = low + down.astype(f32), high + up.astype(f32)
        down, up = send_back(low.astype(bf16)), send_on(high.astype(bf16))
    query_grad, mine = backward([own], (0,), q_sums, True)
    if half == 1:
        total = jnp.stack([mine[0] + down.astype(f32), mine[1] + up.astype(f32)])
    else:
        total = mine + down.astype(f32) + up.astype(f32)
    return query_grad, total[0].astype(bf16), total[1].astype(bf16)


def local(queries, key_rows, value_rows, out_grad, owner_slot, block_links):
    rows = queries.shape[0]
    peers = lax.axis_size("seq")
    q_width, kv_width = queries.shape[1], key_rows.shape[1]
    slots = 4 * peers * max(1, rows // peers // 2)
    gathered = 2 * (peers - 1) * rows * 2 * kv_width
    relayed = slots * (3 * q_width + 4 * kv_width) + 4 * rows * 2 * kv_width
    fits = peers % 2 == 0 and rows % LANES == 0 and peers * rows // BLOCK <= LANES and block_links.size <= LANES
    plan = gather_plan if fits and gathered <= relayed else relay_plan
    return plan(queries, key_rows, value_rows, out_grad, owner_slot, block_links)


def solution(mesh):
    return jax.shard_map(
        local,
        mesh=mesh,
        in_specs=(
            P(("parts", "seq"), "head"),
            P(("parts", "seq"), "head"),
            P(("parts", "seq"), "head"),
            P(("parts", "seq"), "head"),
            P(("parts", "seq")),
            P(("parts", "seq"), None),
        ),
        out_specs=(
            P(("parts", "seq"), "head"),
            P(("parts", "seq"), "head"),
            P(("parts", "seq"), "head"),
        ),
        check_vma=False,
    )
```

```python
import functools

import jax
import jax.numpy as jnp
from jax import lax
from jax.experimental import pallas as pl
from jax.experimental.pallas import tpu as pltpu
from jax.sharding import PartitionSpec as P

HEAD_DIM = 128
BLOCK = 128


def padded(value, sides, width):
    for axis, dim in sides:
        peers, length = (lax.axis_size(axis), value.shape[dim])
        up = [(i, (i + 1) % peers) for i in range(peers - 1)]
        down = [(j, i) for i, j in up]
        last = lax.slice_in_dim(value, length - width, length, axis=dim)
        leading = lax.slice_in_dim(value, 0, width, axis=dim)
        before = lax.ppermute(last, axis, up)
        after = lax.ppermute(leading, axis, down)
        value = jnp.concatenate([before, value, after], axis=dim)
    return value


def from_behind(value, axis, by):
    peers = lax.axis_size(axis)
    pairs = [(i, i + by) for i in range(peers) if 0 <= i + by < peers]
    return lax.ppermute(value, axis, pairs)


def head_major(matrix, heads):
    return matrix.reshape(matrix.shape[0], heads, -1).transpose(1, 0, 2)


def relay_plan(queries, key_rows, value_rows, out_grad, owner_slot, block_links):
    row_count = queries.shape[0]
    seq_count = lax.axis_size("seq")
    capacity = 4 * max(1, row_count // seq_count // 2)
    slots = seq_count * capacity
    kv_width = key_rows.shape[1]
    kv_heads = kv_width // HEAD_DIM
    group_size = queries.shape[1] // kv_width
    score_scale = HEAD_DIM ** (-0.5)
    owner_dev = owner_slot // row_count
    owner_row = owner_slot % row_count
    member = (owner_dev[:, None] == jnp.arange(seq_count, dtype=jnp.int32)[None, :]).astype(
        jnp.int32
    )
    within = jnp.sum(jnp.cumsum(member, 0) * member, 1) - 1
    placed = owner_dev * capacity + within

    def pack_rows(matrix):
        return (
            jnp.zeros((slots, matrix.shape[1]), matrix.dtype)
            .at[placed]
            .set(matrix)
            .reshape(seq_count, capacity, matrix.shape[1])
        )

    vacant = jnp.array([row_count // 16, row_count % 16], jnp.float32)
    row_codes = jnp.stack([owner_row // 16, owner_row % 16], 1).astype(jnp.float32)
    code_buffer = (
        jnp.broadcast_to(vacant, (slots, 2))
        .at[placed]
        .set(row_codes)
        .astype(jnp.bfloat16)
        .reshape(seq_count, capacity, 2)
    )
    q_in, k_in, v_in, g_in, codes_in = (
        lax.all_to_all(pack_rows(queries), "seq", split_axis=0, concat_axis=0, tiled=True),
        lax.all_to_all(pack_rows(key_rows), "seq", split_axis=0, concat_axis=0, tiled=True),
        lax.all_to_all(pack_rows(value_rows), "seq", split_axis=0, concat_axis=0, tiled=True),
        lax.all_to_all(pack_rows(out_grad), "seq", split_axis=0, concat_axis=0, tiled=True),
        lax.all_to_all(code_buffer, "seq", split_axis=0, concat_axis=0, tiled=True),
    )
    arrived = codes_in.reshape(slots, 2).astype(jnp.float32)
    target = (arrived[:, 0] * 16.0 + arrived[:, 1]).astype(jnp.int32)

    def unpack_rows(buffer):
        flat_rows = buffer.reshape(slots, buffer.shape[2])
        return (
            jnp.zeros((row_count, flat_rows.shape[1]), flat_rows.dtype)
            .at[target]
            .set(flat_rows, mode="drop")
        )

    q_own = unpack_rows(q_in)
    k_own = unpack_rows(k_in)
    v_own = unpack_rows(v_in)
    g_own = unpack_rows(g_in)
    blocks = row_count // BLOCK
    span = block_links.shape[1]
    offset = (
        jnp.arange(3 * blocks, dtype=jnp.int32)[None, :]
        - jnp.arange(blocks, dtype=jnp.int32)[:, None]
    )
    selector = offset[:, :, None] == jnp.arange(span, dtype=jnp.int32)[None, None, :]
    allowed = jnp.sum(jnp.where(selector, block_links[:, None, :], 0), 2) > 0
    token_mask = jnp.repeat(jnp.repeat(allowed, BLOCK, 0), BLOCK, 1)
    kv_pair = jnp.concatenate([k_own, v_own], 1)
    kv_wide = padded(kv_pair, (("seq", 0),), row_count)

    def scores_of(q_group, k_group):
        raw_scores = (
            jnp.einsum("rgd,kd->grk", q_group, k_group, preferred_element_type=jnp.float32)
            * score_scale
        )
        return jnp.where(token_mask[None], raw_scores, -jnp.inf)

    def forward_head(operands):
        q_group, k_group, v_group = operands
        scores = scores_of(q_group, k_group)
        row_top = jnp.max(scores, -1, keepdims=True)
        log_total = row_top + jnp.log(jnp.sum(jnp.exp(scores - row_top), -1, keepdims=True))
        probs = jnp.exp(scores - log_total).astype(jnp.bfloat16)
        attended = jnp.einsum(
            "grk,kd->rgd", probs, v_group, preferred_element_type=jnp.float32
        ).astype(jnp.bfloat16)
        return (attended, log_total)

    def backward_head(operands):
        q_group, k_group, v_group, g_group, attended, log_total = operands
        weights = jnp.exp(scores_of(q_group, k_group) - log_total)
        row_delta = jnp.sum(g_group.astype(jnp.float32) * attended.astype(jnp.float32), -1).T[
            :, :, None
        ]
        d_probs = jnp.einsum("rgd,kd->grk", g_group, v_group, preferred_element_type=jnp.float32)
        d_scores = (weights * (d_probs - row_delta)).astype(jnp.bfloat16)
        q_grad = (
            jnp.einsum("grk,kd->rgd", d_scores, k_group, preferred_element_type=jnp.float32)
            * score_scale
        ).astype(jnp.bfloat16)
        k_grad = (
            jnp.einsum("grk,rgd->kd", d_scores, q_group, preferred_element_type=jnp.float32)
            * score_scale
        )
        v_grad = jnp.einsum(
            "grk,rgd->kd", weights.astype(jnp.bfloat16), g_group, preferred_element_type=jnp.float32
        )
        return (q_grad, k_grad, v_grad)

    query_heads = q_own.reshape(row_count, kv_heads, group_size, HEAD_DIM).transpose(1, 0, 2, 3)
    grad_heads = g_own.reshape(row_count, kv_heads, group_size, HEAD_DIM).transpose(1, 0, 2, 3)
    key_heads = head_major(kv_wide[:, :kv_width], kv_heads)
    value_heads = head_major(kv_wide[:, kv_width:], kv_heads)
    attended, log_total = lax.map(forward_head, (query_heads, key_heads, value_heads))
    q_grads, k_grads, v_grads = lax.map(
        backward_head, (query_heads, key_heads, value_heads, grad_heads, attended, log_total)
    )
    q_grad_own = q_grads.transpose(1, 0, 2, 3).reshape(row_count, kv_heads * group_size * HEAD_DIM)
    kv_grads = jnp.concatenate(
        [
            k_grads.transpose(1, 0, 2).reshape(3 * row_count, kv_width),
            v_grads.transpose(1, 0, 2).reshape(3 * row_count, kv_width),
        ],
        1,
    )
    from_above = from_behind(kv_grads[:row_count].astype(jnp.bfloat16), "seq", -1).astype(
        jnp.float32
    )
    from_below = from_behind(kv_grads[2 * row_count :].astype(jnp.bfloat16), "seq", 1).astype(
        jnp.float32
    )
    kv_total = (kv_grads[row_count : 2 * row_count] + from_above + from_below).astype(jnp.bfloat16)
    pick_rows = jnp.minimum(target, row_count - 1)

    def gather_back(matrix):
        return matrix[pick_rows].reshape(seq_count, capacity, matrix.shape[1])

    q_back, k_back, v_back = (
        lax.all_to_all(gather_back(q_grad_own), "seq", split_axis=0, concat_axis=0, tiled=True),
        lax.all_to_all(
            gather_back(kv_total[:, :kv_width]), "seq", split_axis=0, concat_axis=0, tiled=True
        ),
        lax.all_to_all(
            gather_back(kv_total[:, kv_width:]), "seq", split_axis=0, concat_axis=0, tiled=True
        ),
    )

    def settle_rows(buffer):
        return buffer.reshape(slots, buffer.shape[2])[placed]

    return (settle_rows(q_back), settle_rows(k_back), settle_rows(v_back))


LOG2_E = 1.4426950408889634
MASKED = -1e30
LANES = 128
NT = (((1,), (1,)), ((), ()))
NN = (((1,), (0,)), ((), ()))
IN_VMEM = pl.BlockSpec(memory_space=pltpu.VMEM)
IN_SMEM = pl.BlockSpec(memory_space=pltpu.SMEM)


def dot(a, b, dims):
    return lax.dot_general(a, b, dims, preferred_element_type=jnp.float32)


def flip(a):
    return a.astype(jnp.float32).T.astype(jnp.bfloat16)


def columns(ref, at):
    return ref[:, at * HEAD_DIM : (at + 1) * HEAD_DIM]


def stacked_heads(ref, head, group):
    return jnp.concatenate([columns(ref, head * group + j) for j in range(group)], 0)


def masks_kernel(peers, blocks_dev, span, order_ref, notes_ref, slots_ref, key_hot_ref, query_mask_ref):
    f32, bf16 = jnp.float32, jnp.bfloat16
    rows = lax.broadcasted_iota(jnp.int32, (LANES, LANES), 0)
    lanes = lax.broadcasted_iota(jnp.int32, (LANES, LANES), 1)
    slot_rows = slots_ref.shape[0]

    def hot(slots):
        return (rows == slots // BLOCK).astype(f32).T.astype(bf16)

    for r in range(peers):
        shard = notes_ref[order_ref[r]]
        for i in range(slot_rows):
            key_hot_ref[r, i * LANES : (i + 1) * LANES, :] = hot(shard[i : i + 1, :])
    owners = lax.broadcasted_iota(jnp.int32, (LANES, peers), 0) // blocks_dev
    spread = (owners == lax.broadcasted_iota(jnp.int32, (LANES, peers), 1)).astype(f32)
    link_rows = jnp.concatenate([notes_ref[p][slot_rows : slot_rows + 1, :] for p in range(peers)], 0).astype(f32)
    of_block = dot(spread, link_rows, NN)
    table = jnp.zeros((LANES, LANES), f32)
    for s in range(span):
        picked = jnp.sum(jnp.where(lanes == (rows % blocks_dev) * span + s, of_block, 0.0), 1, keepdims=True)
        table = table + jnp.where(lanes == rows + s - span // 2, picked, 0.0)
    table = table.astype(bf16)
    for i in range(slot_rows):
        linked = dot(hot(slots_ref[i : i + 1, :]), table, NN)
        query_mask_ref[i * LANES : (i + 1) * LANES, :] = jnp.where(linked > 0.5, 0.0, MASKED).astype(bf16)


def keys_of(shards, head):
    return jnp.concatenate([columns(k, head) for k, _, _ in shards], 0)


def values_of(shards, head):
    return jnp.concatenate([columns(v, head) for _, v, _ in shards], 0)


def split(refs, count, hot_ref, at):
    shards = []
    for i in range(count):
        shards.append((refs[i].at[0], refs[i].at[1], hot_ref.at[at[i]]))
    return shards


def masked_scores(q_ref, mask, shards, hots, head, group):
    queries = jnp.concatenate([stacked_heads(q_ref, head, group), jnp.concatenate([mask] * group, 0)], 1)
    return dot(jnp.concatenate([keys_of(shards, head), hots], 1), queries, NT)


def absorb(scores, values, state):
    factor = HEAD_DIM ** (-0.5) * LOG2_E
    top = jnp.max(scores, 0, keepdims=True)
    if state is not None:
        top = jnp.maximum(top, state[0])
    weights = jnp.exp2((scores - top) * factor)
    total = jnp.sum(weights, 0, keepdims=True)
    mixed = dot(flip(values), weights.astype(jnp.bfloat16), NN)
    if state is not None:
        keep = jnp.exp2((state[0] - top) * factor)
        total = total + state[1] * keep
        mixed = mixed + state[2] * keep
    return top, total, mixed


def backprop(q_ref, g_ref, shards, scores, head, group, norm, delta):
    scale = HEAD_DIM ** (-0.5)
    queries, grads = stacked_heads(q_ref, head, group), stacked_heads(g_ref, head, group)
    weights = jnp.exp2(scores * (scale * LOG2_E) - norm)
    d_scores = (weights * (dot(values_of(shards, head), grads, NT) - delta)).astype(jnp.bfloat16)
    k_grad = dot(d_scores, queries, NN) * scale
    v_grad = dot(weights.astype(jnp.bfloat16), grads, NN)
    return k_grad, v_grad, dot(flip(keys_of(shards, head)), d_scores, NN)


def forward_kernel(at, heads, group, q_ref, mask_ref, hot_ref, *refs):
    shards = split(refs, len(at), hot_ref, at)
    state, outs = refs[len(at) : -3], refs[-3:]
    hots = jnp.concatenate([hot[...] for _, _, hot in shards], 0)
    for head in range(heads):
        scores = masked_scores(q_ref, mask_ref[...], shards, hots, head, group)
        before = [s[head] for s in state] if state else None
        for out, value in zip(outs, absorb(scores, values_of(shards, head), before)):
            out[head] = value


def turn_kernel(at, heads, group, q_ref, g_ref, mask_ref, hot_ref, k_ref, v_ref, top, total, mixed, norm_ref, delta_ref, q_out, k_out, v_out):
    shards = [(k_ref, v_ref, hot_ref.at[at])]
    for head in range(heads):
        scores = masked_scores(q_ref, mask_ref[...], shards, hot_ref[at], head, group)
        state = absorb(scores, values_of(shards, head), (top[head], total[head], mixed[head]))
        norm = state[0] * (HEAD_DIM ** (-0.5) * LOG2_E) + jnp.log2(state[1])
        attended = (state[2] / state[1]).astype(jnp.bfloat16).astype(jnp.float32)
        grads = stacked_heads(g_ref, head, group).astype(jnp.float32).T
        delta = jnp.sum(grads * attended, 0, keepdims=True)
        norm_ref[head], delta_ref[head] = norm, delta
        k_grad, v_grad, q_out[head] = backprop(q_ref, g_ref, shards, scores, head, group, norm, delta)
        span = slice(head * HEAD_DIM, (head + 1) * HEAD_DIM)
        k_out[:, span], v_out[:, span] = k_grad.astype(jnp.bfloat16), v_grad.astype(jnp.bfloat16)


def backward_kernel(at, heads, group, last, q_ref, g_ref, mask_ref, hot_ref, *refs):
    count = len(at)
    shards = split(refs, count, hot_ref, at)
    norm_ref, delta_ref, q_in, q_out = refs[count : count + 4]
    hots = jnp.concatenate([hot[...] for _, _, hot in shards], 0)
    rows = q_ref.shape[0]
    for head in range(heads):
        scores = masked_scores(q_ref, mask_ref[...], shards, hots, head, group)
        k_grad, v_grad, q_terms = backprop(q_ref, g_ref, shards, scores, head, group, norm_ref[head], delta_ref[head])
        span = slice(head * HEAD_DIM, (head + 1) * HEAD_DIM)
        for i, out in enumerate(refs[count + 4 :]):
            out[0, :, span] = k_grad[i * rows : (i + 1) * rows]
            out[1, :, span] = v_grad[i * rows : (i + 1) * rows]
        q_sums = q_in[head] + q_terms
        if last:
            q_sums = q_sums * HEAD_DIM ** (-0.5)
            for j in range(group):
                part = q_sums[:, j * rows : (j + 1) * rows].T
                q_out[:, (head * group + j) * HEAD_DIM : (head * group + j + 1) * HEAD_DIM] = part.astype(jnp.bfloat16)
        else:
            q_out[head] = q_sums


def gather_plan(queries, key_rows, value_rows, out_grad, owner_slot, block_links):
    rows = queries.shape[0]
    peers = lax.axis_size("seq")
    half = peers // 2
    width = key_rows.shape[1]
    heads = width // HEAD_DIM
    group = queries.shape[1] // width
    f32, bf16 = jnp.float32, jnp.bfloat16
    ring = list(range(0, peers, 2)) + list(range(peers - 1, 0, -2))
    onward = [(ring[i], ring[(i + 1) % peers]) for i in range(peers)]
    back = [(b, a) for a, b in onward]

    def send_on(value):
        return lax.ppermute(value, "seq", onward)

    def send_back(value):
        return lax.ppermute(value, "seq", back)

    def call(kernel, args, outs, products, aliases):
        return pl.pallas_call(
            kernel,
            in_specs=[IN_VMEM] * len(args),
            out_specs=[IN_VMEM] * len(outs),
            out_shape=outs,
            input_output_aliases=aliases,
            cost_estimate=pl.CostEstimate(
                flops=4 * products * heads * group * rows * rows * HEAD_DIM, bytes_accessed=4 * rows * width, transcendentals=0
            ),
            compiler_params=pltpu.CompilerParams(vmem_limit_bytes=32 * 1024 * 1024),
        )(*args)

    own = jnp.stack([key_rows, value_rows])
    span = block_links.shape[1]
    slots = owner_slot.reshape(rows // LANES, LANES)
    links = jnp.pad(block_links.reshape(1, -1), ((0, 0), (0, LANES - block_links.size)))
    notes = jnp.concatenate([slots, links], 0)
    notes = jnp.pad(notes, ((0, -notes.shape[0] % 8), (0, 0)))
    notes = jnp.broadcast_to(notes[None], (peers,) + notes.shape)
    notes = lax.all_to_all(notes, "seq", split_axis=0, concat_axis=0, tiled=True)
    behind, ahead = [own], [own]
    for r in range(1, half):
        low, high = send_on(behind[-1]), send_back(ahead[-1])
        if r == 1:
            low, high, notes = lax.optimization_barrier((low, high, notes))
        else:
            low, high = lax.optimization_barrier((low, high))
        behind.append(low)
        ahead.append(high)
    far = (send_on(behind[-1][0]), send_back(ahead[-1][1]))
    me = lax.axis_index("seq")
    place = jnp.where(me % 2 == 0, me // 2, peers - (me + 1) // 2)
    place = (place - jnp.arange(peers, dtype=jnp.int32)) % peers
    order = jnp.where(place < half, 2 * place, 2 * peers - 1 - 2 * place)
    hot, mask = pl.pallas_call(
        functools.partial(masks_kernel, peers, rows // BLOCK, span),
        in_specs=[IN_SMEM, IN_VMEM, IN_VMEM],
        out_specs=[IN_VMEM] * 2,
        out_shape=[jax.ShapeDtypeStruct((peers, rows, LANES), bf16), jax.ShapeDtypeStruct((rows, LANES), bf16)],
        compiler_params=pltpu.CompilerParams(vmem_limit_bytes=32 * 1024 * 1024),
    )(order, notes, slots)

    lines = jax.ShapeDtypeStruct((heads, 1, group * rows), f32)
    talls = jax.ShapeDtypeStruct((heads, HEAD_DIM, group * rows), f32)
    pairs = jax.ShapeDtypeStruct((2, rows, width), f32)
    single = jax.ShapeDtypeStruct((rows, width), bf16)

    def forward(shards, at, state):
        args = [queries, mask, hot, *shards, *state]
        kernel = functools.partial(forward_kernel, at, heads, group)
        aliases = {len(args) - 3 + i: i for i in range(3)} if state else {}
        return call(kernel, args, [lines, lines, talls], 2 * len(at), aliases)

    def backward(shards, at, q_sums, last=False):
        args = [queries, out_grad, mask, hot, *shards, norm, delta, q_sums]
        q_out = jax.ShapeDtypeStruct(queries.shape, bf16) if last else talls
        kernel = functools.partial(backward_kernel, at, heads, group, last)
        return call(kernel, args, [q_out] + [pairs] * len(at), 5 * len(at), {} if last else {len(args) - 1: 0})

    near = [own] + ([behind[1], ahead[1]] if half > 1 else [])
    state = forward(near, (0, 1, peers - 1)[: len(near)], ())
    for r in range(2, half):
        state = forward([behind[r], ahead[r]], (r, peers - r), state)
    norm, delta, q_sums, far_k, far_v = call(
        functools.partial(turn_kernel, half, heads, group),
        [queries, out_grad, mask, hot, *far, *state],
        [lines, lines, talls, single, single],
        7,
        {6: 0, 7: 1, 8: 2},
    )
    down, up = send_back(far_k), send_on(far_v)
    for r in range(half - 1, 0, -1):
        q_sums, low, high = backward([behind[r], ahead[r]], (r, peers - r), q_sums)
        if r == half - 1:
            low = jnp.stack([low[0] + down.astype(f32), low[1]])
            high = jnp.stack([high[0], high[1] + up.astype(f32)])
        else:
            low, high = low + down.astype(f32), high + up.astype(f32)
        down, up = send_back(low.astype(bf16)), send_on(high.astype(bf16))
    query_grad, mine = backward([own], (0,), q_sums, True)
    if half == 1:
        total = jnp.stack([mine[0] + down.astype(f32), mine[1] + up.astype(f32)])
    else:
        total = mine + down.astype(f32) + up.astype(f32)
    return query_grad, total[0].astype(bf16), total[1].astype(bf16)


def local(queries, key_rows, value_rows, out_grad, owner_slot, block_links):
    rows = queries.shape[0]
    peers = lax.axis_size("seq")
    q_width, kv_width = queries.shape[1], key_rows.shape[1]
    slots = 4 * peers * max(1, rows // peers // 2)
    gathered = 2 * (peers - 1) * rows * 2 * kv_width
    relayed = slots * (3 * q_width + 4 * kv_width) + 4 * rows * 2 * kv_width
    fits = peers % 2 == 0 and rows % LANES == 0 and peers * rows // BLOCK <= LANES and block_links.size <= LANES
    plan = gather_plan if fits and gathered <= relayed else relay_plan
    return plan(queries, key_rows, value_rows, out_grad, owner_slot, block_links)


def solution(mesh):
    return jax.shard_map(
        local,
        mesh=mesh,
        in_specs=(
            P(("parts", "seq"), "head"),
            P(("parts", "seq"), "head"),
            P(("parts", "seq"), "head"),
            P(("parts", "seq"), "head"),
            P(("parts", "seq")),
            P(("parts", "seq"), None),
        ),
        out_specs=(
            P(("parts", "seq"), "head"),
            P(("parts", "seq"), "head"),
            P(("parts", "seq"), "head"),
        ),
        check_vma=False,
    )
```

```python
import functools

import jax
import jax.numpy as jnp
from jax import lax
from jax.experimental import pallas as pl
from jax.experimental.pallas import tpu as pltpu
from jax.sharding import PartitionSpec as P

HEAD_DIM = 128
BLOCK = 128


def padded(value, sides, width):
    for axis, dim in sides:
        peers, length = (lax.axis_size(axis), value.shape[dim])
        up = [(i, (i + 1) % peers) for i in range(peers - 1)]
        down = [(j, i) for i, j in up]
        last = lax.slice_in_dim(value, length - width, length, axis=dim)
        leading = lax.slice_in_dim(value, 0, width, axis=dim)
        before = lax.ppermute(last, axis, up)
        after = lax.ppermute(leading, axis, down)
        value = jnp.concatenate([before, value, after], axis=dim)
    return value


def from_behind(value, axis, by):
    peers = lax.axis_size(axis)
    pairs = [(i, i + by) for i in range(peers) if 0 <= i + by < peers]
    return lax.ppermute(value, axis, pairs)


def head_major(matrix, heads):
    return matrix.reshape(matrix.shape[0], heads, -1).transpose(1, 0, 2)


def relay_plan(queries, key_rows, value_rows, out_grad, owner_slot, block_links):
    row_count = queries.shape[0]
    seq_count = lax.axis_size("seq")
    capacity = 4 * max(1, row_count // seq_count // 2)
    slots = seq_count * capacity
    kv_width = key_rows.shape[1]
    kv_heads = kv_width // HEAD_DIM
    group_size = queries.shape[1] // kv_width
    score_scale = HEAD_DIM ** (-0.5)
    owner_dev = owner_slot // row_count
    owner_row = owner_slot % row_count
    member = (owner_dev[:, None] == jnp.arange(seq_count, dtype=jnp.int32)[None, :]).astype(
        jnp.int32
    )
    within = jnp.sum(jnp.cumsum(member, 0) * member, 1) - 1
    placed = owner_dev * capacity + within

    def pack_rows(matrix):
        return (
            jnp.zeros((slots, matrix.shape[1]), matrix.dtype)
            .at[placed]
            .set(matrix)
            .reshape(seq_count, capacity, matrix.shape[1])
        )

    vacant = jnp.array([row_count // 16, row_count % 16], jnp.float32)
    row_codes = jnp.stack([owner_row // 16, owner_row % 16], 1).astype(jnp.float32)
    code_buffer = (
        jnp.broadcast_to(vacant, (slots, 2))
        .at[placed]
        .set(row_codes)
        .astype(jnp.bfloat16)
        .reshape(seq_count, capacity, 2)
    )
    q_in, k_in, v_in, g_in, codes_in = (
        lax.all_to_all(pack_rows(queries), "seq", split_axis=0, concat_axis=0, tiled=True),
        lax.all_to_all(pack_rows(key_rows), "seq", split_axis=0, concat_axis=0, tiled=True),
        lax.all_to_all(pack_rows(value_rows), "seq", split_axis=0, concat_axis=0, tiled=True),
        lax.all_to_all(pack_rows(out_grad), "seq", split_axis=0, concat_axis=0, tiled=True),
        lax.all_to_all(code_buffer, "seq", split_axis=0, concat_axis=0, tiled=True),
    )
    arrived = codes_in.reshape(slots, 2).astype(jnp.float32)
    target = (arrived[:, 0] * 16.0 + arrived[:, 1]).astype(jnp.int32)

    def unpack_rows(buffer):
        flat_rows = buffer.reshape(slots, buffer.shape[2])
        return (
            jnp.zeros((row_count, flat_rows.shape[1]), flat_rows.dtype)
            .at[target]
            .set(flat_rows, mode="drop")
        )

    q_own = unpack_rows(q_in)
    k_own = unpack_rows(k_in)
    v_own = unpack_rows(v_in)
    g_own = unpack_rows(g_in)
    blocks = row_count // BLOCK
    span = block_links.shape[1]
    offset = (
        jnp.arange(3 * blocks, dtype=jnp.int32)[None, :]
        - jnp.arange(blocks, dtype=jnp.int32)[:, None]
    )
    selector = offset[:, :, None] == jnp.arange(span, dtype=jnp.int32)[None, None, :]
    allowed = jnp.sum(jnp.where(selector, block_links[:, None, :], 0), 2) > 0
    token_mask = jnp.repeat(jnp.repeat(allowed, BLOCK, 0), BLOCK, 1)
    kv_pair = jnp.concatenate([k_own, v_own], 1)
    kv_wide = padded(kv_pair, (("seq", 0),), row_count)

    def scores_of(q_group, k_group):
        raw_scores = (
            jnp.einsum("rgd,kd->grk", q_group, k_group, preferred_element_type=jnp.float32)
            * score_scale
        )
        return jnp.where(token_mask[None], raw_scores, -jnp.inf)

    def forward_head(operands):
        q_group, k_group, v_group = operands
        scores = scores_of(q_group, k_group)
        row_top = jnp.max(scores, -1, keepdims=True)
        log_total = row_top + jnp.log(jnp.sum(jnp.exp(scores - row_top), -1, keepdims=True))
        probs = jnp.exp(scores - log_total).astype(jnp.bfloat16)
        attended = jnp.einsum(
            "grk,kd->rgd", probs, v_group, preferred_element_type=jnp.float32
        ).astype(jnp.bfloat16)
        return (attended, log_total)

    def backward_head(operands):
        q_group, k_group, v_group, g_group, attended, log_total = operands
        weights = jnp.exp(scores_of(q_group, k_group) - log_total)
        row_delta = jnp.sum(g_group.astype(jnp.float32) * attended.astype(jnp.float32), -1).T[
            :, :, None
        ]
        d_probs = jnp.einsum("rgd,kd->grk", g_group, v_group, preferred_element_type=jnp.float32)
        d_scores = (weights * (d_probs - row_delta)).astype(jnp.bfloat16)
        q_grad = (
            jnp.einsum("grk,kd->rgd", d_scores, k_group, preferred_element_type=jnp.float32)
            * score_scale
        ).astype(jnp.bfloat16)
        k_grad = (
            jnp.einsum("grk,rgd->kd", d_scores, q_group, preferred_element_type=jnp.float32)
            * score_scale
        )
        v_grad = jnp.einsum(
            "grk,rgd->kd", weights.astype(jnp.bfloat16), g_group, preferred_element_type=jnp.float32
        )
        return (q_grad, k_grad, v_grad)

    query_heads = q_own.reshape(row_count, kv_heads, group_size, HEAD_DIM).transpose(1, 0, 2, 3)
    grad_heads = g_own.reshape(row_count, kv_heads, group_size, HEAD_DIM).transpose(1, 0, 2, 3)
    key_heads = head_major(kv_wide[:, :kv_width], kv_heads)
    value_heads = head_major(kv_wide[:, kv_width:], kv_heads)
    attended, log_total = lax.map(forward_head, (query_heads, key_heads, value_heads))
    q_grads, k_grads, v_grads = lax.map(
        backward_head, (query_heads, key_heads, value_heads, grad_heads, attended, log_total)
    )
    q_grad_own = q_grads.transpose(1, 0, 2, 3).reshape(row_count, kv_heads * group_size * HEAD_DIM)
    kv_grads = jnp.concatenate(
        [
            k_grads.transpose(1, 0, 2).reshape(3 * row_count, kv_width),
            v_grads.transpose(1, 0, 2).reshape(3 * row_count, kv_width),
        ],
        1,
    )
    from_above = from_behind(kv_grads[:row_count].astype(jnp.bfloat16), "seq", -1).astype(
        jnp.float32
    )
    from_below = from_behind(kv_grads[2 * row_count :].astype(jnp.bfloat16), "seq", 1).astype(
        jnp.float32
    )
    kv_total = (kv_grads[row_count : 2 * row_count] + from_above + from_below).astype(jnp.bfloat16)
    pick_rows = jnp.minimum(target, row_count - 1)

    def gather_back(matrix):
        return matrix[pick_rows].reshape(seq_count, capacity, matrix.shape[1])

    q_back, k_back, v_back = (
        lax.all_to_all(gather_back(q_grad_own), "seq", split_axis=0, concat_axis=0, tiled=True),
        lax.all_to_all(
            gather_back(kv_total[:, :kv_width]), "seq", split_axis=0, concat_axis=0, tiled=True
        ),
        lax.all_to_all(
            gather_back(kv_total[:, kv_width:]), "seq", split_axis=0, concat_axis=0, tiled=True
        ),
    )

    def settle_rows(buffer):
        return buffer.reshape(slots, buffer.shape[2])[placed]

    return (settle_rows(q_back), settle_rows(k_back), settle_rows(v_back))


LOG2_E = 1.4426950408889634
MASKED = -1e30
LANES = 128
NT = (((1,), (1,)), ((), ()))
NN = (((1,), (0,)), ((), ()))
IN_VMEM = pl.BlockSpec(memory_space=pltpu.VMEM)
IN_SMEM = pl.BlockSpec(memory_space=pltpu.SMEM)


def dot(a, b, dims):
    return lax.dot_general(a, b, dims, preferred_element_type=jnp.float32)


def flip(a):
    return a.astype(jnp.float32).T.astype(jnp.bfloat16)


def columns(ref, at):
    return ref[:, at * HEAD_DIM : (at + 1) * HEAD_DIM]


def stacked_heads(ref, head, group):
    return jnp.concatenate([columns(ref, head * group + j) for j in range(group)], 0)


def masks_kernel(peers, blocks_dev, span, order_ref, notes_ref, slots_ref, key_hot_ref, query_mask_ref):
    f32, bf16 = jnp.float32, jnp.bfloat16
    rows = lax.broadcasted_iota(jnp.int32, (LANES, LANES), 0)
    lanes = lax.broadcasted_iota(jnp.int32, (LANES, LANES), 1)
    slot_rows = slots_ref.shape[0]

    def hot(slots):
        return (rows == slots // BLOCK).astype(f32).T.astype(bf16)

    for r in range(peers):
        shard = notes_ref[order_ref[r]]
        for i in range(slot_rows):
            key_hot_ref[r, i * LANES : (i + 1) * LANES, :] = hot(shard[i : i + 1, :])
    owners = lax.broadcasted_iota(jnp.int32, (LANES, peers), 0) // blocks_dev
    spread = (owners == lax.broadcasted_iota(jnp.int32, (LANES, peers), 1)).astype(f32)
    link_rows = jnp.concatenate([notes_ref[p][slot_rows : slot_rows + 1, :] for p in range(peers)], 0).astype(f32)
    of_block = dot(spread, link_rows, NN)
    table = jnp.zeros((LANES, LANES), f32)
    for s in range(span):
        picked = jnp.sum(jnp.where(lanes == (rows % blocks_dev) * span + s, of_block, 0.0), 1, keepdims=True)
        table = table + jnp.where(lanes == rows + s - span // 2, picked, 0.0)
    table = table.astype(bf16)
    for i in range(slot_rows):
        linked = dot(hot(slots_ref[i : i + 1, :]), table, NN)
        query_mask_ref[i * LANES : (i + 1) * LANES, :] = jnp.where(linked > 0.5, 0.0, MASKED).astype(bf16)


def keys_of(shards, head):
    return jnp.concatenate([columns(k, head) for k, _, _ in shards], 0)


def values_of(shards, head):
    return jnp.concatenate([columns(v, head) for _, v, _ in shards], 0)


def split(refs, count, hot_ref, at):
    shards = []
    for i in range(count):
        shards.append((refs[i].at[0], refs[i].at[1], hot_ref.at[at[i]]))
    return shards


def masked_scores(q_ref, mask, shards, hots, head, group, first):
    queries = jnp.concatenate([stacked_heads(q_ref, first + head, group), jnp.concatenate([mask] * group, 0)], 1)
    return dot(jnp.concatenate([keys_of(shards, head), hots], 1), queries, NT)


def absorb(scores, values, state):
    factor = HEAD_DIM ** (-0.5) * LOG2_E
    top = jnp.max(scores, 0, keepdims=True)
    if state is not None:
        top = jnp.maximum(top, state[0])
    weights = jnp.exp2((scores - top) * factor)
    total = jnp.sum(weights, 0, keepdims=True)
    mixed = dot(flip(values), weights.astype(jnp.bfloat16), NN)
    if state is not None:
        keep = jnp.exp2((state[0] - top) * factor)
        total = total + state[1] * keep
        mixed = mixed + state[2] * keep
    return top, total, mixed


def backprop(q_ref, g_ref, shards, scores, head, group, first, norm, delta):
    scale = HEAD_DIM ** (-0.5)
    queries, grads = stacked_heads(q_ref, first + head, group), stacked_heads(g_ref, first + head, group)
    weights = jnp.exp2(scores * (scale * LOG2_E) - norm)
    d_scores = (weights * (dot(values_of(shards, head), grads, NT) - delta)).astype(jnp.bfloat16)
    k_grad = dot(d_scores, queries, NN) * scale
    v_grad = dot(weights.astype(jnp.bfloat16), grads, NN)
    return k_grad, v_grad, dot(flip(keys_of(shards, head)), d_scores, NN)


def forward_kernel(at, heads, group, first, q_ref, mask_ref, hot_ref, *refs):
    shards = split(refs, len(at), hot_ref, at)
    state, outs = refs[len(at) : -3], refs[-3:]
    hots = jnp.concatenate([hot[...] for _, _, hot in shards], 0)
    for head in range(heads):
        scores = masked_scores(q_ref, mask_ref[...], shards, hots, head, group, first)
        before = [s[head] for s in state] if state else None
        for out, value in zip(outs, absorb(scores, values_of(shards, head), before)):
            out[head] = value


def turn_kernel(at, heads, group, first, q_ref, g_ref, mask_ref, hot_ref, far_ref, top, total, mixed, norm_ref, delta_ref, q_out, grads_out):
    shards = split([far_ref], 1, hot_ref, (at,))
    for head in range(heads):
        scores = masked_scores(q_ref, mask_ref[...], shards, hot_ref[at], head, group, first)
        state = absorb(scores, values_of(shards, head), (top[head], total[head], mixed[head]))
        norm = state[0] * (HEAD_DIM ** (-0.5) * LOG2_E) + jnp.log2(state[1])
        attended = (state[2] / state[1]).astype(jnp.bfloat16).astype(jnp.float32)
        grads = stacked_heads(g_ref, first + head, group).astype(jnp.float32).T
        delta = jnp.sum(grads * attended, 0, keepdims=True)
        norm_ref[head], delta_ref[head] = norm, delta
        k_grad, v_grad, q_out[head] = backprop(q_ref, g_ref, shards, scores, head, group, first, norm, delta)
        store_grads([grads_out], head, k_grad, v_grad)


def backward_kernel(at, heads, group, first, q_ref, g_ref, mask_ref, hot_ref, *refs):
    count = len(at)
    shards = split(refs, count, hot_ref, at)
    norm_ref, delta_ref, q_in, q_out = refs[count : count + 4]
    hots = jnp.concatenate([hot[...] for _, _, hot in shards], 0)
    for head in range(heads):
        scores = masked_scores(q_ref, mask_ref[...], shards, hots, head, group, first)
        k_grad, v_grad, q_terms = backprop(q_ref, g_ref, shards, scores, head, group, first, norm_ref[head], delta_ref[head])
        store_grads(refs[count + 4 :], head, k_grad, v_grad)
        q_out[head] = q_in[head] + q_terms


def store_grads(outs, head, k_grad, v_grad):
    span = slice(head * HEAD_DIM, (head + 1) * HEAD_DIM)
    for i, out in enumerate(outs):
        rows = out.shape[1]
        out[0, :, span] = k_grad[i * rows : (i + 1) * rows].astype(out.dtype)
        out[1, :, span] = v_grad[i * rows : (i + 1) * rows].astype(out.dtype)


def last_kernel(chunks, heads, group, q_ref, g_ref, mask_ref, hot_ref, *refs):
    outs = refs[4 * chunks :]
    rows = q_ref.shape[0]
    for c in range(chunks):
        own_ref, norm_ref, delta_ref, q_in = refs[4 * c : 4 * c + 4]
        shards = split([own_ref], 1, hot_ref, (0,))
        first = c * heads
        for head in range(heads):
            scores = masked_scores(q_ref, mask_ref[...], shards, hot_ref[0], head, group, first)
            k_grad, v_grad, q_terms = backprop(q_ref, g_ref, shards, scores, head, group, first, norm_ref[head], delta_ref[head])
            store_grads([outs[1 + c]], head, k_grad, v_grad)
            q_sums = (q_in[head] + q_terms) * HEAD_DIM ** (-0.5)
            for j in range(group):
                at = (first + head) * group + j
                outs[0][:, at * HEAD_DIM : (at + 1) * HEAD_DIM] = q_sums[:, j * rows : (j + 1) * rows].T.astype(jnp.bfloat16)


def gather_plan(queries, key_rows, value_rows, out_grad, owner_slot, block_links):
    rows = queries.shape[0]
    peers = lax.axis_size("seq")
    half = peers // 2
    kv_heads = key_rows.shape[1] // HEAD_DIM
    group = queries.shape[1] // key_rows.shape[1]
    chunks = 2
    heads = kv_heads // chunks
    width = heads * HEAD_DIM
    each = range(chunks)
    f32, bf16 = jnp.float32, jnp.bfloat16
    ring = list(range(0, peers, 2)) + list(range(peers - 1, 0, -2))
    onward = [(ring[i], ring[(i + 1) % peers]) for i in range(peers)]
    back = [(b, a) for a, b in onward]

    def send_on(value):
        return lax.ppermute(value, "seq", onward)

    def send_back(value):
        return lax.ppermute(value, "seq", back)

    def call(kernel, args, outs, products, aliases):
        return pl.pallas_call(
            kernel,
            in_specs=[IN_VMEM] * len(args),
            out_specs=[IN_VMEM] * len(outs),
            out_shape=outs,
            input_output_aliases=aliases,
            cost_estimate=pl.CostEstimate(
                flops=products * heads * group * rows * rows, bytes_accessed=4 * rows * width, transcendentals=0
            ),
            compiler_params=pltpu.CompilerParams(vmem_limit_bytes=32 * 1024 * 1024),
        )(*args)

    span = block_links.shape[1]
    slots = owner_slot.reshape(rows // LANES, LANES)
    links = jnp.pad(block_links.reshape(1, -1), ((0, 0), (0, LANES - block_links.size)))
    notes = jnp.concatenate([slots, links], 0)
    notes = jnp.pad(notes, ((0, -notes.shape[0] % 8), (0, 0)))[None]
    notes = lax.all_to_all(jnp.broadcast_to(notes, (peers,) + notes.shape[1:]), "seq", split_axis=0, concat_axis=0, tiled=True)
    me = lax.axis_index("seq")
    place = jnp.where(me % 2 == 0, me // 2, peers - (me + 1) // 2)
    place = (place - jnp.arange(peers, dtype=jnp.int32)) % peers
    order = jnp.where(place < half, 2 * place, 2 * peers - 1 - 2 * place)

    lines = jax.ShapeDtypeStruct((heads, 1, group * rows), f32)
    talls = jax.ShapeDtypeStruct((heads, HEAD_DIM, group * rows), f32)
    pairs = jax.ShapeDtypeStruct((2, rows, width), f32)

    def forward(c, shards, at, state):
        args = [queries, mask, hot, *shards, *state]
        kernel = functools.partial(forward_kernel, at, heads, group, c * heads)
        aliases = {len(args) - 3 + i: i for i in range(3)} if state else {}
        return call(kernel, args, [lines, lines, talls], 2 * len(at), aliases)

    def backward(c, shards, at, norm, delta, q_sums):
        args = [queries, out_grad, mask, hot, *shards, norm, delta, q_sums]
        kernel = functools.partial(backward_kernel, at, heads, group, c * heads)
        return call(kernel, args, [talls] + [pairs] * len(at), 5 * len(at), {len(args) - 1: 0})

    own = [jnp.stack([key_rows[:, c * width : (c + 1) * width], value_rows[:, c * width : (c + 1) * width]]) for c in each]
    behind, ahead = [[v] for v in own], [[v] for v in own]
    state = [() for _ in each]
    hot = mask = None

    def catch_up(c, r):
        shards, at = [behind[c][r], ahead[c][r]], (r, peers - r)
        if r == 1:
            shards, at = [own[c]] + shards, (0,) + at
        state[c] = tuple(forward(c, shards, at, state[c]))

    for r in range(1, half):
        for c in each:
            low, high = send_on(behind[c][-1]), send_back(ahead[c][-1])
            if r > 1:
                catch_up(c, r - 1)
                low, high, state[c] = lax.optimization_barrier((low, high, state[c]))
            elif c == 0:
                low, high, notes = lax.optimization_barrier((low, high, notes))
            behind[c].append(low)
            ahead[c].append(high)
        if r == 1:
            hot, mask = pl.pallas_call(
                functools.partial(masks_kernel, peers, rows // BLOCK, span),
                in_specs=[IN_SMEM, IN_VMEM, IN_VMEM],
                out_specs=[IN_VMEM] * 2,
                out_shape=[jax.ShapeDtypeStruct((peers, rows, LANES), bf16), jax.ShapeDtypeStruct((rows, LANES), bf16)],
                compiler_params=pltpu.CompilerParams(vmem_limit_bytes=32 * 1024 * 1024),
            )(order, notes, slots)
    far = [send_back(ahead[c][-1]) if c % 2 else send_on(behind[c][-1]) for c in each]
    norm, delta, q_sums, down, up = [[None] * chunks for _ in range(5)]
    for c in each:
        catch_up(c, half - 1)
        norm[c], delta[c], q_sums[c], sums = call(
            functools.partial(turn_kernel, half, heads, group, c * heads),
            [queries, out_grad, mask, hot, far[c], *state[c]],
            [lines, lines, talls, jax.ShapeDtypeStruct(pairs.shape, bf16)],
            7,
            {5: 0, 6: 1, 7: 2},
        )
        if c + 1 < chunks:
            sums, state[c + 1] = lax.optimization_barrier((sums, state[c + 1]))
        else:
            sums, norm[0] = lax.optimization_barrier((sums, norm[0]))
        if c % 2:
            up[c] = send_on(sums)
        else:
            down[c] = send_back(sums)
    for r in range(half - 1, 0, -1):
        for c in each:
            q_sums[c], low, high = backward(c, [behind[c][r], ahead[c][r]], (r, peers - r), norm[c], delta[c], q_sums[c])
            low = low if down[c] is None else low + down[c].astype(f32)
            high = high if up[c] is None else high + up[c].astype(f32)
            after = (c + 1) % chunks
            low, high, norm[after] = lax.optimization_barrier((low.astype(bf16), high.astype(bf16), norm[after]))
            down[c], up[c] = send_back(low), send_on(high)
    args = [queries, out_grad, mask, hot]
    for c in each:
        args += [own[c], norm[c], delta[c], q_sums[c]]
    query_grad, *mine = call(
        functools.partial(last_kernel, chunks, heads, group),
        args,
        [jax.ShapeDtypeStruct(queries.shape, bf16)] + [pairs] * chunks,
        5 * chunks,
        {},
    )
    total = [(mine[c] + down[c].astype(f32) + up[c].astype(f32)).astype(bf16) for c in each]
    return query_grad, jnp.concatenate([t[0] for t in total], 1), jnp.concatenate([t[1] for t in total], 1)


def local(queries, key_rows, value_rows, out_grad, owner_slot, block_links):
    rows = queries.shape[0]
    peers = lax.axis_size("seq")
    q_width, kv_width = queries.shape[1], key_rows.shape[1]
    slots = 4 * peers * max(1, rows // peers // 2)
    gathered = 2 * (peers - 1) * rows * 2 * kv_width
    relayed = slots * (3 * q_width + 4 * kv_width) + 4 * rows * 2 * kv_width
    fits = kv_width % (2 * HEAD_DIM) == 0 and peers > 2 and peers & (peers - 1) == 0 and rows % LANES == 0 and peers * rows // BLOCK <= LANES and block_links.size <= LANES
    plan = gather_plan if fits and gathered <= relayed else relay_plan
    return plan(queries, key_rows, value_rows, out_grad, owner_slot, block_links)


def solution(mesh):
    return jax.shard_map(
        local,
        mesh=mesh,
        in_specs=(
            P(("parts", "seq"), "head"),
            P(("parts", "seq"), "head"),
            P(("parts", "seq"), "head"),
            P(("parts", "seq"), "head"),
            P(("parts", "seq")),
            P(("parts", "seq"), None),
        ),
        out_specs=(
            P(("parts", "seq"), "head"),
            P(("parts", "seq"), "head"),
            P(("parts", "seq"), "head"),
        ),
        check_vma=False,
    )
```

```python
import functools

import jax
import jax.numpy as jnp
from jax import lax
from jax.experimental import pallas as pl
from jax.experimental.pallas import tpu as pltpu
from jax.sharding import PartitionSpec as P

HEAD_DIM = 128
BLOCK = 128


def padded(value, sides, width):
    for axis, dim in sides:
        peers, length = (lax.axis_size(axis), value.shape[dim])
        up = [(i, (i + 1) % peers) for i in range(peers - 1)]
        down = [(j, i) for i, j in up]
        last = lax.slice_in_dim(value, length - width, length, axis=dim)
        leading = lax.slice_in_dim(value, 0, width, axis=dim)
        before = lax.ppermute(last, axis, up)
        after = lax.ppermute(leading, axis, down)
        value = jnp.concatenate([before, value, after], axis=dim)
    return value


def from_behind(value, axis, by):
    peers = lax.axis_size(axis)
    pairs = [(i, i + by) for i in range(peers) if 0 <= i + by < peers]
    return lax.ppermute(value, axis, pairs)


def head_major(matrix, heads):
    return matrix.reshape(matrix.shape[0], heads, -1).transpose(1, 0, 2)


def relay_plan(queries, key_rows, value_rows, out_grad, owner_slot, block_links):
    row_count = queries.shape[0]
    seq_count = lax.axis_size("seq")
    capacity = 4 * max(1, row_count // seq_count // 2)
    slots = seq_count * capacity
    kv_width = key_rows.shape[1]
    kv_heads = kv_width // HEAD_DIM
    group_size = queries.shape[1] // kv_width
    score_scale = HEAD_DIM ** (-0.5)
    owner_dev = owner_slot // row_count
    owner_row = owner_slot % row_count
    member = (owner_dev[:, None] == jnp.arange(seq_count, dtype=jnp.int32)[None, :]).astype(
        jnp.int32
    )
    within = jnp.sum(jnp.cumsum(member, 0) * member, 1) - 1
    placed = owner_dev * capacity + within

    def pack_rows(matrix):
        return (
            jnp.zeros((slots, matrix.shape[1]), matrix.dtype)
            .at[placed]
            .set(matrix)
            .reshape(seq_count, capacity, matrix.shape[1])
        )

    vacant = jnp.array([row_count // 16, row_count % 16], jnp.float32)
    row_codes = jnp.stack([owner_row // 16, owner_row % 16], 1).astype(jnp.float32)
    code_buffer = (
        jnp.broadcast_to(vacant, (slots, 2))
        .at[placed]
        .set(row_codes)
        .astype(jnp.bfloat16)
        .reshape(seq_count, capacity, 2)
    )
    q_in, k_in, v_in, g_in, codes_in = (
        lax.all_to_all(pack_rows(queries), "seq", split_axis=0, concat_axis=0, tiled=True),
        lax.all_to_all(pack_rows(key_rows), "seq", split_axis=0, concat_axis=0, tiled=True),
        lax.all_to_all(pack_rows(value_rows), "seq", split_axis=0, concat_axis=0, tiled=True),
        lax.all_to_all(pack_rows(out_grad), "seq", split_axis=0, concat_axis=0, tiled=True),
        lax.all_to_all(code_buffer, "seq", split_axis=0, concat_axis=0, tiled=True),
    )
    arrived = codes_in.reshape(slots, 2).astype(jnp.float32)
    target = (arrived[:, 0] * 16.0 + arrived[:, 1]).astype(jnp.int32)

    def unpack_rows(buffer):
        flat_rows = buffer.reshape(slots, buffer.shape[2])
        return (
            jnp.zeros((row_count, flat_rows.shape[1]), flat_rows.dtype)
            .at[target]
            .set(flat_rows, mode="drop")
        )

    q_own = unpack_rows(q_in)
    k_own = unpack_rows(k_in)
    v_own = unpack_rows(v_in)
    g_own = unpack_rows(g_in)
    blocks = row_count // BLOCK
    span = block_links.shape[1]
    offset = (
        jnp.arange(3 * blocks, dtype=jnp.int32)[None, :]
        - jnp.arange(blocks, dtype=jnp.int32)[:, None]
    )
    selector = offset[:, :, None] == jnp.arange(span, dtype=jnp.int32)[None, None, :]
    allowed = jnp.sum(jnp.where(selector, block_links[:, None, :], 0), 2) > 0
    token_mask = jnp.repeat(jnp.repeat(allowed, BLOCK, 0), BLOCK, 1)
    kv_pair = jnp.concatenate([k_own, v_own], 1)
    kv_wide = padded(kv_pair, (("seq", 0),), row_count)

    def scores_of(q_group, k_group):
        raw_scores = (
            jnp.einsum("rgd,kd->grk", q_group, k_group, preferred_element_type=jnp.float32)
            * score_scale
        )
        return jnp.where(token_mask[None], raw_scores, -jnp.inf)

    def forward_head(operands):
        q_group, k_group, v_group = operands
        scores = scores_of(q_group, k_group)
        row_top = jnp.max(scores, -1, keepdims=True)
        log_total = row_top + jnp.log(jnp.sum(jnp.exp(scores - row_top), -1, keepdims=True))
        probs = jnp.exp(scores - log_total).astype(jnp.bfloat16)
        attended = jnp.einsum(
            "grk,kd->rgd", probs, v_group, preferred_element_type=jnp.float32
        ).astype(jnp.bfloat16)
        return (attended, log_total)

    def backward_head(operands):
        q_group, k_group, v_group, g_group, attended, log_total = operands
        weights = jnp.exp(scores_of(q_group, k_group) - log_total)
        row_delta = jnp.sum(g_group.astype(jnp.float32) * attended.astype(jnp.float32), -1).T[
            :, :, None
        ]
        d_probs = jnp.einsum("rgd,kd->grk", g_group, v_group, preferred_element_type=jnp.float32)
        d_scores = (weights * (d_probs - row_delta)).astype(jnp.bfloat16)
        q_grad = (
            jnp.einsum("grk,kd->rgd", d_scores, k_group, preferred_element_type=jnp.float32)
            * score_scale
        ).astype(jnp.bfloat16)
        k_grad = (
            jnp.einsum("grk,rgd->kd", d_scores, q_group, preferred_element_type=jnp.float32)
            * score_scale
        )
        v_grad = jnp.einsum(
            "grk,rgd->kd", weights.astype(jnp.bfloat16), g_group, preferred_element_type=jnp.float32
        )
        return (q_grad, k_grad, v_grad)

    query_heads = q_own.reshape(row_count, kv_heads, group_size, HEAD_DIM).transpose(1, 0, 2, 3)
    grad_heads = g_own.reshape(row_count, kv_heads, group_size, HEAD_DIM).transpose(1, 0, 2, 3)
    key_heads = head_major(kv_wide[:, :kv_width], kv_heads)
    value_heads = head_major(kv_wide[:, kv_width:], kv_heads)
    attended, log_total = lax.map(forward_head, (query_heads, key_heads, value_heads))
    q_grads, k_grads, v_grads = lax.map(
        backward_head, (query_heads, key_heads, value_heads, grad_heads, attended, log_total)
    )
    q_grad_own = q_grads.transpose(1, 0, 2, 3).reshape(row_count, kv_heads * group_size * HEAD_DIM)
    kv_grads = jnp.concatenate(
        [
            k_grads.transpose(1, 0, 2).reshape(3 * row_count, kv_width),
            v_grads.transpose(1, 0, 2).reshape(3 * row_count, kv_width),
        ],
        1,
    )
    from_above = from_behind(kv_grads[:row_count].astype(jnp.bfloat16), "seq", -1).astype(
        jnp.float32
    )
    from_below = from_behind(kv_grads[2 * row_count :].astype(jnp.bfloat16), "seq", 1).astype(
        jnp.float32
    )
    kv_total = (kv_grads[row_count : 2 * row_count] + from_above + from_below).astype(jnp.bfloat16)
    pick_rows = jnp.minimum(target, row_count - 1)

    def gather_back(matrix):
        return matrix[pick_rows].reshape(seq_count, capacity, matrix.shape[1])

    q_back, k_back, v_back = (
        lax.all_to_all(gather_back(q_grad_own), "seq", split_axis=0, concat_axis=0, tiled=True),
        lax.all_to_all(
            gather_back(kv_total[:, :kv_width]), "seq", split_axis=0, concat_axis=0, tiled=True
        ),
        lax.all_to_all(
            gather_back(kv_total[:, kv_width:]), "seq", split_axis=0, concat_axis=0, tiled=True
        ),
    )

    def settle_rows(buffer):
        return buffer.reshape(slots, buffer.shape[2])[placed]

    return (settle_rows(q_back), settle_rows(k_back), settle_rows(v_back))


LOG2_E = 1.4426950408889634
MASKED = -1e30
LANES = 128
NT = (((1,), (1,)), ((), ()))
NN = (((1,), (0,)), ((), ()))
IN_VMEM = pl.BlockSpec(memory_space=pltpu.VMEM)
IN_SMEM = pl.BlockSpec(memory_space=pltpu.SMEM)


def dot(a, b, dims):
    return lax.dot_general(a, b, dims, preferred_element_type=jnp.float32)


def flip(a):
    return a.astype(jnp.float32).T.astype(jnp.bfloat16)


def columns(ref, at):
    return ref[:, lanes_of(at)]


def lanes_of(at):
    return pl.ds(pl.multiple_of(at * HEAD_DIM, HEAD_DIM), HEAD_DIM)


def stacked_heads(ref, head, group):
    return jnp.concatenate([columns(ref, head * group + j) for j in range(group)], 0)


def masks_kernel(peers, blocks_dev, span, order_ref, notes_ref, slots_ref, key_hot_ref, query_mask_ref):
    f32, bf16 = jnp.float32, jnp.bfloat16
    rows = lax.broadcasted_iota(jnp.int32, (LANES, LANES), 0)
    lanes = lax.broadcasted_iota(jnp.int32, (LANES, LANES), 1)
    slot_rows = slots_ref.shape[0]

    def hot(slots):
        return (rows == slots // BLOCK).astype(f32).T.astype(bf16)

    for r in range(peers):
        shard = notes_ref[order_ref[r]]
        for i in range(slot_rows):
            key_hot_ref[r, i * LANES : (i + 1) * LANES, :] = hot(shard[i : i + 1, :])
    owners = lax.broadcasted_iota(jnp.int32, (LANES, peers), 0) // blocks_dev
    spread = (owners == lax.broadcasted_iota(jnp.int32, (LANES, peers), 1)).astype(f32)
    link_rows = jnp.concatenate([notes_ref[p][slot_rows : slot_rows + 1, :] for p in range(peers)], 0).astype(f32)
    of_block = dot(spread, link_rows, NN)
    table = jnp.zeros((LANES, LANES), f32)
    for s in range(span):
        picked = jnp.sum(jnp.where(lanes == (rows % blocks_dev) * span + s, of_block, 0.0), 1, keepdims=True)
        table = table + jnp.where(lanes == rows + s - span // 2, picked, 0.0)
    table = table.astype(bf16)
    for i in range(slot_rows):
        linked = dot(hot(slots_ref[i : i + 1, :]), table, NN)
        query_mask_ref[i * LANES : (i + 1) * LANES, :] = jnp.where(linked > 0.5, 0.0, MASKED).astype(bf16)


def keys_of(shards, head):
    return jnp.concatenate([columns(k, head) for k, _, _ in shards], 0)


def values_of(shards, head):
    return jnp.concatenate([columns(v, head) for _, v, _ in shards], 0)


def split(refs, count, hot_ref, at):
    shards = []
    for i in range(count):
        shards.append((refs[i].at[0], refs[i].at[1], hot_ref.at[at[i]]))
    return shards


def masked_scores(q_ref, mask, shards, hots, head, group, first):
    queries = jnp.concatenate([stacked_heads(q_ref, first + head, group), jnp.concatenate([mask] * group, 0)], 1)
    return dot(jnp.concatenate([keys_of(shards, head), hots], 1), queries, NT)


def absorb(scores, values, state):
    factor = HEAD_DIM ** (-0.5) * LOG2_E
    top = jnp.max(scores, 0, keepdims=True)
    if state is not None:
        top = jnp.maximum(top, state[0])
    weights = jnp.exp2((scores - top) * factor)
    total = jnp.sum(weights, 0, keepdims=True)
    mixed = dot(flip(values), weights.astype(jnp.bfloat16), NN)
    if state is not None:
        keep = jnp.exp2((state[0] - top) * factor)
        total = total + state[1] * keep
        mixed = mixed + state[2] * keep
    return top, total, mixed


def backprop(q_ref, g_ref, shards, scores, head, group, first, norm, delta):
    scale = HEAD_DIM ** (-0.5)
    queries, grads = stacked_heads(q_ref, first + head, group), stacked_heads(g_ref, first + head, group)
    weights = jnp.exp2(scores * (scale * LOG2_E) - norm)
    d_scores = (weights * (dot(values_of(shards, head), grads, NT) - delta)).astype(jnp.bfloat16)
    k_grad = dot(d_scores, queries, NN) * scale
    v_grad = dot(weights.astype(jnp.bfloat16), grads, NN)
    return k_grad, v_grad, dot(flip(keys_of(shards, head)), d_scores, NN)


def forward_kernel(at, heads, group, first, q_ref, mask_ref, hot_ref, *refs):
    shards = split(refs, len(at), hot_ref, at)
    state, outs = refs[len(at) : -3], refs[-3:]
    hots = jnp.concatenate([hot[...] for _, _, hot in shards], 0)
    @pl.loop(0, heads)
    def _(head):
        scores = masked_scores(q_ref, mask_ref[...], shards, hots, head, group, first)
        before = [s[head] for s in state] if state else None
        for out, value in zip(outs, absorb(scores, values_of(shards, head), before)):
            out[head] = value


def turn_kernel(at, heads, group, first, q_ref, g_ref, mask_ref, hot_ref, far_ref, top, total, mixed, norm_ref, delta_ref, q_out, grads_out):
    shards = split([far_ref], 1, hot_ref, (at,))
    @pl.loop(0, heads)
    def _(head):
        scores = masked_scores(q_ref, mask_ref[...], shards, hot_ref[at], head, group, first)
        state = absorb(scores, values_of(shards, head), (top[head], total[head], mixed[head]))
        norm = state[0] * (HEAD_DIM ** (-0.5) * LOG2_E) + jnp.log2(state[1])
        attended = (state[2] / state[1]).astype(jnp.bfloat16).astype(jnp.float32)
        grads = stacked_heads(g_ref, first + head, group).astype(jnp.float32).T
        delta = jnp.sum(grads * attended, 0, keepdims=True)
        norm_ref[head], delta_ref[head] = norm, delta
        k_grad, v_grad, q_out[head] = backprop(q_ref, g_ref, shards, scores, head, group, first, norm, delta)
        store_grads([grads_out], head, k_grad, v_grad)


def backward_kernel(at, heads, group, first, q_ref, g_ref, mask_ref, hot_ref, *refs):
    count = len(at)
    shards = split(refs, count, hot_ref, at)
    norm_ref, delta_ref, q_in, q_out = refs[count : count + 4]
    hots = jnp.concatenate([hot[...] for _, _, hot in shards], 0)
    @pl.loop(0, heads)
    def _(head):
        scores = masked_scores(q_ref, mask_ref[...], shards, hots, head, group, first)
        k_grad, v_grad, q_terms = backprop(q_ref, g_ref, shards, scores, head, group, first, norm_ref[head], delta_ref[head])
        store_grads(refs[count + 4 :], head, k_grad, v_grad)
        q_out[head] = q_in[head] + q_terms


def store_grads(outs, head, k_grad, v_grad):
    span = lanes_of(head)
    for i, out in enumerate(outs):
        rows = out.shape[1]
        out[0, :, span] = k_grad[i * rows : (i + 1) * rows].astype(out.dtype)
        out[1, :, span] = v_grad[i * rows : (i + 1) * rows].astype(out.dtype)


def last_kernel(chunks, heads, group, q_ref, g_ref, mask_ref, hot_ref, *refs):
    outs = refs[4 * chunks :]
    rows = q_ref.shape[0]
    for c in range(chunks):
        own_ref, norm_ref, delta_ref, q_in = refs[4 * c : 4 * c + 4]
        shards = split([own_ref], 1, hot_ref, (0,))
        first = c * heads
        @pl.loop(0, heads)
        def _(head):
            scores = masked_scores(q_ref, mask_ref[...], shards, hot_ref[0], head, group, first)
            k_grad, v_grad, q_terms = backprop(q_ref, g_ref, shards, scores, head, group, first, norm_ref[head], delta_ref[head])
            store_grads([outs[1 + c]], head, k_grad, v_grad)
            q_sums = (q_in[head] + q_terms) * HEAD_DIM ** (-0.5)
            for j in range(group):
                at = (first + head) * group + j
                outs[0][:, lanes_of(at)] = q_sums[:, j * rows : (j + 1) * rows].T.astype(jnp.bfloat16)


def gather_plan(queries, key_rows, value_rows, out_grad, owner_slot, block_links):
    rows = queries.shape[0]
    peers = lax.axis_size("seq")
    half = peers // 2
    kv_heads = key_rows.shape[1] // HEAD_DIM
    group = queries.shape[1] // key_rows.shape[1]
    chunks = 2
    heads = kv_heads // chunks
    width = heads * HEAD_DIM
    each = range(chunks)
    f32, bf16 = jnp.float32, jnp.bfloat16
    ring = list(range(0, peers, 2)) + list(range(peers - 1, 0, -2))
    onward = [(ring[i], ring[(i + 1) % peers]) for i in range(peers)]
    back = [(b, a) for a, b in onward]

    def send_on(value):
        return lax.ppermute(value, "seq", onward)

    def send_back(value):
        return lax.ppermute(value, "seq", back)

    def call(kernel, args, outs, products, aliases):
        return pl.pallas_call(
            kernel,
            in_specs=[IN_VMEM] * len(args),
            out_specs=[IN_VMEM] * len(outs),
            out_shape=outs,
            input_output_aliases=aliases,
            cost_estimate=pl.CostEstimate(
                flops=products * heads * group * rows * rows, bytes_accessed=4 * rows * width, transcendentals=0
            ),
            compiler_params=pltpu.CompilerParams(vmem_limit_bytes=16 * 1024 * 1024),
        )(*args)

    span = block_links.shape[1]
    slots = owner_slot.reshape(rows // LANES, LANES)
    links = jnp.pad(block_links.reshape(1, -1), ((0, 0), (0, LANES - block_links.size)))
    notes = jnp.concatenate([slots, links], 0)
    notes = jnp.pad(notes, ((0, -notes.shape[0] % 8), (0, 0)))[None]
    notes = lax.all_to_all(jnp.broadcast_to(notes, (peers,) + notes.shape[1:]), "seq", split_axis=0, concat_axis=0, tiled=True)
    me = lax.axis_index("seq")
    place = jnp.where(me % 2 == 0, me // 2, peers - (me + 1) // 2)
    place = (place - jnp.arange(peers, dtype=jnp.int32)) % peers
    order = jnp.where(place < half, 2 * place, 2 * peers - 1 - 2 * place)

    lines = jax.ShapeDtypeStruct((heads, 1, group * rows), f32)
    talls = jax.ShapeDtypeStruct((heads, HEAD_DIM, group * rows), f32)
    pairs = jax.ShapeDtypeStruct((2, rows, width), f32)

    def forward(c, shards, at, state):
        args = [queries, mask, hot, *shards, *state]
        kernel = functools.partial(forward_kernel, at, heads, group, c * heads)
        aliases = {len(args) - 3 + i: i for i in range(3)} if state else {}
        return call(kernel, args, [lines, lines, talls], 2 * len(at), aliases)

    def backward(c, shards, at, norm, delta, q_sums):
        args = [queries, out_grad, mask, hot, *shards, norm, delta, q_sums]
        kernel = functools.partial(backward_kernel, at, heads, group, c * heads)
        return call(kernel, args, [talls] + [pairs] * len(at), 5 * len(at), {len(args) - 1: 0})

    own = [jnp.stack([key_rows[:, c * width : (c + 1) * width], value_rows[:, c * width : (c + 1) * width]]) for c in each]
    behind, ahead = [[v] for v in own], [[v] for v in own]
    state = [() for _ in each]
    hot = mask = None

    def catch_up(c, r):
        shards, at = [behind[c][r], ahead[c][r]], (r, peers - r)
        if r == 1:
            shards, at = [own[c]] + shards, (0,) + at
        state[c] = tuple(forward(c, shards, at, state[c]))

    for r in range(1, half):
        for c in each:
            low, high = send_on(behind[c][-1]), send_back(ahead[c][-1])
            if r > 1:
                catch_up(c, r - 1)
                low, high, state[c] = lax.optimization_barrier((low, high, state[c]))
            elif c == 0:
                low, high, notes = lax.optimization_barrier((low, high, notes))
            behind[c].append(low)
            ahead[c].append(high)
        if r == 1:
            hot, mask = pl.pallas_call(
                functools.partial(masks_kernel, peers, rows // BLOCK, span),
                in_specs=[IN_SMEM, IN_VMEM, IN_VMEM],
                out_specs=[IN_VMEM] * 2,
                out_shape=[jax.ShapeDtypeStruct((peers, rows, LANES), bf16), jax.ShapeDtypeStruct((rows, LANES), bf16)],
                compiler_params=pltpu.CompilerParams(vmem_limit_bytes=16 * 1024 * 1024),
            )(order, notes, slots)
    far = [send_back(ahead[c][-1]) if c % 2 else send_on(behind[c][-1]) for c in each]
    norm, delta, q_sums, down, up = [[None] * chunks for _ in range(5)]
    for c in each:
        catch_up(c, half - 1)
        norm[c], delta[c], q_sums[c], sums = call(
            functools.partial(turn_kernel, half, heads, group, c * heads),
            [queries, out_grad, mask, hot, far[c], *state[c]],
            [lines, lines, talls, jax.ShapeDtypeStruct(pairs.shape, bf16)],
            7,
            {5: 0, 6: 1, 7: 2},
        )
        if c + 1 < chunks:
            sums, state[c + 1] = lax.optimization_barrier((sums, state[c + 1]))
        else:
            sums, norm[0] = lax.optimization_barrier((sums, norm[0]))
        if c % 2:
            up[c] = send_on(sums)
        else:
            down[c] = send_back(sums)
    for r in range(half - 1, 0, -1):
        for c in each:
            q_sums[c], low, high = backward(c, [behind[c][r], ahead[c][r]], (r, peers - r), norm[c], delta[c], q_sums[c])
            low = low if down[c] is None else low + down[c].astype(f32)
            high = high if up[c] is None else high + up[c].astype(f32)
            after = (c + 1) % chunks
            low, high, norm[after] = lax.optimization_barrier((low.astype(bf16), high.astype(bf16), norm[after]))
            down[c], up[c] = send_back(low), send_on(high)
    args = [queries, out_grad, mask, hot]
    for c in each:
        args += [own[c], norm[c], delta[c], q_sums[c]]
    query_grad, *mine = call(
        functools.partial(last_kernel, chunks, heads, group),
        args,
        [jax.ShapeDtypeStruct(queries.shape, bf16)] + [pairs] * chunks,
        5 * chunks,
        {},
    )
    total = [(mine[c] + down[c].astype(f32) + up[c].astype(f32)).astype(bf16) for c in each]
    return query_grad, jnp.concatenate([t[0] for t in total], 1), jnp.concatenate([t[1] for t in total], 1)


def local(queries, key_rows, value_rows, out_grad, owner_slot, block_links):
    rows = queries.shape[0]
    peers = lax.axis_size("seq")
    q_width, kv_width = queries.shape[1], key_rows.shape[1]
    slots = 4 * peers * max(1, rows // peers // 2)
    gathered = 2 * (peers - 1) * rows * 2 * kv_width
    relayed = slots * (3 * q_width + 4 * kv_width) + 4 * rows * 2 * kv_width
    fits = kv_width % (2 * HEAD_DIM) == 0 and peers > 2 and peers & (peers - 1) == 0 and rows % LANES == 0 and peers * rows // BLOCK <= LANES and block_links.size <= LANES
    plan = gather_plan if fits and gathered <= relayed else relay_plan
    return plan(queries, key_rows, value_rows, out_grad, owner_slot, block_links)


def solution(mesh):
    return jax.shard_map(
        local,
        mesh=mesh,
        in_specs=(
            P(("parts", "seq"), "head"),
            P(("parts", "seq"), "head"),
            P(("parts", "seq"), "head"),
            P(("parts", "seq"), "head"),
            P(("parts", "seq")),
            P(("parts", "seq"), None),
        ),
        out_specs=(
            P(("parts", "seq"), "head"),
            P(("parts", "seq"), "head"),
            P(("parts", "seq"), "head"),
        ),
        check_vma=False,
    )
```

```python
import functools

import jax
import jax.numpy as jnp
from jax import lax
from jax.experimental import pallas as pl
from jax.experimental.pallas import tpu as pltpu
from jax.sharding import PartitionSpec as P

HEAD_DIM = 128
BLOCK = 128


def padded(value, sides, width):
    for axis, dim in sides:
        peers, length = (lax.axis_size(axis), value.shape[dim])
        up = [(i, (i + 1) % peers) for i in range(peers - 1)]
        down = [(j, i) for i, j in up]
        last = lax.slice_in_dim(value, length - width, length, axis=dim)
        leading = lax.slice_in_dim(value, 0, width, axis=dim)
        before = lax.ppermute(last, axis, up)
        after = lax.ppermute(leading, axis, down)
        value = jnp.concatenate([before, value, after], axis=dim)
    return value


def from_behind(value, axis, by):
    peers = lax.axis_size(axis)
    pairs = [(i, i + by) for i in range(peers) if 0 <= i + by < peers]
    return lax.ppermute(value, axis, pairs)


def head_major(matrix, heads):
    return matrix.reshape(matrix.shape[0], heads, -1).transpose(1, 0, 2)


def relay_plan(queries, key_rows, value_rows, out_grad, owner_slot, block_links):
    row_count = queries.shape[0]
    seq_count = lax.axis_size("seq")
    capacity = 4 * max(1, row_count // seq_count // 2)
    slots = seq_count * capacity
    kv_width = key_rows.shape[1]
    kv_heads = kv_width // HEAD_DIM
    group_size = queries.shape[1] // kv_width
    score_scale = HEAD_DIM ** (-0.5)
    owner_dev = owner_slot // row_count
    owner_row = owner_slot % row_count
    member = (owner_dev[:, None] == jnp.arange(seq_count, dtype=jnp.int32)[None, :]).astype(
        jnp.int32
    )
    within = jnp.sum(jnp.cumsum(member, 0) * member, 1) - 1
    placed = owner_dev * capacity + within

    def pack_rows(matrix):
        return (
            jnp.zeros((slots, matrix.shape[1]), matrix.dtype)
            .at[placed]
            .set(matrix)
            .reshape(seq_count, capacity, matrix.shape[1])
        )

    vacant = jnp.array([row_count // 16, row_count % 16], jnp.float32)
    row_codes = jnp.stack([owner_row // 16, owner_row % 16], 1).astype(jnp.float32)
    code_buffer = (
        jnp.broadcast_to(vacant, (slots, 2))
        .at[placed]
        .set(row_codes)
        .astype(jnp.bfloat16)
        .reshape(seq_count, capacity, 2)
    )
    q_in, k_in, v_in, g_in, codes_in = (
        lax.all_to_all(pack_rows(queries), "seq", split_axis=0, concat_axis=0, tiled=True),
        lax.all_to_all(pack_rows(key_rows), "seq", split_axis=0, concat_axis=0, tiled=True),
        lax.all_to_all(pack_rows(value_rows), "seq", split_axis=0, concat_axis=0, tiled=True),
        lax.all_to_all(pack_rows(out_grad), "seq", split_axis=0, concat_axis=0, tiled=True),
        lax.all_to_all(code_buffer, "seq", split_axis=0, concat_axis=0, tiled=True),
    )
    arrived = codes_in.reshape(slots, 2).astype(jnp.float32)
    target = (arrived[:, 0] * 16.0 + arrived[:, 1]).astype(jnp.int32)

    def unpack_rows(buffer):
        flat_rows = buffer.reshape(slots, buffer.shape[2])
        return (
            jnp.zeros((row_count, flat_rows.shape[1]), flat_rows.dtype)
            .at[target]
            .set(flat_rows, mode="drop")
        )

    q_own = unpack_rows(q_in)
    k_own = unpack_rows(k_in)
    v_own = unpack_rows(v_in)
    g_own = unpack_rows(g_in)
    blocks = row_count // BLOCK
    span = block_links.shape[1]
    offset = (
        jnp.arange(3 * blocks, dtype=jnp.int32)[None, :]
        - jnp.arange(blocks, dtype=jnp.int32)[:, None]
    )
    selector = offset[:, :, None] == jnp.arange(span, dtype=jnp.int32)[None, None, :]
    allowed = jnp.sum(jnp.where(selector, block_links[:, None, :], 0), 2) > 0
    token_mask = jnp.repeat(jnp.repeat(allowed, BLOCK, 0), BLOCK, 1)
    kv_pair = jnp.concatenate([k_own, v_own], 1)
    kv_wide = padded(kv_pair, (("seq", 0),), row_count)

    def scores_of(q_group, k_group):
        raw_scores = (
            jnp.einsum("rgd,kd->grk", q_group, k_group, preferred_element_type=jnp.float32)
            * score_scale
        )
        return jnp.where(token_mask[None], raw_scores, -jnp.inf)

    def forward_head(operands):
        q_group, k_group, v_group = operands
        scores = scores_of(q_group, k_group)
        row_top = jnp.max(scores, -1, keepdims=True)
        log_total = row_top + jnp.log(jnp.sum(jnp.exp(scores - row_top), -1, keepdims=True))
        probs = jnp.exp(scores - log_total).astype(jnp.bfloat16)
        attended = jnp.einsum(
            "grk,kd->rgd", probs, v_group, preferred_element_type=jnp.float32
        ).astype(jnp.bfloat16)
        return (attended, log_total)

    def backward_head(operands):
        q_group, k_group, v_group, g_group, attended, log_total = operands
        weights = jnp.exp(scores_of(q_group, k_group) - log_total)
        row_delta = jnp.sum(g_group.astype(jnp.float32) * attended.astype(jnp.float32), -1).T[
            :, :, None
        ]
        d_probs = jnp.einsum("rgd,kd->grk", g_group, v_group, preferred_element_type=jnp.float32)
        d_scores = (weights * (d_probs - row_delta)).astype(jnp.bfloat16)
        q_grad = (
            jnp.einsum("grk,kd->rgd", d_scores, k_group, preferred_element_type=jnp.float32)
            * score_scale
        ).astype(jnp.bfloat16)
        k_grad = (
            jnp.einsum("grk,rgd->kd", d_scores, q_group, preferred_element_type=jnp.float32)
            * score_scale
        )
        v_grad = jnp.einsum(
            "grk,rgd->kd", weights.astype(jnp.bfloat16), g_group, preferred_element_type=jnp.float32
        )
        return (q_grad, k_grad, v_grad)

    query_heads = q_own.reshape(row_count, kv_heads, group_size, HEAD_DIM).transpose(1, 0, 2, 3)
    grad_heads = g_own.reshape(row_count, kv_heads, group_size, HEAD_DIM).transpose(1, 0, 2, 3)
    key_heads = head_major(kv_wide[:, :kv_width], kv_heads)
    value_heads = head_major(kv_wide[:, kv_width:], kv_heads)
    attended, log_total = lax.map(forward_head, (query_heads, key_heads, value_heads))
    q_grads, k_grads, v_grads = lax.map(
        backward_head, (query_heads, key_heads, value_heads, grad_heads, attended, log_total)
    )
    q_grad_own = q_grads.transpose(1, 0, 2, 3).reshape(row_count, kv_heads * group_size * HEAD_DIM)
    kv_grads = jnp.concatenate(
        [
            k_grads.transpose(1, 0, 2).reshape(3 * row_count, kv_width),
            v_grads.transpose(1, 0, 2).reshape(3 * row_count, kv_width),
        ],
        1,
    )
    from_above = from_behind(kv_grads[:row_count].astype(jnp.bfloat16), "seq", -1).astype(
        jnp.float32
    )
    from_below = from_behind(kv_grads[2 * row_count :].astype(jnp.bfloat16), "seq", 1).astype(
        jnp.float32
    )
    kv_total = (kv_grads[row_count : 2 * row_count] + from_above + from_below).astype(jnp.bfloat16)
    pick_rows = jnp.minimum(target, row_count - 1)

    def gather_back(matrix):
        return matrix[pick_rows].reshape(seq_count, capacity, matrix.shape[1])

    q_back, k_back, v_back = (
        lax.all_to_all(gather_back(q_grad_own), "seq", split_axis=0, concat_axis=0, tiled=True),
        lax.all_to_all(
            gather_back(kv_total[:, :kv_width]), "seq", split_axis=0, concat_axis=0, tiled=True
        ),
        lax.all_to_all(
            gather_back(kv_total[:, kv_width:]), "seq", split_axis=0, concat_axis=0, tiled=True
        ),
    )

    def settle_rows(buffer):
        return buffer.reshape(slots, buffer.shape[2])[placed]

    return (settle_rows(q_back), settle_rows(k_back), settle_rows(v_back))


LOG2_E = 1.4426950408889634
MASKED = -1e30
LANES = 128
NT = (((1,), (1,)), ((), ()))
NN = (((1,), (0,)), ((), ()))
IN_VMEM = pl.BlockSpec(memory_space=pltpu.VMEM)
IN_SMEM = pl.BlockSpec(memory_space=pltpu.SMEM)


def dot(a, b, dims):
    return lax.dot_general(a, b, dims, preferred_element_type=jnp.float32)


def flip(a):
    return a.astype(jnp.float32).T.astype(jnp.bfloat16)


def columns(ref, at):
    return ref[:, lanes_of(at)]


def lanes_of(at):
    return pl.ds(pl.multiple_of(at * HEAD_DIM, HEAD_DIM), HEAD_DIM)


def stacked_heads(ref, head, group):
    return jnp.concatenate([columns(ref, head * group + j) for j in range(group)], 0)


def masks_kernel(peers, blocks_dev, span, order_ref, notes_ref, slots_ref, key_hot_ref, query_mask_ref):
    f32, bf16 = jnp.float32, jnp.bfloat16
    rows = lax.broadcasted_iota(jnp.int32, (LANES, LANES), 0)
    lanes = lax.broadcasted_iota(jnp.int32, (LANES, LANES), 1)
    slot_rows = slots_ref.shape[0]

    def hot(slots):
        return (rows == slots // BLOCK).astype(f32).T.astype(bf16)

    for r in range(peers):
        shard = notes_ref[order_ref[r]]
        for i in range(slot_rows):
            key_hot_ref[r, i * LANES : (i + 1) * LANES, :] = hot(shard[i : i + 1, :])
    owners = lax.broadcasted_iota(jnp.int32, (LANES, peers), 0) // blocks_dev
    spread = (owners == lax.broadcasted_iota(jnp.int32, (LANES, peers), 1)).astype(f32)
    link_rows = jnp.concatenate([notes_ref[p][slot_rows : slot_rows + 1, :] for p in range(peers)], 0).astype(f32)
    of_block = dot(spread, link_rows, NN)
    table = jnp.zeros((LANES, LANES), f32)
    for s in range(span):
        picked = jnp.sum(jnp.where(lanes == (rows % blocks_dev) * span + s, of_block, 0.0), 1, keepdims=True)
        table = table + jnp.where(lanes == rows + s - span // 2, picked, 0.0)
    table = table.astype(bf16)
    for i in range(slot_rows):
        linked = dot(hot(slots_ref[i : i + 1, :]), table, NN)
        query_mask_ref[i * LANES : (i + 1) * LANES, :] = jnp.where(linked > 0.5, 0.0, MASKED).astype(bf16)


def keys_of(shards, head):
    return jnp.concatenate([columns(k, head) for k, _, _ in shards], 0)


def values_of(shards, head):
    return jnp.concatenate([columns(v, head) for _, v, _ in shards], 0)


def split(refs, count, hot_ref, at):
    shards = [(refs[2 * i], refs[2 * i + 1], hot_ref.at[at[i]]) for i in range(count)]
    if at[0] == 0:
        keys, values, hot = shards[0]
        shards[0] = (keys.at[0], values.at[1], hot)
    return shards


def masked_scores(q_ref, mask, shards, hots, head, group, first):
    queries = jnp.concatenate([stacked_heads(q_ref, first + head, group), jnp.concatenate([mask] * group, 0)], 1)
    return dot(jnp.concatenate([keys_of(shards, first + head), hots], 1), queries, NT)


def absorb(scores, values, state):
    factor = HEAD_DIM ** (-0.5) * LOG2_E
    top = jnp.max(scores, 0, keepdims=True)
    if state is not None:
        top = jnp.maximum(top, state[0])
    weights = jnp.exp2((scores - top) * factor)
    total = jnp.sum(weights, 0, keepdims=True)
    mixed = dot(flip(values), weights.astype(jnp.bfloat16), NN)
    if state is not None:
        keep = jnp.exp2((state[0] - top) * factor)
        total = total + state[1] * keep
        mixed = mixed + state[2] * keep
    return top, total, mixed


def backprop(q_ref, g_ref, shards, scores, head, group, first, norm, delta):
    scale = HEAD_DIM ** (-0.5)
    queries, grads = stacked_heads(q_ref, first + head, group), stacked_heads(g_ref, first + head, group)
    weights = jnp.exp2(scores * (scale * LOG2_E) - norm)
    d_scores = (weights * (dot(values_of(shards, first + head), grads, NT) - delta)).astype(jnp.bfloat16)
    k_grad = dot(d_scores, queries, NN) * scale
    v_grad = dot(weights.astype(jnp.bfloat16), grads, NN)
    return k_grad, v_grad, dot(flip(keys_of(shards, first + head)), d_scores, NN)


def forward_kernel(at, heads, group, first, q_ref, mask_ref, hot_ref, *refs):
    shards = split(refs, len(at), hot_ref, at)
    state, outs = refs[2 * len(at) : -3], refs[-3:]
    rows = q_ref.shape[0]
    factor = HEAD_DIM ** (-0.5) * LOG2_E

    @pl.loop(0, heads)
    def _(head):
        keys = [jnp.concatenate([columns(k, first + head), hot[...]], 1) for k, _, hot in shards]
        values = flip(values_of(shards, first + head))
        scores, tops = [], []
        for j in range(group):
            span = slice(j * rows, (j + 1) * rows)
            query = jnp.concatenate([columns(q_ref, (first + head) * group + j), mask_ref[...]], 1)
            scores.append([dot(key, query, NT) for key in keys])
            tops.append(functools.reduce(jnp.maximum, [jnp.max(s, 0, keepdims=True) for s in scores[j]]))
            if state:
                tops[j] = jnp.maximum(tops[j], state[0][head][:, span])
        for j in range(group):
            span = slice(j * rows, (j + 1) * rows)
            weights = [jnp.exp2((s - tops[j]) * factor) for s in scores[j]]
            total = sum(jnp.sum(w, 0, keepdims=True) for w in weights)
            mixed = dot(values, jnp.concatenate([w.astype(jnp.bfloat16) for w in weights], 0), NN)
            if state:
                keep = jnp.exp2((state[0][head][:, span] - tops[j]) * factor)
                total = total + state[1][head][:, span] * keep
                mixed = mixed + state[2][head][:, span] * keep
            outs[0][head, :, span], outs[1][head, :, span], outs[2][head, :, span] = tops[j], total, mixed


def turn_kernel(at, heads, group, first, q_ref, g_ref, mask_ref, hot_ref, k_ref, v_ref, top, total, mixed, norm_ref, delta_ref, q_out, grads_out):
    shards = split([k_ref, v_ref], 1, hot_ref, (at,))
    @pl.loop(0, heads)
    def _(head):
        scores = masked_scores(q_ref, mask_ref[...], shards, hot_ref[at], head, group, first)
        state = absorb(scores, values_of(shards, first + head), (top[head], total[head], mixed[head]))
        norm = state[0] * (HEAD_DIM ** (-0.5) * LOG2_E) + jnp.log2(state[1])
        attended = (state[2] / state[1]).astype(jnp.bfloat16).astype(jnp.float32)
        grads = stacked_heads(g_ref, first + head, group).astype(jnp.float32).T
        delta = jnp.sum(grads * attended, 0, keepdims=True)
        norm_ref[head], delta_ref[head] = norm, delta
        k_grad, v_grad, q_out[head] = backprop(q_ref, g_ref, shards, scores, head, group, first, norm, delta)
        store_grads([grads_out], head, k_grad, v_grad)


def backward_kernel(at, heads, group, first, q_ref, g_ref, mask_ref, hot_ref, *refs):
    count = len(at)
    shards = split(refs, count, hot_ref, at)
    norm_ref, delta_ref, q_in, q_out = refs[2 * count : 2 * count + 4]
    hots = jnp.concatenate([hot[...] for _, _, hot in shards], 0)
    @pl.loop(0, heads)
    def _(head):
        scores = masked_scores(q_ref, mask_ref[...], shards, hots, head, group, first)
        k_grad, v_grad, q_terms = backprop(q_ref, g_ref, shards, scores, head, group, first, norm_ref[head], delta_ref[head])
        store_grads(refs[2 * count + 4 :], head, k_grad, v_grad)
        q_out[head] = q_in[head] + q_terms


def store_grads(outs, head, k_grad, v_grad):
    span = lanes_of(head)
    for i, out in enumerate(outs):
        rows = out.shape[1]
        out[0, :, span] = k_grad[i * rows : (i + 1) * rows].astype(out.dtype)
        out[1, :, span] = v_grad[i * rows : (i + 1) * rows].astype(out.dtype)


def last_kernel(heads, group, first, q_ref, g_ref, mask_ref, hot_ref, k_ref, v_ref, norm_ref, delta_ref, *refs):
    *q_sums, q_out, grads_out = refs
    shards = split([k_ref, v_ref], 1, hot_ref, (0,))
    rows = q_ref.shape[0]

    def finish(at, sums):
        for j in range(group):
            q_out[:, lanes_of(at * group + j)] = (sums[:, j * rows : (j + 1) * rows] * HEAD_DIM ** (-0.5)).T.astype(jnp.bfloat16)

    @pl.loop(0, heads)
    def _(head):
        scores = masked_scores(q_ref, mask_ref[...], shards, hot_ref[0], head, group, first)
        k_grad, v_grad, q_terms = backprop(q_ref, g_ref, shards, scores, head, group, first, norm_ref[head], delta_ref[head])
        store_grads([grads_out], head, k_grad, v_grad)
        finish(first + head, q_sums[-1][head] + q_terms)
        for c, done in enumerate(q_sums[:-1]):
            finish(c * heads + head, done[head])


def gather_plan(queries, key_rows, value_rows, out_grad, owner_slot, block_links):
    rows = queries.shape[0]
    peers = lax.axis_size("seq")
    half = peers // 2
    kv_heads = key_rows.shape[1] // HEAD_DIM
    group = queries.shape[1] // key_rows.shape[1]
    chunks = 2
    heads = kv_heads // chunks
    width = heads * HEAD_DIM
    each = range(chunks)
    f32, bf16 = jnp.float32, jnp.bfloat16
    ring = list(range(0, peers, 2)) + list(range(peers - 1, 0, -2))
    onward = [(ring[i], ring[(i + 1) % peers]) for i in range(peers)]
    back = [(b, a) for a, b in onward]

    def send_on(value):
        return lax.ppermute(value, "seq", onward)

    def send_back(value):
        return lax.ppermute(value, "seq", back)

    def call(kernel, args, outs, products, aliases):
        return pl.pallas_call(
            kernel,
            in_specs=[IN_VMEM] * len(args),
            out_specs=[IN_VMEM] * len(outs),
            out_shape=outs,
            input_output_aliases=aliases,
            cost_estimate=pl.CostEstimate(
                flops=products, bytes_accessed=rows, transcendentals=0
            ),
            compiler_params=pltpu.CompilerParams(vmem_limit_bytes=16 * 1024 * 1024),
        )(*args)

    span = block_links.shape[1]
    slots = owner_slot.reshape(rows // LANES, LANES)
    links = jnp.pad(block_links.reshape(1, -1), ((0, 0), (0, LANES - block_links.size)))
    notes = jnp.concatenate([slots, links], 0)
    notes = jnp.pad(notes, ((0, -notes.shape[0] % 8), (0, 0)))[None]
    notes = lax.all_to_all(jnp.broadcast_to(notes, (peers,) + notes.shape[1:]), "seq", split_axis=0, concat_axis=0, tiled=True)
    me = lax.axis_index("seq")
    place = jnp.where(me % 2 == 0, me // 2, peers - (me + 1) // 2)
    place = (place - jnp.arange(peers, dtype=jnp.int32)) % peers
    order = jnp.where(place < half, 2 * place, 2 * peers - 1 - 2 * place)

    lines = jax.ShapeDtypeStruct((heads, 1, group * rows), f32)
    talls = jax.ShapeDtypeStruct((heads, HEAD_DIM, group * rows), f32)
    pairs = jax.ShapeDtypeStruct((2, rows, width), f32)

    def forward(c, shards, at, state):
        args = [queries, mask, hot, *shards, *state]
        kernel = functools.partial(forward_kernel, at, heads, group, c * heads)
        aliases = {len(args) - 3 + i: i for i in range(3)} if state else {}
        return call(kernel, args, [lines, lines, talls], 2 * len(at), aliases)

    def backward(c, shards, at, norm, delta, q_sums):
        args = [queries, out_grad, mask, hot, *shards, norm, delta, q_sums]
        kernel = functools.partial(backward_kernel, at, heads, group, c * heads)
        return call(kernel, args, [talls] + [pairs] * len(at), 5 * len(at), {len(args) - 1: 0})

    own = (key_rows, value_rows)
    behind, ahead = [[v] for v in own], [[v] for v in own]
    state = [() for _ in each]
    hot = mask = None

    def pair_at(r):
        return [side[i][r] for side in (behind, ahead) for i in range(2)]

    def catch_up(c, r):
        shards, at = pair_at(r), (r, peers - r)
        if r == 1:
            shards, at = [own, own, *shards], (0,) + at
        state[c] = tuple(forward(c, shards, at, state[c]))

    for r in range(1, half):
        for c in each:
            low, high = send_on(behind[c][-1]), send_back(ahead[c][-1])
            if (r, c) == (1, 0):
                low, high, own = lax.optimization_barrier((low, high, own))
                own = jnp.stack(own)
            elif (r, c) == (1, 1):
                low, high, notes = lax.optimization_barrier((low, high, notes))
            elif (r, c) == (2, 0):
                low, high = lax.optimization_barrier((low, high))
            elif (r, c) == (2, 1):
                catch_up(0, 1)
                low, high, state[0] = lax.optimization_barrier((low, high, state[0]))
                catch_up(1, 1)
            else:
                if c:
                    catch_up(0, r - 1)
                low, high, state[:] = lax.optimization_barrier((low, high, state))
                if c:
                    catch_up(1, r - 1)
            behind[c].append(low)
            ahead[c].append(high)
        if r == 1:
            hot, mask = pl.pallas_call(
                functools.partial(masks_kernel, peers, rows // BLOCK, span),
                in_specs=[IN_SMEM, IN_VMEM, IN_VMEM],
                out_specs=[IN_VMEM] * 2,
                out_shape=[jax.ShapeDtypeStruct((peers, rows, LANES), bf16), jax.ShapeDtypeStruct((rows, LANES), bf16)],
                compiler_params=pltpu.CompilerParams(vmem_limit_bytes=16 * 1024 * 1024),
            )(order, notes, slots)
    far = (send_on(behind[0][-1]), send_back(ahead[1][-1]))
    norm, delta, q_sums, down, up = [[None] * chunks for _ in range(5)]
    for c in each:
        catch_up(c, half - 1)
        norm[c], delta[c], q_sums[c], sums = call(
            functools.partial(turn_kernel, half, heads, group, c * heads),
            [queries, out_grad, mask, hot, *far, *state[c]],
            [lines, lines, talls, jax.ShapeDtypeStruct(pairs.shape, bf16)],
            7,
            {6: 0, 7: 1, 8: 2},
        )
        if c + 1 < chunks:
            sums, state[c + 1] = lax.optimization_barrier((sums, state[c + 1]))
        else:
            sums, norm[0] = lax.optimization_barrier((sums, norm[0]))
        if c % 2:
            up[c] = send_on(sums)
        else:
            down[c] = send_back(sums)
    for r in range(half - 1, 0, -1):
        for c in each:
            q_sums[c], low, high = backward(c, pair_at(r), (r, peers - r), norm[c], delta[c], q_sums[c])
            low = low if down[c] is None else low + down[c].astype(f32)
            high = high if up[c] is None else high + up[c].astype(f32)
            after = (c + 1) % chunks
            low, high, norm[after] = lax.optimization_barrier((low.astype(bf16), high.astype(bf16), norm[after]))
            down[c], up[c] = send_back(low), send_on(high)
    total = []
    for c in each:
        if c + 1 < chunks:
            q_sums[c], mine = backward(c, [own, own], (0,), norm[c], delta[c], q_sums[c])
        else:
            query_grad, mine = call(
                functools.partial(last_kernel, heads, group, c * heads),
                [queries, out_grad, mask, hot, own, own, norm[c], delta[c], *q_sums],
                [jax.ShapeDtypeStruct(queries.shape, bf16), pairs],
                5,
                {},
            )
        total.append((mine + down[c].astype(f32) + up[c].astype(f32)).astype(bf16))
        if c + 1 < chunks:
            total[c], norm[c + 1] = lax.optimization_barrier((total[c], norm[c + 1]))
    total = jnp.concatenate(total, 2)
    return query_grad, total[0], total[1]


def local(queries, key_rows, value_rows, out_grad, owner_slot, block_links):
    rows = queries.shape[0]
    peers = lax.axis_size("seq")
    q_width, kv_width = queries.shape[1], key_rows.shape[1]
    slots = 4 * peers * max(1, rows // peers // 2)
    gathered = 2 * (peers - 1) * rows * 2 * kv_width
    relayed = slots * (3 * q_width + 4 * kv_width) + 4 * rows * 2 * kv_width
    fits = kv_width % (2 * HEAD_DIM) == 0 and peers > 2 and peers & (peers - 1) == 0 and rows % LANES == 0 and peers * rows // BLOCK <= LANES and block_links.size <= LANES
    plan = gather_plan if fits and gathered <= relayed else relay_plan
    return plan(queries, key_rows, value_rows, out_grad, owner_slot, block_links)


def solution(mesh):
    return jax.shard_map(
        local,
        mesh=mesh,
        in_specs=(
            P(("parts", "seq"), "head"),
            P(("parts", "seq"), "head"),
            P(("parts", "seq"), "head"),
            P(("parts", "seq"), "head"),
            P(("parts", "seq")),
            P(("parts", "seq"), None),
        ),
        out_specs=(
            P(("parts", "seq"), "head"),
            P(("parts", "seq"), "head"),
            P(("parts", "seq"), "head"),
        ),
        check_vma=False,
    )
```

```python
import functools

import jax
import jax.numpy as jnp
from jax import lax
from jax.experimental import pallas as pl
from jax.experimental.pallas import tpu as pltpu
from jax.sharding import PartitionSpec as P

HEAD_DIM = 128
BLOCK = 128


def padded(value, sides, width):
    for axis, dim in sides:
        peers, length = (lax.axis_size(axis), value.shape[dim])
        up = [(i, (i + 1) % peers) for i in range(peers - 1)]
        down = [(j, i) for i, j in up]
        last = lax.slice_in_dim(value, length - width, length, axis=dim)
        leading = lax.slice_in_dim(value, 0, width, axis=dim)
        before = lax.ppermute(last, axis, up)
        after = lax.ppermute(leading, axis, down)
        value = jnp.concatenate([before, value, after], axis=dim)
    return value


def from_behind(value, axis, by):
    peers = lax.axis_size(axis)
    pairs = [(i, i + by) for i in range(peers) if 0 <= i + by < peers]
    return lax.ppermute(value, axis, pairs)


def head_major(matrix, heads):
    return matrix.reshape(matrix.shape[0], heads, -1).transpose(1, 0, 2)


def relay_plan(queries, key_rows, value_rows, out_grad, owner_slot, block_links):
    row_count = queries.shape[0]
    seq_count = lax.axis_size("seq")
    capacity = 4 * max(1, row_count // seq_count // 2)
    slots = seq_count * capacity
    kv_width = key_rows.shape[1]
    kv_heads = kv_width // HEAD_DIM
    group_size = queries.shape[1] // kv_width
    score_scale = HEAD_DIM ** (-0.5)
    owner_dev = owner_slot // row_count
    owner_row = owner_slot % row_count
    member = (owner_dev[:, None] == jnp.arange(seq_count, dtype=jnp.int32)[None, :]).astype(
        jnp.int32
    )
    within = jnp.sum(jnp.cumsum(member, 0) * member, 1) - 1
    placed = owner_dev * capacity + within

    def pack_rows(matrix):
        return (
            jnp.zeros((slots, matrix.shape[1]), matrix.dtype)
            .at[placed]
            .set(matrix)
            .reshape(seq_count, capacity, matrix.shape[1])
        )

    vacant = jnp.array([row_count // 16, row_count % 16], jnp.float32)
    row_codes = jnp.stack([owner_row // 16, owner_row % 16], 1).astype(jnp.float32)
    code_buffer = (
        jnp.broadcast_to(vacant, (slots, 2))
        .at[placed]
        .set(row_codes)
        .astype(jnp.bfloat16)
        .reshape(seq_count, capacity, 2)
    )
    q_in, k_in, v_in, g_in, codes_in = (
        lax.all_to_all(pack_rows(queries), "seq", split_axis=0, concat_axis=0, tiled=True),
        lax.all_to_all(pack_rows(key_rows), "seq", split_axis=0, concat_axis=0, tiled=True),
        lax.all_to_all(pack_rows(value_rows), "seq", split_axis=0, concat_axis=0, tiled=True),
        lax.all_to_all(pack_rows(out_grad), "seq", split_axis=0, concat_axis=0, tiled=True),
        lax.all_to_all(code_buffer, "seq", split_axis=0, concat_axis=0, tiled=True),
    )
    arrived = codes_in.reshape(slots, 2).astype(jnp.float32)
    target = (arrived[:, 0] * 16.0 + arrived[:, 1]).astype(jnp.int32)

    def unpack_rows(buffer):
        flat_rows = buffer.reshape(slots, buffer.shape[2])
        return (
            jnp.zeros((row_count, flat_rows.shape[1]), flat_rows.dtype)
            .at[target]
            .set(flat_rows, mode="drop")
        )

    q_own = unpack_rows(q_in)
    k_own = unpack_rows(k_in)
    v_own = unpack_rows(v_in)
    g_own = unpack_rows(g_in)
    blocks = row_count // BLOCK
    span = block_links.shape[1]
    offset = (
        jnp.arange(3 * blocks, dtype=jnp.int32)[None, :]
        - jnp.arange(blocks, dtype=jnp.int32)[:, None]
    )
    selector = offset[:, :, None] == jnp.arange(span, dtype=jnp.int32)[None, None, :]
    allowed = jnp.sum(jnp.where(selector, block_links[:, None, :], 0), 2) > 0
    token_mask = jnp.repeat(jnp.repeat(allowed, BLOCK, 0), BLOCK, 1)
    kv_pair = jnp.concatenate([k_own, v_own], 1)
    kv_wide = padded(kv_pair, (("seq", 0),), row_count)

    def scores_of(q_group, k_group):
        raw_scores = (
            jnp.einsum("rgd,kd->grk", q_group, k_group, preferred_element_type=jnp.float32)
            * score_scale
        )
        return jnp.where(token_mask[None], raw_scores, -jnp.inf)

    def forward_head(operands):
        q_group, k_group, v_group = operands
        scores = scores_of(q_group, k_group)
        row_top = jnp.max(scores, -1, keepdims=True)
        log_total = row_top + jnp.log(jnp.sum(jnp.exp(scores - row_top), -1, keepdims=True))
        probs = jnp.exp(scores - log_total).astype(jnp.bfloat16)
        attended = jnp.einsum(
            "grk,kd->rgd", probs, v_group, preferred_element_type=jnp.float32
        ).astype(jnp.bfloat16)
        return (attended, log_total)

    def backward_head(operands):
        q_group, k_group, v_group, g_group, attended, log_total = operands
        weights = jnp.exp(scores_of(q_group, k_group) - log_total)
        row_delta = jnp.sum(g_group.astype(jnp.float32) * attended.astype(jnp.float32), -1).T[
            :, :, None
        ]
        d_probs = jnp.einsum("rgd,kd->grk", g_group, v_group, preferred_element_type=jnp.float32)
        d_scores = (weights * (d_probs - row_delta)).astype(jnp.bfloat16)
        q_grad = (
            jnp.einsum("grk,kd->rgd", d_scores, k_group, preferred_element_type=jnp.float32)
            * score_scale
        ).astype(jnp.bfloat16)
        k_grad = (
            jnp.einsum("grk,rgd->kd", d_scores, q_group, preferred_element_type=jnp.float32)
            * score_scale
        )
        v_grad = jnp.einsum(
            "grk,rgd->kd", weights.astype(jnp.bfloat16), g_group, preferred_element_type=jnp.float32
        )
        return (q_grad, k_grad, v_grad)

    query_heads = q_own.reshape(row_count, kv_heads, group_size, HEAD_DIM).transpose(1, 0, 2, 3)
    grad_heads = g_own.reshape(row_count, kv_heads, group_size, HEAD_DIM).transpose(1, 0, 2, 3)
    key_heads = head_major(kv_wide[:, :kv_width], kv_heads)
    value_heads = head_major(kv_wide[:, kv_width:], kv_heads)
    attended, log_total = lax.map(forward_head, (query_heads, key_heads, value_heads))
    q_grads, k_grads, v_grads = lax.map(
        backward_head, (query_heads, key_heads, value_heads, grad_heads, attended, log_total)
    )
    q_grad_own = q_grads.transpose(1, 0, 2, 3).reshape(row_count, kv_heads * group_size * HEAD_DIM)
    kv_grads = jnp.concatenate(
        [
            k_grads.transpose(1, 0, 2).reshape(3 * row_count, kv_width),
            v_grads.transpose(1, 0, 2).reshape(3 * row_count, kv_width),
        ],
        1,
    )
    from_above = from_behind(kv_grads[:row_count].astype(jnp.bfloat16), "seq", -1).astype(
        jnp.float32
    )
    from_below = from_behind(kv_grads[2 * row_count :].astype(jnp.bfloat16), "seq", 1).astype(
        jnp.float32
    )
    kv_total = (kv_grads[row_count : 2 * row_count] + from_above + from_below).astype(jnp.bfloat16)
    pick_rows = jnp.minimum(target, row_count - 1)

    def gather_back(matrix):
        return matrix[pick_rows].reshape(seq_count, capacity, matrix.shape[1])

    q_back, k_back, v_back = (
        lax.all_to_all(gather_back(q_grad_own), "seq", split_axis=0, concat_axis=0, tiled=True),
        lax.all_to_all(
            gather_back(kv_total[:, :kv_width]), "seq", split_axis=0, concat_axis=0, tiled=True
        ),
        lax.all_to_all(
            gather_back(kv_total[:, kv_width:]), "seq", split_axis=0, concat_axis=0, tiled=True
        ),
    )

    def settle_rows(buffer):
        return buffer.reshape(slots, buffer.shape[2])[placed]

    return (settle_rows(q_back), settle_rows(k_back), settle_rows(v_back))


LOG2_E = 1.4426950408889634
MASKED = -1e30
LANES = 128
SAVED_FROM = 3
NT = (((1,), (1,)), ((), ()))
NN = (((1,), (0,)), ((), ()))
IN_VMEM = pl.BlockSpec(memory_space=pltpu.VMEM)
IN_SMEM = pl.BlockSpec(memory_space=pltpu.SMEM)


def dot(a, b, dims):
    return lax.dot_general(a, b, dims, preferred_element_type=jnp.float32)


def flip(a):
    return a.astype(jnp.float32).T.astype(jnp.bfloat16)


def columns(ref, at):
    return ref[:, lanes_of(at)]


def lanes_of(at):
    return pl.ds(pl.multiple_of(at * HEAD_DIM, HEAD_DIM), HEAD_DIM)


def stacked_heads(ref, head, group):
    return jnp.concatenate([columns(ref, head * group + j) for j in range(group)], 0)


def masks_kernel(peers, blocks_dev, span, slot_rows, notes_ref, key_hot_ref, query_mask_ref):
    f32, bf16 = jnp.float32, jnp.bfloat16
    rows = lax.broadcasted_iota(jnp.int32, (LANES, LANES), 0)
    lanes = lax.broadcasted_iota(jnp.int32, (LANES, LANES), 1)

    def hot(slots):
        return (rows == slots // BLOCK).astype(f32).T.astype(bf16)

    me = lax.axis_index("seq")
    place = jnp.where(me % 2 == 0, me // 2, peers - (me + 1) // 2)
    for r in range(peers):
        behind = (place + peers - r) % peers
        shard = notes_ref[jnp.where(behind < peers // 2, 2 * behind, 2 * peers - 1 - 2 * behind)]
        for i in range(slot_rows):
            key_hot_ref[r, i * LANES : (i + 1) * LANES, :] = hot(shard[i : i + 1, :])
    owners = lax.broadcasted_iota(jnp.int32, (LANES, peers), 0) // blocks_dev
    spread = (owners == lax.broadcasted_iota(jnp.int32, (LANES, peers), 1)).astype(f32)
    link_rows = jnp.concatenate([notes_ref[p][slot_rows : slot_rows + 1, :] for p in range(peers)], 0).astype(f32)
    of_block = dot(spread, link_rows, NN)
    table = jnp.zeros((LANES, LANES), f32)
    for s in range(span):
        picked = jnp.sum(jnp.where(lanes == (rows % blocks_dev) * span + s, of_block, 0.0), 1, keepdims=True)
        table = table + jnp.where(lanes == rows + s - span // 2, picked, 0.0)
    table = table.astype(bf16)
    linked = dot(key_hot_ref[0], table, NN)
    query_mask_ref[...] = jnp.where(linked > 0.5, 0.0, MASKED).astype(bf16)


def keys_of(shards, head):
    return jnp.concatenate([columns(k, head) for k, _, _ in shards], 0)


def values_of(shards, head):
    return jnp.concatenate([columns(v, head) for _, v, _ in shards], 0)


def split(refs, count, hot_ref, at):
    shards = [(refs[2 * i], refs[2 * i + 1], hot_ref.at[at[i]]) for i in range(count)]
    if at[0] == 0:
        keys, values, hot = shards[0]
        shards[0] = (keys.at[0], values.at[1], hot)
    return shards


def masked_scores(q_ref, mask, shards, hots, head, group, first):
    queries = jnp.concatenate([stacked_heads(q_ref, first + head, group), jnp.concatenate([mask] * group, 0)], 1)
    return dot(jnp.concatenate([keys_of(shards, first + head), hots], 1), queries, NT)


def absorb(scores, values, state):
    factor = HEAD_DIM ** (-0.5) * LOG2_E
    top = jnp.max(scores, 0, keepdims=True)
    if state is not None:
        top = jnp.maximum(top, state[0])
    weights = jnp.exp2((scores - top) * factor)
    total = jnp.sum(weights, 0, keepdims=True)
    mixed = dot(flip(values), weights.astype(jnp.bfloat16), NN)
    if state is not None:
        keep = jnp.exp2((state[0] - top) * factor)
        total = total + state[1] * keep
        mixed = mixed + state[2] * keep
    return top, total, mixed


def backprop(q_ref, g_ref, shards, scores, head, group, first, norm, delta):
    scale = HEAD_DIM ** (-0.5)
    queries, grads = stacked_heads(q_ref, first + head, group), stacked_heads(g_ref, first + head, group)
    weights = jnp.exp2(scores * (scale * LOG2_E) - norm)
    d_scores = (weights * (dot(values_of(shards, first + head), grads, NT) - delta)).astype(jnp.bfloat16)
    k_grad = dot(d_scores, queries, NN) * scale
    v_grad = dot(weights.astype(jnp.bfloat16), grads, NN)
    return k_grad, v_grad, dot(flip(keys_of(shards, first + head)), d_scores, NN)


def forward_kernel(at, heads, group, first, saved, q_ref, mask_ref, hot_ref, *refs):
    shards = split(refs, len(at), hot_ref, at)
    state, outs = refs[2 * len(at) : -3 - saved], refs[len(refs) - 3 - saved :]
    rows = q_ref.shape[0]
    factor = HEAD_DIM ** (-0.5) * LOG2_E

    @pl.loop(0, heads)
    def _(head):
        keys = [jnp.concatenate([columns(k, first + head), hot[...]], 1) for k, _, hot in shards]
        values = flip(values_of(shards, first + head))
        scores, tops = [], []
        for j in range(group):
            span = slice(j * rows, (j + 1) * rows)
            query = jnp.concatenate([columns(q_ref, (first + head) * group + j), mask_ref[...]], 1)
            scores.append([dot(key, query, NT) for key in keys])
            if saved:
                for i, part in enumerate(scores[j]):
                    outs[3][head, i * rows : (i + 1) * rows, span] = part
            tops.append(functools.reduce(jnp.maximum, [jnp.max(s, 0, keepdims=True) for s in scores[j]]))
            if state:
                tops[j] = jnp.maximum(tops[j], state[0][head][:, span])
        for j in range(group):
            span = slice(j * rows, (j + 1) * rows)
            weights = [jnp.exp2((s - tops[j]) * factor) for s in scores[j]]
            total = sum(jnp.sum(w, 0, keepdims=True) for w in weights)
            mixed = dot(values, jnp.concatenate([w.astype(jnp.bfloat16) for w in weights], 0), NN)
            if state:
                keep = jnp.exp2((state[0][head][:, span] - tops[j]) * factor)
                total = total + state[1][head][:, span] * keep
                mixed = mixed + state[2][head][:, span] * keep
            outs[0][head, :, span], outs[1][head, :, span], outs[2][head, :, span] = tops[j], total, mixed


def turn_kernel(at, heads, group, first, q_ref, g_ref, mask_ref, hot_ref, k_ref, v_ref, top, total, mixed, norm_ref, delta_ref, q_out, grads_out):
    shards = split([k_ref, v_ref], 1, hot_ref, (at,))
    @pl.loop(0, heads)
    def _(head):
        scores = masked_scores(q_ref, mask_ref[...], shards, hot_ref[at], head, group, first)
        state = absorb(scores, values_of(shards, first + head), (top[head], total[head], mixed[head]))
        norm = state[0] * (HEAD_DIM ** (-0.5) * LOG2_E) + jnp.log2(state[1])
        attended = (state[2] / state[1]).astype(jnp.bfloat16).astype(jnp.float32)
        grads = stacked_heads(g_ref, first + head, group).astype(jnp.float32).T
        delta = jnp.sum(grads * attended, 0, keepdims=True)
        norm_ref[head], delta_ref[head] = norm, delta
        k_grad, v_grad, q_out[head] = backprop(q_ref, g_ref, shards, scores, head, group, first, norm, delta)
        store_grads([grads_out], head, k_grad, v_grad)


def backward_kernel(at, heads, group, first, saved, q_ref, g_ref, mask_ref, hot_ref, *refs):
    count = len(at)
    if saved:
        scores_ref, *refs = refs
    shards = split(refs, count, hot_ref, at)
    norm_ref, delta_ref, q_in, q_out = refs[2 * count : 2 * count + 4]
    hots = jnp.concatenate([hot[...] for _, _, hot in shards], 0)
    @pl.loop(0, heads)
    def _(head):
        scores = scores_ref[head] if saved else masked_scores(q_ref, mask_ref[...], shards, hots, head, group, first)
        k_grad, v_grad, q_terms = backprop(q_ref, g_ref, shards, scores, head, group, first, norm_ref[head], delta_ref[head])
        store_grads(refs[2 * count + 4 :], head, k_grad, v_grad)
        q_out[head] = q_in[head] + q_terms


def store_grads(outs, head, k_grad, v_grad):
    span = lanes_of(head)
    for i, out in enumerate(outs):
        rows = out.shape[1]
        out[0, :, span] = k_grad[i * rows : (i + 1) * rows].astype(out.dtype)
        out[1, :, span] = v_grad[i * rows : (i + 1) * rows].astype(out.dtype)


def finish_kernel(heads, group, *refs):
    *q_sums, q_out = refs
    rows = q_out.shape[0]

    @pl.loop(0, heads)
    def _(head):
        for c, sums in enumerate(q_sums):
            for j in range(group):
                part = sums[head, :, j * rows : (j + 1) * rows] * HEAD_DIM ** (-0.5)
                q_out[:, lanes_of((c * heads + head) * group + j)] = part.T.astype(jnp.bfloat16)


def gather_plan(queries, key_rows, value_rows, out_grad, owner_slot, block_links):
    rows = queries.shape[0]
    peers = lax.axis_size("seq")
    half = peers // 2
    kv_heads = key_rows.shape[1] // HEAD_DIM
    group = queries.shape[1] // key_rows.shape[1]
    chunks = 2
    heads = kv_heads // chunks
    width = heads * HEAD_DIM
    each = range(chunks)
    f32, bf16 = jnp.float32, jnp.bfloat16
    ring = list(range(0, peers, 2)) + list(range(peers - 1, 0, -2))
    onward = [(ring[i], ring[(i + 1) % peers]) for i in range(peers)]
    back = [(b, a) for a, b in onward]

    def send_on(value):
        return lax.ppermute(value, "seq", onward)

    def send_back(value):
        return lax.ppermute(value, "seq", back)

    def call(kernel, args, outs, products, aliases):
        return pl.pallas_call(
            kernel,
            in_specs=[IN_VMEM] * len(args),
            out_specs=[IN_VMEM] * len(outs),
            out_shape=outs,
            input_output_aliases=aliases,
            cost_estimate=pl.CostEstimate(
                flops=products, bytes_accessed=rows, transcendentals=0
            ),
            compiler_params=pltpu.CompilerParams(vmem_limit_bytes=12 * 1024 * 1024),
        )(*args)

    span = block_links.shape[1]
    slots = owner_slot.reshape(rows // LANES, LANES)
    links = jnp.pad(block_links.reshape(1, -1), ((0, 0), (0, LANES - block_links.size)))
    notes = jnp.concatenate([slots, links], 0)
    notes = jnp.pad(notes, ((0, -notes.shape[0] % 8), (0, 0)))[None]
    notes = lax.all_to_all(jnp.broadcast_to(notes, (peers,) + notes.shape[1:]), "seq", split_axis=0, concat_axis=0, tiled=True)
    lines = jax.ShapeDtypeStruct((heads, 1, group * rows), f32)
    talls = jax.ShapeDtypeStruct((heads, HEAD_DIM, group * rows), f32)
    pairs = jax.ShapeDtypeStruct((2, rows, width), f32)

    def forward(c, shards, at, state, saved):
        args = [queries, mask, hot, *shards, *state]
        kernel = functools.partial(forward_kernel, at, heads, group, c * heads, saved)
        aliases = {len(args) - 3 + i: i for i in range(3)} if state else {}
        kept = [jax.ShapeDtypeStruct((heads, len(at) * rows, group * rows), f32)] * saved
        return call(kernel, args, [lines, lines, talls] + kept, 2 * len(at), aliases)

    def backward(c, shards, at, norm, delta, q_sums, scores=None):
        saved = scores is not None
        args = [queries, out_grad, mask, hot, *([scores] * saved), *shards, norm, delta, q_sums]
        kernel = functools.partial(backward_kernel, at, heads, group, c * heads, saved)
        return call(kernel, args, [talls] + [pairs] * len(at), 5 * len(at), {len(args) - 1: 0})

    own = (key_rows, value_rows)
    behind, ahead = [[v] for v in own], [[v] for v in own]
    state = [() for _ in each]
    hot = mask = None
    scores = {}

    def pair_at(r):
        return [side[i][r] for side in (behind, ahead) for i in range(2)]

    def catch_up(c, r):
        shards, at = pair_at(r), (r, peers - r)
        if r == 1:
            shards, at = [own, own, *shards], (0,) + at
        *state[c], = forward(c, shards, at, state[c], r >= SAVED_FROM)
        if r >= SAVED_FROM:
            scores[c, r] = state[c].pop()

    for r in range(1, half):
        for c in each:
            low, high = send_on(behind[c][-1]), send_back(ahead[c][-1])
            if (r, c) == (1, 0):
                low, high, own = lax.optimization_barrier((low, high, own))
                own = jnp.stack(own)
            elif (r, c) == (1, 1):
                low, high, notes = lax.optimization_barrier((low, high, notes))
            elif (r, c) == (2, 0):
                low, high, own = lax.optimization_barrier((low, high, own))
            elif (r, c) == (2, 1):
                catch_up(0, 1)
                low, high, state[0] = lax.optimization_barrier((low, high, state[0]))
                catch_up(1, 1)
            else:
                if c:
                    catch_up(0, r - 1)
                low, high, state[:] = lax.optimization_barrier((low, high, state))
                if c:
                    catch_up(1, r - 1)
            behind[c].append(low)
            ahead[c].append(high)
        if r == 1:
            hot, mask = pl.pallas_call(
                functools.partial(masks_kernel, peers, rows // BLOCK, span, rows // LANES),
                in_specs=[IN_VMEM],
                out_specs=[IN_VMEM] * 2,
                out_shape=[jax.ShapeDtypeStruct((peers, rows, LANES), bf16), jax.ShapeDtypeStruct((rows, LANES), bf16)],
                compiler_params=pltpu.CompilerParams(vmem_limit_bytes=12 * 1024 * 1024),
            )(notes)
    far = (send_on(behind[0][-1]), send_back(ahead[1][-1]))
    norm, delta, q_sums, down, up = [[None] * chunks for _ in range(5)]
    for c in each:
        catch_up(c, half - 1)
    state[:] = lax.optimization_barrier(state)
    for c in each:
        norm[c], delta[c], q_sums[c], sums = call(
            functools.partial(turn_kernel, half, heads, group, c * heads),
            [queries, out_grad, mask, hot, *far, *state[c]],
            [lines, lines, talls, jax.ShapeDtypeStruct(pairs.shape, bf16)],
            7,
            {6: 0, 7: 1, 8: 2},
        )
        if c + 1 < chunks:
            sums, state[c + 1] = lax.optimization_barrier((sums, state[c + 1]))
        else:
            sums, norm[0] = lax.optimization_barrier((sums, norm[0]))
        if c % 2:
            up[c] = send_on(sums)
        else:
            down[c] = send_back(sums)
    for r in range(half - 1, 0, -1):
        for c in each:
            q_sums[c], low, high = backward(c, pair_at(r), (r, peers - r), norm[c], delta[c], q_sums[c], scores.get((c, r)))
            low = low if down[c] is None else low + down[c].astype(f32)
            high = high if up[c] is None else high + up[c].astype(f32)
            after = (c + 1) % chunks
            low, high, norm[after] = lax.optimization_barrier((low.astype(bf16), high.astype(bf16), norm[after]))
            down[c], up[c] = send_back(low), send_on(high)
    total = []
    for c in each:
        q_sums[c], mine = backward(c, [own, own], (0,), norm[c], delta[c], q_sums[c])
        total.append((mine + down[c].astype(f32) + up[c].astype(f32)).astype(bf16))
    total[0], q_sums = lax.optimization_barrier((total[0], q_sums))
    (query_grad,) = call(
        functools.partial(finish_kernel, heads, group), q_sums, [jax.ShapeDtypeStruct(queries.shape, bf16)], 0, {}
    )
    total = jnp.concatenate(total, 2)
    return query_grad, total[0], total[1]


def local(queries, key_rows, value_rows, out_grad, owner_slot, block_links):
    rows = queries.shape[0]
    peers = lax.axis_size("seq")
    q_width, kv_width = queries.shape[1], key_rows.shape[1]
    slots = 4 * peers * max(1, rows // peers // 2)
    gathered = 2 * (peers - 1) * rows * 2 * kv_width
    relayed = slots * (3 * q_width + 4 * kv_width) + 4 * rows * 2 * kv_width
    fits = kv_width % (2 * HEAD_DIM) == 0 and peers > 2 and peers & (peers - 1) == 0 and rows % LANES == 0 and peers * rows // BLOCK <= LANES and block_links.size <= LANES
    plan = gather_plan if fits and gathered <= relayed else relay_plan
    return plan(queries, key_rows, value_rows, out_grad, owner_slot, block_links)


def solution(mesh):
    return jax.shard_map(
        local,
        mesh=mesh,
        in_specs=(
            P(("parts", "seq"), "head"),
            P(("parts", "seq"), "head"),
            P(("parts", "seq"), "head"),
            P(("parts", "seq"), "head"),
            P(("parts", "seq")),
            P(("parts", "seq"), None),
        ),
        out_specs=(
            P(("parts", "seq"), "head"),
            P(("parts", "seq"), "head"),
            P(("parts", "seq"), "head"),
        ),
        check_vma=False,
    )
```

```python
import functools

import jax
import jax.numpy as jnp
from jax import lax
from jax.experimental import pallas as pl
from jax.experimental.pallas import tpu as pltpu
from jax.sharding import PartitionSpec as P

HEAD_DIM = 128
BLOCK = 128


def padded(value, sides, width):
    for axis, dim in sides:
        peers, length = (lax.axis_size(axis), value.shape[dim])
        up = [(i, (i + 1) % peers) for i in range(peers - 1)]
        down = [(j, i) for i, j in up]
        last = lax.slice_in_dim(value, length - width, length, axis=dim)
        leading = lax.slice_in_dim(value, 0, width, axis=dim)
        before = lax.ppermute(last, axis, up)
        after = lax.ppermute(leading, axis, down)
        value = jnp.concatenate([before, value, after], axis=dim)
    return value


def from_behind(value, axis, by):
    peers = lax.axis_size(axis)
    pairs = [(i, i + by) for i in range(peers) if 0 <= i + by < peers]
    return lax.ppermute(value, axis, pairs)


def head_major(matrix, heads):
    return matrix.reshape(matrix.shape[0], heads, -1).transpose(1, 0, 2)


def relay_plan(queries, key_rows, value_rows, out_grad, owner_slot, block_links):
    row_count = queries.shape[0]
    seq_count = lax.axis_size("seq")
    capacity = 4 * max(1, row_count // seq_count // 2)
    slots = seq_count * capacity
    kv_width = key_rows.shape[1]
    kv_heads = kv_width // HEAD_DIM
    group_size = queries.shape[1] // kv_width
    score_scale = HEAD_DIM ** (-0.5)
    owner_dev = owner_slot // row_count
    owner_row = owner_slot % row_count
    member = (owner_dev[:, None] == jnp.arange(seq_count, dtype=jnp.int32)[None, :]).astype(
        jnp.int32
    )
    within = jnp.sum(jnp.cumsum(member, 0) * member, 1) - 1
    placed = owner_dev * capacity + within

    def pack_rows(matrix):
        return (
            jnp.zeros((slots, matrix.shape[1]), matrix.dtype)
            .at[placed]
            .set(matrix)
            .reshape(seq_count, capacity, matrix.shape[1])
        )

    vacant = jnp.array([row_count // 16, row_count % 16], jnp.float32)
    row_codes = jnp.stack([owner_row // 16, owner_row % 16], 1).astype(jnp.float32)
    code_buffer = (
        jnp.broadcast_to(vacant, (slots, 2))
        .at[placed]
        .set(row_codes)
        .astype(jnp.bfloat16)
        .reshape(seq_count, capacity, 2)
    )
    q_in, k_in, v_in, g_in, codes_in = (
        lax.all_to_all(pack_rows(queries), "seq", split_axis=0, concat_axis=0, tiled=True),
        lax.all_to_all(pack_rows(key_rows), "seq", split_axis=0, concat_axis=0, tiled=True),
        lax.all_to_all(pack_rows(value_rows), "seq", split_axis=0, concat_axis=0, tiled=True),
        lax.all_to_all(pack_rows(out_grad), "seq", split_axis=0, concat_axis=0, tiled=True),
        lax.all_to_all(code_buffer, "seq", split_axis=0, concat_axis=0, tiled=True),
    )
    arrived = codes_in.reshape(slots, 2).astype(jnp.float32)
    target = (arrived[:, 0] * 16.0 + arrived[:, 1]).astype(jnp.int32)

    def unpack_rows(buffer):
        flat_rows = buffer.reshape(slots, buffer.shape[2])
        return (
            jnp.zeros((row_count, flat_rows.shape[1]), flat_rows.dtype)
            .at[target]
            .set(flat_rows, mode="drop")
        )

    q_own = unpack_rows(q_in)
    k_own = unpack_rows(k_in)
    v_own = unpack_rows(v_in)
    g_own = unpack_rows(g_in)
    blocks = row_count // BLOCK
    span = block_links.shape[1]
    offset = (
        jnp.arange(3 * blocks, dtype=jnp.int32)[None, :]
        - jnp.arange(blocks, dtype=jnp.int32)[:, None]
    )
    selector = offset[:, :, None] == jnp.arange(span, dtype=jnp.int32)[None, None, :]
    allowed = jnp.sum(jnp.where(selector, block_links[:, None, :], 0), 2) > 0
    token_mask = jnp.repeat(jnp.repeat(allowed, BLOCK, 0), BLOCK, 1)
    kv_pair = jnp.concatenate([k_own, v_own], 1)
    kv_wide = padded(kv_pair, (("seq", 0),), row_count)

    def scores_of(q_group, k_group):
        raw_scores = (
            jnp.einsum("rgd,kd->grk", q_group, k_group, preferred_element_type=jnp.float32)
            * score_scale
        )
        return jnp.where(token_mask[None], raw_scores, -jnp.inf)

    def forward_head(operands):
        q_group, k_group, v_group = operands
        scores = scores_of(q_group, k_group)
        row_top = jnp.max(scores, -1, keepdims=True)
        log_total = row_top + jnp.log(jnp.sum(jnp.exp(scores - row_top), -1, keepdims=True))
        probs = jnp.exp(scores - log_total).astype(jnp.bfloat16)
        attended = jnp.einsum(
            "grk,kd->rgd", probs, v_group, preferred_element_type=jnp.float32
        ).astype(jnp.bfloat16)
        return (attended, log_total)

    def backward_head(operands):
        q_group, k_group, v_group, g_group, attended, log_total = operands
        weights = jnp.exp(scores_of(q_group, k_group) - log_total)
        row_delta = jnp.sum(g_group.astype(jnp.float32) * attended.astype(jnp.float32), -1).T[
            :, :, None
        ]
        d_probs = jnp.einsum("rgd,kd->grk", g_group, v_group, preferred_element_type=jnp.float32)
        d_scores = (weights * (d_probs - row_delta)).astype(jnp.bfloat16)
        q_grad = (
            jnp.einsum("grk,kd->rgd", d_scores, k_group, preferred_element_type=jnp.float32)
            * score_scale
        ).astype(jnp.bfloat16)
        k_grad = (
            jnp.einsum("grk,rgd->kd", d_scores, q_group, preferred_element_type=jnp.float32)
            * score_scale
        )
        v_grad = jnp.einsum(
            "grk,rgd->kd", weights.astype(jnp.bfloat16), g_group, preferred_element_type=jnp.float32
        )
        return (q_grad, k_grad, v_grad)

    query_heads = q_own.reshape(row_count, kv_heads, group_size, HEAD_DIM).transpose(1, 0, 2, 3)
    grad_heads = g_own.reshape(row_count, kv_heads, group_size, HEAD_DIM).transpose(1, 0, 2, 3)
    key_heads = head_major(kv_wide[:, :kv_width], kv_heads)
    value_heads = head_major(kv_wide[:, kv_width:], kv_heads)
    attended, log_total = lax.map(forward_head, (query_heads, key_heads, value_heads))
    q_grads, k_grads, v_grads = lax.map(
        backward_head, (query_heads, key_heads, value_heads, grad_heads, attended, log_total)
    )
    q_grad_own = q_grads.transpose(1, 0, 2, 3).reshape(row_count, kv_heads * group_size * HEAD_DIM)
    kv_grads = jnp.concatenate(
        [
            k_grads.transpose(1, 0, 2).reshape(3 * row_count, kv_width),
            v_grads.transpose(1, 0, 2).reshape(3 * row_count, kv_width),
        ],
        1,
    )
    from_above = from_behind(kv_grads[:row_count].astype(jnp.bfloat16), "seq", -1).astype(
        jnp.float32
    )
    from_below = from_behind(kv_grads[2 * row_count :].astype(jnp.bfloat16), "seq", 1).astype(
        jnp.float32
    )
    kv_total = (kv_grads[row_count : 2 * row_count] + from_above + from_below).astype(jnp.bfloat16)
    pick_rows = jnp.minimum(target, row_count - 1)

    def gather_back(matrix):
        return matrix[pick_rows].reshape(seq_count, capacity, matrix.shape[1])

    q_back, k_back, v_back = (
        lax.all_to_all(gather_back(q_grad_own), "seq", split_axis=0, concat_axis=0, tiled=True),
        lax.all_to_all(
            gather_back(kv_total[:, :kv_width]), "seq", split_axis=0, concat_axis=0, tiled=True
        ),
        lax.all_to_all(
            gather_back(kv_total[:, kv_width:]), "seq", split_axis=0, concat_axis=0, tiled=True
        ),
    )

    def settle_rows(buffer):
        return buffer.reshape(slots, buffer.shape[2])[placed]

    return (settle_rows(q_back), settle_rows(k_back), settle_rows(v_back))


LOG2_E = 1.4426950408889634
MASKED = -1e30
LANES = 128
SAVED_FROM = 3
NT = (((1,), (1,)), ((), ()))
NN = (((1,), (0,)), ((), ()))
IN_VMEM = pl.BlockSpec(memory_space=pltpu.VMEM)
IN_SMEM = pl.BlockSpec(memory_space=pltpu.SMEM)


def dot(a, b, dims):
    return lax.dot_general(a, b, dims, preferred_element_type=jnp.float32)


def flip(a):
    return a.astype(jnp.float32).T.astype(jnp.bfloat16)


def columns(ref, at):
    return ref[:, lanes_of(at)]


def lanes_of(at):
    return pl.ds(pl.multiple_of(at * HEAD_DIM, HEAD_DIM), HEAD_DIM)


def stacked_heads(ref, head, group):
    return jnp.concatenate([columns(ref, head * group + j) for j in range(group)], 0)


def masks_kernel(peers, blocks_dev, span, slot_rows, notes_ref, key_hot_ref, query_mask_ref):
    f32, bf16 = jnp.float32, jnp.bfloat16
    rows = lax.broadcasted_iota(jnp.int32, (LANES, LANES), 0)
    lanes = lax.broadcasted_iota(jnp.int32, (LANES, LANES), 1)

    def hot(slots):
        return (rows == slots // BLOCK).astype(f32).T.astype(bf16)

    me = lax.axis_index("seq")
    place = jnp.where(me % 2 == 0, me // 2, peers - (me + 1) // 2)
    for r in range(peers):
        behind = (place + peers - r) % peers
        shard = notes_ref[jnp.where(behind < peers // 2, 2 * behind, 2 * peers - 1 - 2 * behind)]
        for i in range(slot_rows):
            key_hot_ref[r, i * LANES : (i + 1) * LANES, :] = hot(shard[i : i + 1, :])
    owners = lax.broadcasted_iota(jnp.int32, (LANES, peers), 0) // blocks_dev
    spread = (owners == lax.broadcasted_iota(jnp.int32, (LANES, peers), 1)).astype(f32)
    link_rows = jnp.concatenate([notes_ref[p][slot_rows : slot_rows + 1, :] for p in range(peers)], 0).astype(f32)
    of_block = dot(spread, link_rows, NN)
    table = jnp.zeros((LANES, LANES), f32)
    for s in range(span):
        picked = jnp.sum(jnp.where(lanes == (rows % blocks_dev) * span + s, of_block, 0.0), 1, keepdims=True)
        table = table + jnp.where(lanes == rows + s - span // 2, picked, 0.0)
    table = table.astype(bf16)
    linked = dot(key_hot_ref[0], table, NN)
    query_mask_ref[...] = jnp.where(linked > 0.5, 0.0, MASKED).astype(bf16)


def keys_of(shards, head):
    return jnp.concatenate([columns(k, head) for k, _, _ in shards], 0)


def values_of(shards, head):
    return jnp.concatenate([columns(v, head) for _, v, _ in shards], 0)


def split(refs, count, hot_ref, at):
    shards = [(refs[2 * i], refs[2 * i + 1], hot_ref.at[at[i]]) for i in range(count)]
    if at[0] == 0:
        keys, values, hot = shards[0]
        shards[0] = (keys.at[0], values.at[1], hot)
    return shards


def masked_scores(q_ref, mask, shards, hots, head, group, first):
    queries = jnp.concatenate([stacked_heads(q_ref, first + head, group), jnp.concatenate([mask] * group, 0)], 1)
    return dot(jnp.concatenate([keys_of(shards, first + head), hots], 1), queries, NT)


def absorb(scores, values, state):
    factor = HEAD_DIM ** (-0.5) * LOG2_E
    top = jnp.max(scores, 0, keepdims=True)
    if state is not None:
        top = jnp.maximum(top, state[0])
    weights = jnp.exp2((scores - top) * factor)
    total = jnp.sum(weights, 0, keepdims=True)
    mixed = dot(flip(values), weights.astype(jnp.bfloat16), NN)
    if state is not None:
        keep = jnp.exp2((state[0] - top) * factor)
        total = total + state[1] * keep
        mixed = mixed + state[2] * keep
    return top, total, mixed


def backprop(q_ref, g_ref, shards, scores, head, group, first, norm, delta):
    scale = HEAD_DIM ** (-0.5)
    queries, grads = stacked_heads(q_ref, first + head, group), stacked_heads(g_ref, first + head, group)
    weights = jnp.exp2(scores * (scale * LOG2_E) - norm)
    d_scores = (weights * (dot(values_of(shards, first + head), grads, NT) - delta)).astype(jnp.bfloat16)
    k_grad = dot(d_scores, queries, NN) * scale
    v_grad = dot(weights.astype(jnp.bfloat16), grads, NN)
    return k_grad, v_grad, dot(flip(keys_of(shards, first + head)), d_scores, NN)


def forward_kernel(at, heads, group, first, saved, q_ref, mask_ref, hot_ref, *refs):
    shards = split(refs, len(at), hot_ref, at)
    state, outs = refs[2 * len(at) : -3 - saved], refs[len(refs) - 3 - saved :]
    rows = q_ref.shape[0]
    factor = HEAD_DIM ** (-0.5) * LOG2_E

    @pl.loop(0, heads)
    def _(head):
        keys = [jnp.concatenate([columns(k, first + head), hot[...]], 1) for k, _, hot in shards]
        values = flip(values_of(shards, first + head))
        scores, tops = [], []
        for j in range(group):
            span = slice(j * rows, (j + 1) * rows)
            query = jnp.concatenate([columns(q_ref, (first + head) * group + j), mask_ref[...]], 1)
            scores.append([dot(key, query, NT) for key in keys])
            if saved:
                for i, part in enumerate(scores[j]):
                    outs[3][head, i * rows : (i + 1) * rows, span] = part
            tops.append(functools.reduce(jnp.maximum, [jnp.max(s, 0, keepdims=True) for s in scores[j]]))
            if state:
                tops[j] = jnp.maximum(tops[j], state[0][head][:, span])
        for j in range(group):
            span = slice(j * rows, (j + 1) * rows)
            weights = [jnp.exp2((s - tops[j]) * factor) for s in scores[j]]
            total = sum(jnp.sum(w, 0, keepdims=True) for w in weights)
            mixed = dot(values, jnp.concatenate([w.astype(jnp.bfloat16) for w in weights], 0), NN)
            if state:
                keep = jnp.exp2((state[0][head][:, span] - tops[j]) * factor)
                total = total + state[1][head][:, span] * keep
                mixed = mixed + state[2][head][:, span] * keep
            outs[0][head, :, span], outs[1][head, :, span], outs[2][head, :, span] = tops[j], total, mixed


def turn_kernel(at, heads, group, first, q_ref, g_ref, mask_ref, hot_ref, k_ref, v_ref, top, total, mixed, norm_ref, delta_ref, q_out, grads_out):
    shards = split([k_ref, v_ref], 1, hot_ref, (at,))
    @pl.loop(0, heads)
    def _(head):
        scores = masked_scores(q_ref, mask_ref[...], shards, hot_ref[at], head, group, first)
        state = absorb(scores, values_of(shards, first + head), (top[head], total[head], mixed[head]))
        norm = state[0] * (HEAD_DIM ** (-0.5) * LOG2_E) + jnp.log2(state[1])
        attended = (state[2] / state[1]).astype(jnp.bfloat16).astype(jnp.float32)
        grads = stacked_heads(g_ref, first + head, group).astype(jnp.float32).T
        delta = jnp.sum(grads * attended, 0, keepdims=True)
        norm_ref[head], delta_ref[head] = norm, delta
        k_grad, v_grad, q_out[head] = backprop(q_ref, g_ref, shards, scores, head, group, first, norm, delta)
        store_grads([grads_out], head, k_grad, v_grad)


def backward_kernel(at, heads, group, first, saved, q_ref, g_ref, mask_ref, hot_ref, *refs):
    count = len(at)
    if saved:
        scores_ref, *refs = refs
    shards = split(refs, count, hot_ref, at)
    norm_ref, delta_ref, q_in, q_out = refs[2 * count : 2 * count + 4]
    hots = jnp.concatenate([hot[...] for _, _, hot in shards], 0)
    @pl.loop(0, heads)
    def _(head):
        scores = scores_ref[head] if saved else masked_scores(q_ref, mask_ref[...], shards, hots, head, group, first)
        k_grad, v_grad, q_terms = backprop(q_ref, g_ref, shards, scores, head, group, first, norm_ref[head], delta_ref[head])
        store_grads(refs[2 * count + 4 :], head, k_grad, v_grad)
        q_out[head] = q_in[head] + q_terms


def store_grads(outs, head, k_grad, v_grad):
    span = lanes_of(head)
    for i, out in enumerate(outs):
        rows = out.shape[1]
        out[0, :, span] = k_grad[i * rows : (i + 1) * rows].astype(out.dtype)
        out[1, :, span] = v_grad[i * rows : (i + 1) * rows].astype(out.dtype)


def finish_kernel(heads, group, *refs):
    *q_sums, q_out = refs
    rows = q_out.shape[0]

    @pl.loop(0, heads)
    def _(head):
        for c, sums in enumerate(q_sums):
            for j in range(group):
                part = sums[head, :, j * rows : (j + 1) * rows] * HEAD_DIM ** (-0.5)
                q_out[:, lanes_of((c * heads + head) * group + j)] = part.T.astype(jnp.bfloat16)


def gather_plan(queries, key_rows, value_rows, out_grad, owner_slot, block_links):
    rows = queries.shape[0]
    peers = lax.axis_size("seq")
    half = peers // 2
    kv_heads = key_rows.shape[1] // HEAD_DIM
    group = queries.shape[1] // key_rows.shape[1]
    chunks = 2
    heads = kv_heads // chunks
    width = heads * HEAD_DIM
    each = range(chunks)
    f32, bf16 = jnp.float32, jnp.bfloat16
    ring = list(range(0, peers, 2)) + list(range(peers - 1, 0, -2))
    onward = [(ring[i], ring[(i + 1) % peers]) for i in range(peers)]
    back = [(b, a) for a, b in onward]

    def send_on(value):
        return lax.ppermute(value, "seq", onward)

    def send_back(value):
        return lax.ppermute(value, "seq", back)

    def call(kernel, args, outs, products, aliases):
        return pl.pallas_call(
            kernel,
            in_specs=[IN_VMEM] * len(args),
            out_specs=[IN_VMEM] * len(outs),
            out_shape=outs,
            input_output_aliases=aliases,
            cost_estimate=pl.CostEstimate(
                flops=products, bytes_accessed=rows, transcendentals=0
            ),
            compiler_params=pltpu.CompilerParams(vmem_limit_bytes=12 * 1024 * 1024),
        )(*args)

    span = block_links.shape[1]
    slots = owner_slot.reshape(rows // LANES, LANES)
    links = jnp.pad(block_links.reshape(1, -1), ((0, 0), (0, LANES - block_links.size)))
    notes = jnp.concatenate([slots, links], 0)
    notes = jnp.pad(notes, ((0, -notes.shape[0] % 8), (0, 0)))[None]
    notes = lax.all_to_all(jnp.broadcast_to(notes, (peers,) + notes.shape[1:]), "seq", split_axis=0, concat_axis=0, tiled=True)
    lines = jax.ShapeDtypeStruct((heads, 1, group * rows), f32)
    talls = jax.ShapeDtypeStruct((heads, HEAD_DIM, group * rows), f32)
    pairs = jax.ShapeDtypeStruct((2, rows, width), f32)

    def forward(c, shards, at, state, saved):
        args = [queries, mask, hot, *shards, *state]
        kernel = functools.partial(forward_kernel, at, heads, group, c * heads, saved)
        aliases = {len(args) - 3 + i: i for i in range(3)} if state else {}
        kept = [jax.ShapeDtypeStruct((heads, len(at) * rows, group * rows), f32)] * saved
        return call(kernel, args, [lines, lines, talls] + kept, 2 * len(at), aliases)

    def backward(c, shards, at, norm, delta, q_sums, scores=None):
        saved = scores is not None
        args = [queries, out_grad, mask, hot, *([scores] * saved), *shards, norm, delta, q_sums]
        kernel = functools.partial(backward_kernel, at, heads, group, c * heads, saved)
        return call(kernel, args, [talls] + [pairs] * len(at), 5 * len(at), {len(args) - 1: 0})

    own = (key_rows, value_rows)
    behind, ahead = [[v] for v in own], [[v] for v in own]
    state = [() for _ in each]
    hot = mask = None
    scores = {}

    def pair_at(r):
        return [side[i][r] for side in (behind, ahead) for i in range(2)]

    def catch_up(c, r):
        shards, at = pair_at(r), (r, peers - r)
        if r == 1:
            shards, at = [own, own, *shards], (0,) + at
        *state[c], = forward(c, shards, at, state[c], r >= SAVED_FROM)
        if r >= SAVED_FROM:
            scores[c, r] = state[c].pop()

    for r in range(1, half):
        for c in each:
            low, high = send_on(behind[c][-1]), send_back(ahead[c][-1])
            if (r, c) == (1, 0):
                low, high, own = lax.optimization_barrier((low, high, own))
                own = jnp.stack(own)
            elif (r, c) == (1, 1):
                low, high, notes = lax.optimization_barrier((low, high, notes))
            elif (r, c) == (2, 0):
                low, high, own = lax.optimization_barrier((low, high, own))
            elif (r, c) == (2, 1):
                catch_up(0, 1)
                low, high, state[0] = lax.optimization_barrier((low, high, state[0]))
                catch_up(1, 1)
            else:
                if c:
                    catch_up(0, r - 1)
                    catch_up(1, r - 1)
                low, high, state[:] = lax.optimization_barrier((low, high, state))
            behind[c].append(low)
            ahead[c].append(high)
        if r == 1:
            hot, mask = pl.pallas_call(
                functools.partial(masks_kernel, peers, rows // BLOCK, span, rows // LANES),
                in_specs=[IN_VMEM],
                out_specs=[IN_VMEM] * 2,
                out_shape=[jax.ShapeDtypeStruct((peers, rows, LANES), bf16), jax.ShapeDtypeStruct((rows, LANES), bf16)],
                compiler_params=pltpu.CompilerParams(vmem_limit_bytes=12 * 1024 * 1024),
            )(notes)
    far = (send_on(behind[0][-1]), send_back(ahead[1][-1]))
    norm, delta, q_sums, down, up = [[None] * chunks for _ in range(5)]
    for c in each:
        catch_up(c, half - 1)
    state[:] = lax.optimization_barrier(state)
    for c in each:
        norm[c], delta[c], q_sums[c], sums = call(
            functools.partial(turn_kernel, half, heads, group, c * heads),
            [queries, out_grad, mask, hot, *far, *state[c]],
            [lines, lines, talls, jax.ShapeDtypeStruct(pairs.shape, bf16)],
            7,
            {6: 0, 7: 1, 8: 2},
        )
        if c + 1 < chunks:
            sums, state[c + 1] = lax.optimization_barrier((sums, state[c + 1]))
        else:
            sums, norm[0] = lax.optimization_barrier((sums, norm[0]))
        if c % 2:
            up[c] = send_on(sums)
        else:
            down[c] = send_back(sums)
    for r in range(half - 1, 0, -1):
        for c in each:
            q_sums[c], low, high = backward(c, pair_at(r), (r, peers - r), norm[c], delta[c], q_sums[c], scores.get((c, r)))
            low = low if down[c] is None else low + down[c].astype(f32)
            high = high if up[c] is None else high + up[c].astype(f32)
            after = (c + 1) % chunks
            low, high, norm[after] = lax.optimization_barrier((low.astype(bf16), high.astype(bf16), norm[after]))
            down[c], up[c] = send_back(low), send_on(high)
    total = []
    for c in each:
        q_sums[c], mine = backward(c, [own, own], (0,), norm[c], delta[c], q_sums[c])
        total.append((mine + down[c].astype(f32) + up[c].astype(f32)).astype(bf16))
    total[0], q_sums = lax.optimization_barrier((total[0], q_sums))
    (query_grad,) = call(
        functools.partial(finish_kernel, heads, group), q_sums, [jax.ShapeDtypeStruct(queries.shape, bf16)], 0, {}
    )
    total = jnp.concatenate(total, 2)
    return query_grad, total[0], total[1]


def local(queries, key_rows, value_rows, out_grad, owner_slot, block_links):
    rows = queries.shape[0]
    peers = lax.axis_size("seq")
    q_width, kv_width = queries.shape[1], key_rows.shape[1]
    slots = 4 * peers * max(1, rows // peers // 2)
    gathered = 2 * (peers - 1) * rows * 2 * kv_width
    relayed = slots * (3 * q_width + 4 * kv_width) + 4 * rows * 2 * kv_width
    fits = kv_width % (2 * HEAD_DIM) == 0 and peers > 2 and peers & (peers - 1) == 0 and rows % LANES == 0 and peers * rows // BLOCK <= LANES and block_links.size <= LANES
    plan = gather_plan if fits and gathered <= relayed else relay_plan
    return plan(queries, key_rows, value_rows, out_grad, owner_slot, block_links)


def solution(mesh):
    return jax.shard_map(
        local,
        mesh=mesh,
        in_specs=(
            P(("parts", "seq"), "head"),
            P(("parts", "seq"), "head"),
            P(("parts", "seq"), "head"),
            P(("parts", "seq"), "head"),
            P(("parts", "seq")),
            P(("parts", "seq"), None),
        ),
        out_specs=(
            P(("parts", "seq"), "head"),
            P(("parts", "seq"), "head"),
            P(("parts", "seq"), "head"),
        ),
        check_vma=False,
    )
```

```python
import functools

import jax
import jax.numpy as jnp
from jax import lax
from jax.experimental import pallas as pl
from jax.experimental.pallas import tpu as pltpu
from jax.sharding import PartitionSpec as P

HEAD_DIM = 128
BLOCK = 128


def padded(value, sides, width):
    for axis, dim in sides:
        peers, length = (lax.axis_size(axis), value.shape[dim])
        up = [(i, (i + 1) % peers) for i in range(peers - 1)]
        down = [(j, i) for i, j in up]
        last = lax.slice_in_dim(value, length - width, length, axis=dim)
        leading = lax.slice_in_dim(value, 0, width, axis=dim)
        before = lax.ppermute(last, axis, up)
        after = lax.ppermute(leading, axis, down)
        value = jnp.concatenate([before, value, after], axis=dim)
    return value


def from_behind(value, axis, by):
    peers = lax.axis_size(axis)
    pairs = [(i, i + by) for i in range(peers) if 0 <= i + by < peers]
    return lax.ppermute(value, axis, pairs)


def head_major(matrix, heads):
    return matrix.reshape(matrix.shape[0], heads, -1).transpose(1, 0, 2)


def relay_plan(queries, key_rows, value_rows, out_grad, owner_slot, block_links):
    row_count = queries.shape[0]
    seq_count = lax.axis_size("seq")
    capacity = 4 * max(1, row_count // seq_count // 2)
    slots = seq_count * capacity
    kv_width = key_rows.shape[1]
    kv_heads = kv_width // HEAD_DIM
    group_size = queries.shape[1] // kv_width
    score_scale = HEAD_DIM ** (-0.5)
    owner_dev = owner_slot // row_count
    owner_row = owner_slot % row_count
    member = (owner_dev[:, None] == jnp.arange(seq_count, dtype=jnp.int32)[None, :]).astype(
        jnp.int32
    )
    within = jnp.sum(jnp.cumsum(member, 0) * member, 1) - 1
    placed = owner_dev * capacity + within

    def pack_rows(matrix):
        return (
            jnp.zeros((slots, matrix.shape[1]), matrix.dtype)
            .at[placed]
            .set(matrix)
            .reshape(seq_count, capacity, matrix.shape[1])
        )

    vacant = jnp.array([row_count // 16, row_count % 16], jnp.float32)
    row_codes = jnp.stack([owner_row // 16, owner_row % 16], 1).astype(jnp.float32)
    code_buffer = (
        jnp.broadcast_to(vacant, (slots, 2))
        .at[placed]
        .set(row_codes)
        .astype(jnp.bfloat16)
        .reshape(seq_count, capacity, 2)
    )
    q_in, k_in, v_in, g_in, codes_in = (
        lax.all_to_all(pack_rows(queries), "seq", split_axis=0, concat_axis=0, tiled=True),
        lax.all_to_all(pack_rows(key_rows), "seq", split_axis=0, concat_axis=0, tiled=True),
        lax.all_to_all(pack_rows(value_rows), "seq", split_axis=0, concat_axis=0, tiled=True),
        lax.all_to_all(pack_rows(out_grad), "seq", split_axis=0, concat_axis=0, tiled=True),
        lax.all_to_all(code_buffer, "seq", split_axis=0, concat_axis=0, tiled=True),
    )
    arrived = codes_in.reshape(slots, 2).astype(jnp.float32)
    target = (arrived[:, 0] * 16.0 + arrived[:, 1]).astype(jnp.int32)

    def unpack_rows(buffer):
        flat_rows = buffer.reshape(slots, buffer.shape[2])
        return (
            jnp.zeros((row_count, flat_rows.shape[1]), flat_rows.dtype)
            .at[target]
            .set(flat_rows, mode="drop")
        )

    q_own = unpack_rows(q_in)
    k_own = unpack_rows(k_in)
    v_own = unpack_rows(v_in)
    g_own = unpack_rows(g_in)
    blocks = row_count // BLOCK
    span = block_links.shape[1]
    offset = (
        jnp.arange(3 * blocks, dtype=jnp.int32)[None, :]
        - jnp.arange(blocks, dtype=jnp.int32)[:, None]
    )
    selector = offset[:, :, None] == jnp.arange(span, dtype=jnp.int32)[None, None, :]
    allowed = jnp.sum(jnp.where(selector, block_links[:, None, :], 0), 2) > 0
    token_mask = jnp.repeat(jnp.repeat(allowed, BLOCK, 0), BLOCK, 1)
    kv_pair = jnp.concatenate([k_own, v_own], 1)
    kv_wide = padded(kv_pair, (("seq", 0),), row_count)

    def scores_of(q_group, k_group):
        raw_scores = (
            jnp.einsum("rgd,kd->grk", q_group, k_group, preferred_element_type=jnp.float32)
            * score_scale
        )
        return jnp.where(token_mask[None], raw_scores, -jnp.inf)

    def forward_head(operands):
        q_group, k_group, v_group = operands
        scores = scores_of(q_group, k_group)
        row_top = jnp.max(scores, -1, keepdims=True)
        log_total = row_top + jnp.log(jnp.sum(jnp.exp(scores - row_top), -1, keepdims=True))
        probs = jnp.exp(scores - log_total).astype(jnp.bfloat16)
        attended = jnp.einsum(
            "grk,kd->rgd", probs, v_group, preferred_element_type=jnp.float32
        ).astype(jnp.bfloat16)
        return (attended, log_total)

    def backward_head(operands):
        q_group, k_group, v_group, g_group, attended, log_total = operands
        weights = jnp.exp(scores_of(q_group, k_group) - log_total)
        row_delta = jnp.sum(g_group.astype(jnp.float32) * attended.astype(jnp.float32), -1).T[
            :, :, None
        ]
        d_probs = jnp.einsum("rgd,kd->grk", g_group, v_group, preferred_element_type=jnp.float32)
        d_scores = (weights * (d_probs - row_delta)).astype(jnp.bfloat16)
        q_grad = (
            jnp.einsum("grk,kd->rgd", d_scores, k_group, preferred_element_type=jnp.float32)
            * score_scale
        ).astype(jnp.bfloat16)
        k_grad = (
            jnp.einsum("grk,rgd->kd", d_scores, q_group, preferred_element_type=jnp.float32)
            * score_scale
        )
        v_grad = jnp.einsum(
            "grk,rgd->kd", weights.astype(jnp.bfloat16), g_group, preferred_element_type=jnp.float32
        )
        return (q_grad, k_grad, v_grad)

    query_heads = q_own.reshape(row_count, kv_heads, group_size, HEAD_DIM).transpose(1, 0, 2, 3)
    grad_heads = g_own.reshape(row_count, kv_heads, group_size, HEAD_DIM).transpose(1, 0, 2, 3)
    key_heads = head_major(kv_wide[:, :kv_width], kv_heads)
    value_heads = head_major(kv_wide[:, kv_width:], kv_heads)
    attended, log_total = lax.map(forward_head, (query_heads, key_heads, value_heads))
    q_grads, k_grads, v_grads = lax.map(
        backward_head, (query_heads, key_heads, value_heads, grad_heads, attended, log_total)
    )
    q_grad_own = q_grads.transpose(1, 0, 2, 3).reshape(row_count, kv_heads * group_size * HEAD_DIM)
    kv_grads = jnp.concatenate(
        [
            k_grads.transpose(1, 0, 2).reshape(3 * row_count, kv_width),
            v_grads.transpose(1, 0, 2).reshape(3 * row_count, kv_width),
        ],
        1,
    )
    from_above = from_behind(kv_grads[:row_count].astype(jnp.bfloat16), "seq", -1).astype(
        jnp.float32
    )
    from_below = from_behind(kv_grads[2 * row_count :].astype(jnp.bfloat16), "seq", 1).astype(
        jnp.float32
    )
    kv_total = (kv_grads[row_count : 2 * row_count] + from_above + from_below).astype(jnp.bfloat16)
    pick_rows = jnp.minimum(target, row_count - 1)

    def gather_back(matrix):
        return matrix[pick_rows].reshape(seq_count, capacity, matrix.shape[1])

    q_back, k_back, v_back = (
        lax.all_to_all(gather_back(q_grad_own), "seq", split_axis=0, concat_axis=0, tiled=True),
        lax.all_to_all(
            gather_back(kv_total[:, :kv_width]), "seq", split_axis=0, concat_axis=0, tiled=True
        ),
        lax.all_to_all(
            gather_back(kv_total[:, kv_width:]), "seq", split_axis=0, concat_axis=0, tiled=True
        ),
    )

    def settle_rows(buffer):
        return buffer.reshape(slots, buffer.shape[2])[placed]

    return (settle_rows(q_back), settle_rows(k_back), settle_rows(v_back))


LOG2_E = 1.4426950408889634
MASKED = -1e30
LANES = 128
SAVED_FROM = 64
NT = (((1,), (1,)), ((), ()))
NN = (((1,), (0,)), ((), ()))
IN_VMEM = pl.BlockSpec(memory_space=pltpu.VMEM)
IN_SMEM = pl.BlockSpec(memory_space=pltpu.SMEM)


def dot(a, b, dims):
    return lax.dot_general(a, b, dims, preferred_element_type=jnp.float32)


def flip(a):
    return a.astype(jnp.float32).T.astype(jnp.bfloat16)


def columns(ref, at):
    return ref[:, lanes_of(at)]


def lanes_of(at):
    return pl.ds(pl.multiple_of(at * HEAD_DIM, HEAD_DIM), HEAD_DIM)


def stacked_heads(ref, head, group):
    return jnp.concatenate([columns(ref, head * group + j) for j in range(group)], 0)


def masks_kernel(peers, blocks_dev, span, slot_rows, notes_ref, key_hot_ref, query_mask_ref):
    f32, bf16 = jnp.float32, jnp.bfloat16
    rows = lax.broadcasted_iota(jnp.int32, (LANES, LANES), 0)
    lanes = lax.broadcasted_iota(jnp.int32, (LANES, LANES), 1)

    def hot(slots):
        return (rows == slots // BLOCK).astype(f32).T.astype(bf16)

    me = lax.axis_index("seq")
    place = jnp.where(me % 2 == 0, me // 2, peers - (me + 1) // 2)
    for r in range(peers):
        behind = (place + peers - r) % peers
        shard = notes_ref[jnp.where(behind < peers // 2, 2 * behind, 2 * peers - 1 - 2 * behind)]
        for i in range(slot_rows):
            key_hot_ref[r, i * LANES : (i + 1) * LANES, :] = hot(shard[i : i + 1, :])
    owners = lax.broadcasted_iota(jnp.int32, (LANES, peers), 0) // blocks_dev
    spread = (owners == lax.broadcasted_iota(jnp.int32, (LANES, peers), 1)).astype(f32)
    link_rows = jnp.concatenate([notes_ref[p][slot_rows : slot_rows + 1, :] for p in range(peers)], 0).astype(f32)
    of_block = dot(spread, link_rows, NN)
    table = jnp.zeros((LANES, LANES), f32)
    for s in range(span):
        picked = jnp.sum(jnp.where(lanes == (rows % blocks_dev) * span + s, of_block, 0.0), 1, keepdims=True)
        table = table + jnp.where(lanes == rows + s - span // 2, picked, 0.0)
    table = table.astype(bf16)
    linked = dot(key_hot_ref[0], table, NN)
    query_mask_ref[...] = jnp.where(linked > 0.5, 0.0, MASKED).astype(bf16)


def keys_of(shards, head):
    return jnp.concatenate([columns(k, head) for k, _, _ in shards], 0)


def values_of(shards, head):
    return jnp.concatenate([columns(v, head) for _, v, _ in shards], 0)


def split(refs, count, hot_ref, at):
    shards = [(refs[2 * i], refs[2 * i + 1], hot_ref.at[at[i]]) for i in range(count)]
    if at[0] == 0:
        keys, values, hot = shards[0]
        shards[0] = (keys.at[0], values.at[1], hot)
    return shards


def masked_scores(q_ref, mask, shards, hots, head, group, first):
    queries = jnp.concatenate([stacked_heads(q_ref, first + head, group), jnp.concatenate([mask] * group, 0)], 1)
    return dot(jnp.concatenate([keys_of(shards, first + head), hots], 1), queries, NT)


def absorb(scores, values, state):
    factor = HEAD_DIM ** (-0.5) * LOG2_E
    top = jnp.max(scores, 0, keepdims=True)
    if state is not None:
        top = jnp.maximum(top, state[0])
    weights = jnp.exp2((scores - top) * factor)
    total = jnp.sum(weights, 0, keepdims=True)
    mixed = dot(flip(values), weights.astype(jnp.bfloat16), NN)
    if state is not None:
        keep = jnp.exp2((state[0] - top) * factor)
        total = total + state[1] * keep
        mixed = mixed + state[2] * keep
    return top, total, mixed


def backprop(q_ref, g_ref, shards, scores, head, group, first, norm, delta):
    scale = HEAD_DIM ** (-0.5)
    queries, grads = stacked_heads(q_ref, first + head, group), stacked_heads(g_ref, first + head, group)
    weights = jnp.exp2(scores * (scale * LOG2_E) - norm)
    d_scores = (weights * (dot(values_of(shards, first + head), grads, NT) - delta)).astype(jnp.bfloat16)
    k_grad = dot(d_scores, queries, NN) * scale
    v_grad = dot(weights.astype(jnp.bfloat16), grads, NN)
    return k_grad, v_grad, dot(flip(keys_of(shards, first + head)), d_scores, NN)


def forward_kernel(at, heads, group, first, saved, q_ref, mask_ref, hot_ref, *refs):
    shards = split(refs, len(at), hot_ref, at)
    state, outs = refs[2 * len(at) : -3 - saved], refs[len(refs) - 3 - saved :]
    rows = q_ref.shape[0]
    factor = HEAD_DIM ** (-0.5) * LOG2_E

    @pl.loop(0, heads)
    def _(head):
        keys = [jnp.concatenate([columns(k, first + head), hot[...]], 1) for k, _, hot in shards]
        values = flip(values_of(shards, first + head))
        scores, tops = [], []
        for j in range(group):
            span = slice(j * rows, (j + 1) * rows)
            query = jnp.concatenate([columns(q_ref, (first + head) * group + j), mask_ref[...]], 1)
            scores.append([dot(key, query, NT) for key in keys])
            if saved:
                for i, part in enumerate(scores[j]):
                    outs[3][head, i * rows : (i + 1) * rows, span] = part
            tops.append(functools.reduce(jnp.maximum, [jnp.max(s, 0, keepdims=True) for s in scores[j]]))
            if state:
                tops[j] = jnp.maximum(tops[j], state[0][head][:, span])
        for j in range(group):
            span = slice(j * rows, (j + 1) * rows)
            weights = [jnp.exp2((s - tops[j]) * factor) for s in scores[j]]
            total = sum(jnp.sum(w, 0, keepdims=True) for w in weights)
            mixed = dot(values, jnp.concatenate([w.astype(jnp.bfloat16) for w in weights], 0), NN)
            if state:
                keep = jnp.exp2((state[0][head][:, span] - tops[j]) * factor)
                total = total + state[1][head][:, span] * keep
                mixed = mixed + state[2][head][:, span] * keep
            outs[0][head, :, span], outs[1][head, :, span], outs[2][head, :, span] = tops[j], total, mixed


def turn_kernel(at, heads, group, first, q_ref, g_ref, mask_ref, hot_ref, k_ref, v_ref, top, total, mixed, norm_ref, delta_ref, q_out, grads_out):
    shards = split([k_ref, v_ref], 1, hot_ref, (at,))
    for head in range(heads):
        scores = masked_scores(q_ref, mask_ref[...], shards, hot_ref[at], head, group, first)
        state = absorb(scores, values_of(shards, first + head), (top[head], total[head], mixed[head]))
        norm = state[0] * (HEAD_DIM ** (-0.5) * LOG2_E) + jnp.log2(state[1])
        attended = (state[2] / state[1]).astype(jnp.bfloat16).astype(jnp.float32)
        grads = stacked_heads(g_ref, first + head, group).astype(jnp.float32).T
        delta = jnp.sum(grads * attended, 0, keepdims=True)
        norm_ref[head], delta_ref[head] = norm, delta
        k_grad, v_grad, q_out[head] = backprop(q_ref, g_ref, shards, scores, head, group, first, norm, delta)
        store_grads([grads_out], head, k_grad, v_grad)


def backward_kernel(at, heads, group, first, saved, q_ref, g_ref, mask_ref, hot_ref, *refs):
    count = len(at)
    if saved:
        scores_ref, *refs = refs
    shards = split(refs, count, hot_ref, at)
    norm_ref, delta_ref, q_in, q_out = refs[2 * count : 2 * count + 4]
    hots = jnp.concatenate([hot[...] for _, _, hot in shards], 0)
    @pl.loop(0, heads)
    def _(head):
        scores = scores_ref[head] if saved else masked_scores(q_ref, mask_ref[...], shards, hots, head, group, first)
        k_grad, v_grad, q_terms = backprop(q_ref, g_ref, shards, scores, head, group, first, norm_ref[head], delta_ref[head])
        store_grads(refs[2 * count + 4 :], head, k_grad, v_grad)
        q_out[head] = q_in[head] + q_terms


def store_grads(outs, head, k_grad, v_grad):
    span = lanes_of(head)
    for i, out in enumerate(outs):
        rows = out.shape[1]
        out[0, :, span] = k_grad[i * rows : (i + 1) * rows].astype(out.dtype)
        out[1, :, span] = v_grad[i * rows : (i + 1) * rows].astype(out.dtype)


def finish_kernel(heads, group, *refs):
    *q_sums, q_out = refs
    rows = q_out.shape[0]

    @pl.loop(0, heads)
    def _(head):
        for c, sums in enumerate(q_sums):
            for j in range(group):
                part = sums[head, :, j * rows : (j + 1) * rows] * HEAD_DIM ** (-0.5)
                q_out[:, lanes_of((c * heads + head) * group + j)] = part.T.astype(jnp.bfloat16)


def gather_plan(queries, key_rows, value_rows, out_grad, owner_slot, block_links):
    rows = queries.shape[0]
    peers = lax.axis_size("seq")
    half = peers // 2
    kv_heads = key_rows.shape[1] // HEAD_DIM
    group = queries.shape[1] // key_rows.shape[1]
    chunks = 2
    heads = kv_heads // chunks
    width = heads * HEAD_DIM
    each = range(chunks)
    f32, bf16 = jnp.float32, jnp.bfloat16
    ring = list(range(0, peers, 2)) + list(range(peers - 1, 0, -2))
    onward = [(ring[i], ring[(i + 1) % peers]) for i in range(peers)]
    back = [(b, a) for a, b in onward]

    def send_on(value):
        return lax.ppermute(value, "seq", onward)

    def send_back(value):
        return lax.ppermute(value, "seq", back)

    def call(kernel, args, outs, products, aliases):
        return pl.pallas_call(
            kernel,
            in_specs=[IN_VMEM] * len(args),
            out_specs=[IN_VMEM] * len(outs),
            out_shape=outs,
            input_output_aliases=aliases,
            cost_estimate=pl.CostEstimate(
                flops=products, bytes_accessed=rows, transcendentals=0
            ),
            compiler_params=pltpu.CompilerParams(vmem_limit_bytes=12 * 1024 * 1024),
        )(*args)

    span = block_links.shape[1]
    slots = owner_slot.reshape(rows // LANES, LANES)
    links = jnp.pad(block_links.reshape(1, -1), ((0, 0), (0, LANES - block_links.size)))
    notes = jnp.concatenate([slots, links], 0)
    notes = jnp.pad(notes, ((0, -notes.shape[0] % 8), (0, 0)))[None]
    notes = lax.all_to_all(jnp.broadcast_to(notes, (peers,) + notes.shape[1:]), "seq", split_axis=0, concat_axis=0, tiled=True)
    lines = jax.ShapeDtypeStruct((heads, 1, group * rows), f32)
    talls = jax.ShapeDtypeStruct((heads, HEAD_DIM, group * rows), f32)
    pairs = jax.ShapeDtypeStruct((2, rows, width), f32)

    def forward(c, shards, at, state, saved):
        args = [queries, mask, hot, *shards, *state]
        kernel = functools.partial(forward_kernel, at, heads, group, c * heads, saved)
        aliases = {len(args) - 3 + i: i for i in range(3)} if state else {}
        kept = [jax.ShapeDtypeStruct((heads, len(at) * rows, group * rows), f32)] * saved
        return call(kernel, args, [lines, lines, talls] + kept, 2 * len(at), aliases)

    def backward(c, shards, at, norm, delta, q_sums, scores=None):
        saved = scores is not None
        args = [queries, out_grad, mask, hot, *([scores] * saved), *shards, norm, delta, q_sums]
        kernel = functools.partial(backward_kernel, at, heads, group, c * heads, saved)
        return call(kernel, args, [talls] + [pairs] * len(at), 5 * len(at), {len(args) - 1: 0})

    own = (key_rows, value_rows)
    behind, ahead = [[v] for v in own], [[v] for v in own]
    state = [() for _ in each]
    hot = mask = None
    scores = {}

    def pair_at(r):
        return [side[i][r] for side in (behind, ahead) for i in range(2)]

    def catch_up(c, r):
        shards, at = pair_at(r), (r, peers - r)
        if r == 1:
            shards, at = [own, own, *shards], (0,) + at
        *state[c], = forward(c, shards, at, state[c], r >= SAVED_FROM)
        if r >= SAVED_FROM:
            scores[c, r] = state[c].pop()

    for r in range(1, half):
        for c in each:
            low, high = send_on(behind[c][-1]), send_back(ahead[c][-1])
            if (r, c) == (1, 0):
                low, high, own = lax.optimization_barrier((low, high, own))
                own = jnp.stack(own)
            elif (r, c) == (1, 1):
                low, high, notes = lax.optimization_barrier((low, high, notes))
            elif (r, c) == (2, 0):
                low, high, own = lax.optimization_barrier((low, high, own))
            elif (r, c) == (2, 1):
                catch_up(0, 1)
                low, high, state[0] = lax.optimization_barrier((low, high, state[0]))
                catch_up(1, 1)
            else:
                catch_up(c, r - 1)
                low, high, state[:] = lax.optimization_barrier((low, high, state))
            behind[c].append(low)
            ahead[c].append(high)
        if r == 1:
            hot, mask = pl.pallas_call(
                functools.partial(masks_kernel, peers, rows // BLOCK, span, rows // LANES),
                in_specs=[IN_VMEM],
                out_specs=[IN_VMEM] * 2,
                out_shape=[jax.ShapeDtypeStruct((peers, rows, LANES), bf16), jax.ShapeDtypeStruct((rows, LANES), bf16)],
                compiler_params=pltpu.CompilerParams(vmem_limit_bytes=12 * 1024 * 1024),
            )(notes)
    far = (send_on(behind[0][-1]), send_back(ahead[1][-1]))
    norm, delta, q_sums, down, up = [[None] * chunks for _ in range(5)]
    for c in each:
        catch_up(c, half - 1)
    state[:] = lax.optimization_barrier(state)
    for c in each:
        norm[c], delta[c], q_sums[c], sums = call(
            functools.partial(turn_kernel, half, heads, group, c * heads),
            [queries, out_grad, mask, hot, *far, *state[c]],
            [lines, lines, talls, jax.ShapeDtypeStruct(pairs.shape, bf16)],
            7,
            {6: 0, 7: 1, 8: 2},
        )
        if c + 1 < chunks:
            sums, state[c + 1] = lax.optimization_barrier((sums, state[c + 1]))
        else:
            sums, norm[0] = lax.optimization_barrier((sums, norm[0]))
        if c % 2:
            up[c] = send_on(sums)
        else:
            down[c] = send_back(sums)
    for r in range(half - 1, 0, -1):
        for c in each:
            q_sums[c], low, high = backward(c, pair_at(r), (r, peers - r), norm[c], delta[c], q_sums[c], scores.get((c, r)))
            low = low if down[c] is None else low + down[c].astype(f32)
            high = high if up[c] is None else high + up[c].astype(f32)
            after = (c + 1) % chunks
            low, high, norm[after] = lax.optimization_barrier((low.astype(bf16), high.astype(bf16), norm[after]))
            down[c], up[c] = send_back(low), send_on(high)
    total = []
    for c in each:
        q_sums[c], mine = backward(c, [own, own], (0,), norm[c], delta[c], q_sums[c])
        total.append((mine + down[c].astype(f32) + up[c].astype(f32)).astype(bf16))
    total[0], q_sums = lax.optimization_barrier((total[0], q_sums))
    (query_grad,) = call(
        functools.partial(finish_kernel, heads, group), q_sums, [jax.ShapeDtypeStruct(queries.shape, bf16)], 0, {}
    )
    total = jnp.concatenate(total, 2)
    return query_grad, total[0], total[1]


def local(queries, key_rows, value_rows, out_grad, owner_slot, block_links):
    rows = queries.shape[0]
    peers = lax.axis_size("seq")
    q_width, kv_width = queries.shape[1], key_rows.shape[1]
    slots = 4 * peers * max(1, rows // peers // 2)
    gathered = 2 * (peers - 1) * rows * 2 * kv_width
    relayed = slots * (3 * q_width + 4 * kv_width) + 4 * rows * 2 * kv_width
    fits = kv_width % (2 * HEAD_DIM) == 0 and peers > 2 and peers & (peers - 1) == 0 and rows % LANES == 0 and peers * rows // BLOCK <= LANES and block_links.size <= LANES
    plan = gather_plan if fits and gathered <= relayed else relay_plan
    return plan(queries, key_rows, value_rows, out_grad, owner_slot, block_links)


def solution(mesh):
    return jax.shard_map(
        local,
        mesh=mesh,
        in_specs=(
            P(("parts", "seq"), "head"),
            P(("parts", "seq"), "head"),
            P(("parts", "seq"), "head"),
            P(("parts", "seq"), "head"),
            P(("parts", "seq")),
            P(("parts", "seq"), None),
        ),
        out_specs=(
            P(("parts", "seq"), "head"),
            P(("parts", "seq"), "head"),
            P(("parts", "seq"), "head"),
        ),
        check_vma=False,
    )
```
